256 devices in a mesh: img: 8 (over z_hi, y), mx: 8 (over z_lo, core), my: 4 (over x).
Axes of the slice: x: 4, y: 4, z: 8 (z_hi: 2, z_lo: 4; z = z_hi * 4 + z_lo), core: 2. Of those that a mesh axis runs over, the one named last changes fastest.
Arguments:
- patches: bfloat16 [8192, 6144], P(('img', 'my'), 'mx')
- tile_counts: int32 [16], replicated, may hold values from 1 to 4, as said below
- image_owner: int32 [16], replicated, may hold values from 0 to 7, as said below
- block_target: int32 [8, 8], P('img'), may hold values from 0 to 7, each once within a row
- qkv_weight: bfloat16 [6144, 3, 4096], P('mx', None, 'my')
- out_weight: bfloat16 [4096, 6144], P('my', 'mx'), may hold values from -0.09375 to 0.09375
Outputs:
- routed: bfloat16 [8192, 6144], P(('img', 'my'), 'mx')
The draws below stay inside these ranges and needn't reach their ends.
Inputs may be any that keep to these rules, and one draw needn't show every extreme that they name: `tile_counts`: each image has 1 to 4 blocks; the two images of an arrival group fit its 8 blocks. `image_owner`: the owner of image k is k // 2 or the group whose index differs from it in the lowest bit; every group owns exactly two images, their blocks sum to at most 8, and in every draw some group owns exactly 8 blocks.
All inputs are finite; a program needn't handle non-finite values.
Results may differ from the reference program's by a relative error of at most 0.015.
Values may be sent and summed in bfloat16 or wider, within the bound.
No kernel may reach another device: no remote copies, remote signals or barrier semaphores. Data moves between devices by JAX's collectives and lax.ppermute only.
A program may use at most 128 MiB of HBM per device.

```python
import math
import jax
import jax.numpy as jnp
from jax import lax

D = 6144
HEADS = 32
HD = 128
BLK = 128
BLK_GRP = 8
F = 4096
R = 1024
ROWS = 8192
IMAGES = 16
N_IMG = 8


def layout_draw(key):
    pair_count = IMAGES // 4
    key_tiles, key_order, key_pair, key_side = jax.random.split(key, 4)
    small_tiles = jax.random.randint(key_tiles, (pair_count, 4), 1, BLK_GRP // 4 + 1)
    order_keys = jax.random.split(key_order, pair_count)
    ranking = jax.vmap(lambda single: jax.random.permutation(single, 4))(order_keys)
    upper = (ranking >= 2).astype(jnp.int32)
    forced_pair = jax.random.randint(key_pair, (), 0, pair_count)
    forced_side = jax.random.randint(key_side, (), 0, 2)
    pair_ids = jnp.arange(pair_count, dtype=jnp.int32)[:, None]
    forced = (pair_ids == forced_pair) & (upper == forced_side)
    counts = jnp.where(forced, BLK_GRP // 2, small_tiles)
    owners = 2 * pair_ids + upper
    return (counts.reshape(-1).astype(jnp.int32), owners.reshape(-1).astype(jnp.int32))


def column_scales():
    columns = jnp.arange(D, dtype=jnp.float32)
    return 0.5 * jnp.exp(math.log(3.0) * columns / D)


def draw_tile_counts(key, part):
    shared = layout_draw(key)
    return shared[0]


def draw_image_owner(key, part):
    shared = layout_draw(key)
    return shared[1]


def draw_patches(key, part):
    key = jax.random.fold_in(key, 3)
    key_base, key_rows = jax.random.split(key, 2)
    col_scale = column_scales()
    base = jax.random.normal(key_base, (ROWS, D), jnp.float32)
    row_scale = jnp.exp(jax.random.uniform(key_rows, (ROWS, 1), jnp.float32, math.log(0.5), math.log(5.0)))
    return (base * col_scale[None, :] * row_scale).astype(jnp.bfloat16)


def draw_qkv_weight(key, part):
    key = jax.random.fold_in(key, 5)
    key_base = jax.random.fold_in(key, 0)
    base = jnp.clip(jax.random.normal(key_base, (D, 3, F), jnp.float32), -6.0, 6.0) * D ** (-0.5)
    return base.astype(jnp.bfloat16)


def block_levels(stream_key, extent, cuts, low, high):
    gain = 1.0
    for position, shards_of in cuts:
        heights = jax.random.uniform(jax.random.fold_in(jax.random.fold_in(stream_key, 6), position), (shards_of,), jnp.float32, low / len(cuts), high / len(cuts))
        gain = gain * jnp.repeat(jnp.exp(heights), extent[position] // shards_of).reshape((-1,) + (1,) * (len(extent) - 1 - position))
    return gain


def normal_values(stream_key, dims, width, most, cuts=(), kind=jnp.bfloat16):
    drawn = width * jax.random.normal(stream_key, dims, jnp.float32)
    if cuts:
        drawn = drawn * block_levels(stream_key, dims, cuts, -0.22, 0.18)
    return jnp.clip(drawn, -most, most).astype(kind)


def setup_inputs(seed: int = 0) -> dict:
    key_list = jax.random.split(jax.random.key(seed), 7)
    patches = draw_patches(jax.random.fold_in(key_list[6], 71), 0)
    tile_counts = draw_tile_counts(jax.random.fold_in(key_list[6], 71), 0)
    image_owner = draw_image_owner(jax.random.fold_in(key_list[6], 71), 0)
    block_target = jax.vmap(lambda own: jax.random.permutation(own, BLK_GRP))(jax.random.split(key_list[3], N_IMG)).reshape((N_IMG, BLK_GRP)).astype(jnp.int32)
    qkv_weight = draw_qkv_weight(jax.random.fold_in(key_list[6], 71), 0)
    out_weight = normal_values(key_list[5], (F, D), F ** -0.5, 0.09375, ((0, 4), (1, 8)))
    return dict(patches=patches, tile_counts=tile_counts, image_owner=image_owner, block_target=block_target, qkv_weight=qkv_weight, out_weight=out_weight)


def layout_blocks(tile_counts, image_owner, img_index, blocks):
    images = tile_counts.shape[0]
    positions = jnp.arange(images, dtype=jnp.int32)
    previous = jnp.concatenate([jnp.zeros((1,), jnp.int32), tile_counts[:-1]])
    first_block = jnp.where(positions % 2 == 1, previous, 0).astype(jnp.int32)
    source = (positions // 2).astype(jnp.int32)
    member = (image_owner == img_index).astype(jnp.int32)
    counted = member * tile_counts
    offset = (jnp.cumsum(counted, dtype=jnp.int32) - counted).astype(jnp.int32)
    slot_ids = jnp.arange(blocks, dtype=jnp.int32)[:, None]
    inside = (member[None, :] == 1) & (slot_ids >= offset[None, :]) & (slot_ids < offset[None, :] + tile_counts[None, :])
    hit_table = inside.astype(jnp.int32)
    live_count = lax.optimization_barrier(jnp.sum(hit_table, axis=1, dtype=jnp.int32))
    image_id = (lax.optimization_barrier(jnp.sum(hit_table * positions[None, :], axis=1, dtype=jnp.int32)) + live_count - 1).astype(jnp.int32)
    src_block = lax.optimization_barrier(jnp.sum(hit_table * (first_block[None, :] + slot_ids - offset[None, :]), axis=1, dtype=jnp.int32))
    src_group = lax.optimization_barrier(jnp.sum(hit_table * source[None, :], axis=1, dtype=jnp.int32))
    return (image_id, src_block.astype(jnp.int32), src_group.astype(jnp.int32))

def attend(queries, key_rows, value_rows, row_ids):
    score_scale = queries.shape[1] ** (-0.5)
    scores = jnp.dot(queries, key_rows.T, preferred_element_type=jnp.float32) * score_scale
    allowed = (row_ids[:, None] == row_ids[None, :]) & (row_ids[None, :] >= 0)
    scores = jnp.where(allowed, scores, jnp.float32(-1e+30))
    row_top = lax.optimization_barrier(jnp.max(scores, axis=1, keepdims=True))
    powers = jnp.exp(scores - row_top)
    weights = (powers / lax.optimization_barrier(jnp.sum(powers, axis=1, keepdims=True))).astype(jnp.bfloat16)
    mixture = jnp.dot(weights, value_rows, preferred_element_type=jnp.float32)
    mixture = jnp.where((row_ids >= 0)[:, None], mixture, jnp.float32(0.0))
    return mixture.astype(jnp.bfloat16)

def invert_targets(targets, blocks):
    slot_ids = jnp.arange(blocks, dtype=jnp.int32)
    return lax.optimization_barrier(jnp.sum(jnp.where(targets[None, :] == slot_ids[:, None], slot_ids[None, :], 0), axis=1, dtype=jnp.int32)).astype(jnp.int32)

def reference(patches, tile_counts, image_owner, block_target, qkv_weight, out_weight):
    values = patches.astype(jnp.float32)
    row_sum = lax.optimization_barrier(jnp.sum(values, axis=1))
    row_square = lax.optimization_barrier(jnp.sum(values * values, axis=1))
    mean_row = row_sum / D
    var_row = row_square / D - mean_row * mean_row
    normed = ((values - mean_row[:, None]) * lax.rsqrt(var_row[:, None] + 1e-06)).astype(jnp.bfloat16)
    arrival = normed.reshape(N_IMG * BLK_GRP, BLK, D)
    flat_weight = qkv_weight.reshape(D, 3 * F)

    def one_group(img_index):
        image_id, src_block, src_group = layout_blocks(tile_counts, image_owner, img_index, BLK_GRP)
        packed = jnp.take(arrival, (src_group * BLK_GRP + src_block).astype(jnp.int32), axis=0).reshape(R, D)
        qkv_rows = jnp.dot(packed, flat_weight, preferred_element_type=jnp.float32).astype(jnp.bfloat16)
        qkv_rows = qkv_rows.reshape(R, 3, HEADS, HD)
        row_ids = jnp.repeat(image_id, BLK)

        def one_head(head):
            slab = lax.dynamic_index_in_dim(qkv_rows, head, 2, keepdims=False)
            return attend(slab[:, 0], slab[:, 1], slab[:, 2], row_ids)
        attended = lax.map(one_head, jnp.arange(HEADS, dtype=jnp.int32))
        heads_rows = jnp.transpose(attended, (1, 0, 2)).reshape(R, F)
        branch = jnp.dot(heads_rows, out_weight, preferred_element_type=jnp.float32).astype(jnp.bfloat16)
        inverse = invert_targets(block_target[img_index], BLK_GRP)
        return jnp.take(branch.reshape(BLK_GRP, BLK, D), inverse, axis=0).reshape(R, D)
    routed = lax.map(one_group, jnp.arange(N_IMG, dtype=jnp.int32))
    return routed.reshape(ROWS, D)
```

```python
import jax
import jax.numpy as jnp
from jax import lax
from jax.experimental import pallas as pl
from jax.experimental.pallas import tpu as pltpu
from jax.sharding import PartitionSpec as P

D = 6144
HD = 128
BLK = 128
GRP = 8
R = 1024
SH = 256
DL = 768
CHIP = 2 * DL
IMG_ROWS = 512
ORDER = (0, 2, 1, 3)
F32 = jnp.float32
BF16 = jnp.bfloat16


def swap(block, axis, bits):
    count = lax.axis_size(axis)
    return lax.ppermute(block, axis, [(i, i ^ bits) for i in range(count)])


def shift(block, axis, step):
    count = lax.axis_size(axis)
    return lax.ppermute(block, axis, [((i + step) % count, i) for i in range(count)])


def weight_kernel(sibling, w_ref, keep_ref, send_ref, sems):
    mx = lax.axis_index("mx")
    z = mx >> 1
    lane = (mx & 1) ^ (1 if sibling else 0)
    copies = []
    for place, j in enumerate(ORDER):
        head = lane * 4 + (z ^ j)
        dst = keep_ref if place < 2 else send_ref
        for s in range(3):
            copies.append(
                pltpu.make_async_copy(
                    w_ref.at[s, :, pl.ds(pl.multiple_of(head * HD, HD), HD)],
                    dst.at[:, pl.ds((place % 2) * 3 * HD + s * HD, HD)],
                    sems.at[len(copies)],
                )
            )
    for copy in copies:
        copy.start()
    for copy in copies:
        copy.wait()


def weight_heads(w3, sibling):
    def kernel(w_ref, keep_ref, send_ref, sems):
        weight_kernel(sibling, w_ref, keep_ref, send_ref, sems)

    return pl.pallas_call(
        kernel,
        out_shape=[jax.ShapeDtypeStruct((DL, 6 * HD), BF16)] * 2,
        in_specs=[pl.BlockSpec(memory_space=pl.ANY)],
        out_specs=[pl.BlockSpec(memory_space=pl.ANY)] * 2,
        scratch_shapes=[pltpu.SemaphoreType.DMA((12,))],
        cost_estimate=pl.CostEstimate(flops=0, bytes_accessed=4 * DL * 6 * HD * 2, transcendentals=0),
    )(w3)


def out_weight_kernel(w_ref, out_ref, sems):
    mx = lax.axis_index("mx")
    z = mx >> 1
    copies = []
    for side in range(2):
        lane = (mx & 1) ^ side
        for j in range(4):
            head = lane * 4 + (z ^ j)
            copies.append(
                pltpu.make_async_copy(
                    w_ref.at[pl.ds(pl.multiple_of(head * HD, HD), HD), :],
                    out_ref.at[pl.ds((side * 4 + j) * HD, HD), :],
                    sems.at[len(copies)],
                )
            )
    for copy in copies:
        copy.start()
    for copy in copies:
        copy.wait()


def out_weight_heads(w):
    return pl.pallas_call(
        out_weight_kernel,
        out_shape=jax.ShapeDtypeStruct(w.shape, BF16),
        in_specs=[pl.BlockSpec(memory_space=pl.ANY)],
        out_specs=pl.BlockSpec(memory_space=pl.ANY),
        scratch_shapes=[pltpu.SemaphoreType.DMA((8,))],
        cost_estimate=pl.CostEstimate(flops=0, bytes_accessed=4 * R * DL, transcendentals=0),
    )(w)


def attention_kernel(counts_ref, coef_ref, cs_ref, *refs):
    own, got = refs[0:4], refs[4:8]
    out_ref, qkv = refs[8], refs[9]
    group = lax.axis_index("img")
    my = lax.axis_index("my")
    for k, offset in enumerate((0, 1, 3, 2)):
        coef = coef_ref[k * SH : (k + 1) * SH, :]
        total = own[k][...] + got[k][...].astype(F32)
        for c in range(4):
            total = total + coef[:, c + 1 : c + 2] * cs_ref[c : c + 1, :]
        total = total * coef[:, 0:1]
        shard = (my + offset) & 3
        qkv[pl.ds(pl.multiple_of(shard * SH, SH), SH), :] = total.astype(BF16)
    first = counts_ref[2 * group]
    second = counts_ref[2 * group + 1]
    for image in range(2):
        start = pl.multiple_of(first * BLK, BLK) if image else 0
        live = (second if image else first) * BLK
        q = qkv[pl.ds(start, IMG_ROWS), 0:HD]
        key = qkv[pl.ds(start, IMG_ROWS), HD : 2 * HD]
        value = qkv[pl.ds(start, IMG_ROWS), 2 * HD : 3 * HD]
        rows = lax.broadcasted_iota(jnp.int32, (IMG_ROWS, HD), 0)
        value = jnp.where(rows < live, value, jnp.zeros_like(value))
        scores = lax.dot_general(q, key, (((1,), (1,)), ((), ())), preferred_element_type=F32)
        columns = lax.broadcasted_iota(jnp.int32, (IMG_ROWS, IMG_ROWS), 1)
        scores = jnp.where(columns < live, scores * HD ** (-0.5), F32(-1e30))
        top = jnp.max(scores, axis=1, keepdims=True)
        powers = jnp.exp(scores - top)
        weights = (powers / jnp.sum(powers, axis=1, keepdims=True)).astype(BF16)
        mixture = jnp.dot(weights, value, preferred_element_type=F32)
        out_ref[image * IMG_ROWS : (image + 1) * IMG_ROWS, :] = mixture.astype(BF16)


def attention(counts, coef, cs, own, got):
    vmem = pl.BlockSpec(memory_space=pltpu.VMEM)
    return pl.pallas_call(
        attention_kernel,
        out_shape=jax.ShapeDtypeStruct((R, HD), BF16),
        in_specs=[pl.BlockSpec(memory_space=pltpu.SMEM)] + [vmem] * 10,
        out_specs=vmem,
        scratch_shapes=[pltpu.VMEM((R, 3 * HD), BF16)],
        compiler_params=pltpu.CompilerParams(vmem_limit_bytes=32 << 20),
        cost_estimate=pl.CostEstimate(
            flops=8 * IMG_ROWS * IMG_ROWS * HD, bytes_accessed=4 << 20, transcendentals=2 * IMG_ROWS * IMG_ROWS
        ),
    )(counts, coef, cs, *own, *got)


def route_kernel(counts_ref, owner_ref, target_ref, mine_ref, other_ref, far_ref, near_ref, source):
    group = lax.axis_index("img")
    my = lax.axis_index("my")
    for t in range(GRP):
        source[t] = -1
    base = (group >> 1) * 4
    offset = jnp.int32(0)
    for i in range(4):
        image = base + i
        count = counts_ref[image]
        owned = owner_ref[image] == group
        side = jnp.where((image >> 1) == group, 0, GRP)
        for b in range(4):

            @pl.when(owned & (b < count))
            def _():
                place = target_ref[0, jnp.minimum(offset + b, GRP - 1)]
                source[place] = side + (i & 1) * 4 + b

        offset = offset + jnp.where(owned, count, 0)
    for n, step in enumerate((2, 1, 3, 0)):
        shard = (my + step) & 3
        out_ref = far_ref if n < 2 else near_ref
        for half in range(2):
            src = source[2 * shard + half]
            place = pl.ds((n % 2) * SH + half * BLK, BLK)

            @pl.when(src < 0)
            def _():
                out_ref[place, :] = jnp.zeros((BLK, HD), BF16)

            @pl.when((src >= 0) & (src < GRP))
            def _():
                row = pl.multiple_of(jnp.clip(src, 0, GRP - 1) * BLK, BLK)
                out_ref[place, :] = mine_ref[pl.ds(row, BLK), :]

            @pl.when(src >= GRP)
            def _():
                row = pl.multiple_of(jnp.clip(src - GRP, 0, GRP - 1) * BLK, BLK)
                out_ref[place, :] = other_ref[pl.ds(row, BLK), :]


def route(counts, owner, target, mine, other):
    vmem = pl.BlockSpec(memory_space=pltpu.VMEM)
    smem = pl.BlockSpec(memory_space=pltpu.SMEM)
    return pl.pallas_call(
        route_kernel,
        out_shape=[jax.ShapeDtypeStruct((2 * SH, HD), BF16)] * 2,
        in_specs=[smem] * 3 + [vmem] * 2,
        out_specs=[vmem] * 2,
        scratch_shapes=[pltpu.SMEM((GRP,), jnp.int32)],
        cost_estimate=pl.CostEstimate(flops=0, bytes_accessed=R * HD * 4, transcendentals=0),
    )(counts, owner, target, mine, other)


def shards(patches, tile_counts, image_owner, block_target, qkv_weight, out_weight):
    rows = [patches, shift(patches, "my", 1), shift(patches, "my", -1), shift(patches, "my", 2)]
    w3 = jnp.transpose(qkv_weight, (1, 0, 2))
    theirs_keep, theirs_send = weight_heads(w3, True)
    sib_send = swap(theirs_send, "mx", 1)
    sib_keep = swap(theirs_keep, "mx", 1)
    own_keep, own_send = weight_heads(w3, False)
    wo = out_weight_heads(out_weight)

    ones = jnp.ones((8, DL), BF16)

    def total(a, b):
        return jnp.dot(ones, a, preferred_element_type=F32) + jnp.dot(ones, b, preferred_element_type=F32)

    cs_send = total(own_send, sib_send)
    cs_keep = total(own_keep, sib_keep)

    sums, squares, own, got = [], [], [], []
    for k in range(4):
        xo = rows[k]
        xs = swap(xo, "mx", 1)
        fo, fs = xo.astype(F32), xs.astype(F32)
        s1 = jnp.sum(fo, axis=1) + jnp.sum(fs, axis=1)
        s2 = jnp.sum(fo * fo, axis=1) + jnp.sum(fs * fs, axis=1)
        sums.append(s1)
        squares.append(s2)
        center = (s1 / CHIP)[:, None]
        part = (
            jnp.dot(xo, own_send, preferred_element_type=F32)
            + jnp.dot(xs, sib_send, preferred_element_type=F32)
            - center * cs_send[0:1, :]
        ).astype(BF16)
        first = swap(part, "mx", 2)
        kept = (
            jnp.dot(xo, own_keep, preferred_element_type=F32)
            + jnp.dot(xs, sib_keep, preferred_element_type=F32)
            - center * cs_keep[0:1, :]
        )
        mine = kept + first.astype(F32)
        second = swap(mine[:, 3 * HD :].astype(BF16), "mx", 4)
        own.append(mine[:, : 3 * HD])
        got.append(second)

    stats = jnp.stack(sums + squares, axis=0)
    w = 3 * HD
    cs = [cs_keep[:, :w], cs_send[:, :w], cs_keep[:, w:], cs_send[:, w:]]
    notes = [jnp.concatenate([stats, cs[0]], axis=1)]
    for j in (1, 2, 3):
        notes.append(swap(jnp.concatenate([stats, cs[j]], axis=1), "mx", 2 * j))
    all_stats = jnp.stack([n[:, :SH] for n in notes])
    chip_sum = all_stats[:, 0:4].reshape(4, R)
    chip_sq = all_stats[:, 4:8].reshape(4, R)
    mean = jnp.sum(chip_sum, axis=0) / D
    var = jnp.sum(chip_sq, axis=0) / D - mean * mean
    scale = lax.rsqrt(var + 1e-06)
    apart = chip_sum / CHIP - mean[None, :]
    coef = jnp.concatenate([scale[None, :], apart, jnp.zeros((3, R), F32)], axis=0).T
    cs_rows = jnp.concatenate([n[0:1, SH:] for n in notes], axis=0)

    attended = attention(tile_counts, coef, cs_rows, own, got)
    other = swap(attended, "img", 1)
    far, near = route(tile_counts, image_owner, block_target, attended, other)

    def project(block):
        lane = jnp.concatenate([block] + [swap(block, "mx", 2 * j) for j in (1, 2, 3)], axis=1)
        sib = swap(lane, "mx", 1)
        return jnp.dot(lane, wo[: 4 * HD], preferred_element_type=F32) + jnp.dot(
            sib, wo[4 * HD :], preferred_element_type=F32
        )

    far_out = project(far)
    near_out = project(near)
    from_far = shift(far_out[:SH].astype(BF16), "my", 2)
    from_up = shift(far_out[SH:].astype(BF16), "my", -1)
    from_down = shift(near_out[:SH].astype(BF16), "my", 1)
    out = near_out[SH:] + from_far.astype(F32) + from_up.astype(F32) + from_down.astype(F32)
    return out.astype(BF16)


def solution(mesh):
    in_specs = (
        P(("img", "my"), "mx"),
        P(),
        P(),
        P("img", None),
        P("mx", None, "my"),
        P("my", "mx"),
    )
    out_specs = P(("img", "my"), "mx")
    return jax.shard_map(shards, mesh=mesh, in_specs=in_specs, out_specs=out_specs, check_vma=False)
```

```python
import jax
import jax.numpy as jnp
from jax import lax
from jax.experimental import pallas as pl
from jax.experimental.pallas import tpu as pltpu
from jax.sharding import PartitionSpec as P

D = 6144
HD = 128
BLK = 128
GRP = 8
R = 1024
SH = 256
DL = 768
CHIP = 2 * DL
HEAD = 3 * HD
IMG_ROWS = 512
ORDER = (0, 2, 1, 3)
NOTE = R + HEAD
F32 = jnp.float32
BF16 = jnp.bfloat16

VMEM = pl.BlockSpec(memory_space=pltpu.VMEM)
SMEM = pl.BlockSpec(memory_space=pltpu.SMEM)
ANY = pl.BlockSpec(memory_space=pl.ANY)


def call(kernel, outs, ins, scratch=(), flops=0, moved=1 << 20, exps=0, limit=16, out_specs=None):
    out_shape = [jax.ShapeDtypeStruct(s, d) for s, d in outs]
    return pl.pallas_call(
        kernel,
        out_shape=out_shape,
        in_specs=ins,
        out_specs=out_specs or [VMEM] * len(outs),
        scratch_shapes=list(scratch),
        compiler_params=pltpu.CompilerParams(vmem_limit_bytes=limit << 20),
        cost_estimate=pl.CostEstimate(flops=flops, bytes_accessed=moved, transcendentals=exps),
    )


def swap(block, axis, bits):
    count = lax.axis_size(axis)
    return lax.ppermute(block, axis, [(i, i ^ bits) for i in range(count)])


def shift(block, axis, step):
    count = lax.axis_size(axis)
    return lax.ppermute(block, axis, [((i + step) % count, i) for i in range(count)])


def weight_heads(w3, sibling):
    def kernel(w_ref, keep_ref, send_ref, sems):
        mx = lax.axis_index("mx")
        z = mx >> 1
        lane = (mx & 1) ^ (1 if sibling else 0)
        copies = []
        for place in (2, 3, 0, 1):
            head = lane * 4 + (z ^ ORDER[place])
            dst = keep_ref if place < 2 else send_ref
            for s in range(3):
                copies.append(
                    pltpu.make_async_copy(
                        w_ref.at[s, :, pl.ds(pl.multiple_of(head * HD, HD), HD)],
                        dst.at[:, pl.ds((place % 2) * HEAD + s * HD, HD)],
                        sems.at[len(copies)],
                    )
                )
        for copy in copies:
            copy.start()
        for copy in copies:
            copy.wait()

    shape = ((DL, 2 * HEAD), BF16)
    return call(kernel, [shape, shape], [ANY], [pltpu.SemaphoreType.DMA((12,))], moved=8 * DL * HEAD)(w3)


def out_weight_heads(w):
    def kernel(w_ref, out_ref, sems):
        mx = lax.axis_index("mx")
        z = mx >> 1
        copies = []
        for side in range(2):
            lane = (mx & 1) ^ side
            for j in range(4):
                head = lane * 4 + (z ^ j)
                copies.append(
                    pltpu.make_async_copy(
                        w_ref.at[pl.ds(pl.multiple_of(head * HD, HD), HD), :],
                        out_ref.at[pl.ds((side * 4 + j) * HD, HD), :],
                        sems.at[len(copies)],
                    )
                )
        for copy in copies:
            copy.start()
        for copy in copies:
            copy.wait()

    (out,) = call(kernel, [(w.shape, BF16)], [ANY], [pltpu.SemaphoreType.DMA((8,))], moved=4 * R * DL)(w)
    return out


def table(counts, owner, target):
    def kernel(counts_ref, owner_ref, target_ref, out_ref, source):
        group = lax.axis_index("img")
        my = lax.axis_index("my")
        for t in range(GRP):
            source[t] = -1
        base = (group >> 1) * 4
        offset = jnp.int32(0)
        for i in range(4):
            image = base + i
            count = counts_ref[image]
            owned = owner_ref[image] == group
            side = jnp.where((image >> 1) == group, 0, GRP)
            for b in range(4):

                @pl.when(owned & (b < count))
                def _():
                    place = target_ref[0, jnp.minimum(offset + b, GRP - 1)]
                    source[place] = side + (i & 1) * 4 + b

            offset = offset + jnp.where(owned, count, 0)
        for n, step in enumerate((2, 1, 3, 0)):
            shard = (my + step) & 3
            out_ref[2 * n] = source[2 * shard]
            out_ref[2 * n + 1] = source[2 * shard + 1]
        out_ref[8] = counts_ref[2 * group]
        out_ref[9] = counts_ref[2 * group + 1]

    (out,) = call(
        kernel,
        [((16,), jnp.int32)],
        [SMEM] * 3,
        [pltpu.SMEM((GRP,), jnp.int32)],
        moved=1 << 10,
        limit=4,
        out_specs=[SMEM],
    )(counts, owner, target)
    return out


def load_rows(rows, xo_ref, xs_ref):
    rows[0:SH, 0:DL] = xo_ref[...]
    rows[0:SH, DL:CHIP] = xs_ref[...]
    rows[SH : SH + 16, :] = jnp.ones((16, CHIP), BF16)


def row_stats(xo_ref, xs_ref):
    fo, fs = xo_ref[...].astype(F32), xs_ref[...].astype(F32)
    s1 = jnp.sum(fo, axis=1, keepdims=True) + jnp.sum(fs, axis=1, keepdims=True)
    s2 = jnp.sum(fo * fo, axis=1, keepdims=True) + jnp.sum(fs * fs, axis=1, keepdims=True)
    lane = lax.broadcasted_iota(jnp.int32, (SH, HD), 1)
    return jnp.where(lane == 0, s1, jnp.where(lane == 1, s2, F32(0.0)))


def partial_tile(rows, wo_ref, ws_ref, columns, center):
    acc = jnp.dot(rows[:, 0:DL], wo_ref[:, columns], preferred_element_type=F32)
    acc = acc + jnp.dot(rows[:, DL:CHIP], ws_ref[:, columns], preferred_element_type=F32)
    sums = acc[SH : SH + 8, :]
    return acc[0:SH, :] - center * sums[0:1, :], sums


ROWS_SCRATCH = pltpu.VMEM((SH + 16, CHIP), BF16)
PART_FLOPS = 2 * SH * CHIP * 2 * HEAD


def send_part(xo, xs, wo, ws):
    def kernel(xo_ref, xs_ref, wo_ref, ws_ref, out_ref, stat_ref, rows):
        load_rows(rows, xo_ref, xs_ref)
        stat = row_stats(xo_ref, xs_ref)
        stat_ref[...] = stat
        center = stat[:, 0:1] / CHIP
        for n in range(3):
            columns = slice(n * 256, (n + 1) * 256)
            tile, _ = partial_tile(rows, wo_ref, ws_ref, columns, center)
            out_ref[:, columns] = tile.astype(BF16)

    return call(
        kernel, [((SH, 2 * HEAD), BF16), ((SH, HD), F32)], [VMEM] * 4, [ROWS_SCRATCH], PART_FLOPS
    )(xo, xs, wo, ws)


def keep_part(xo, xs, wo, ws, stat, got):
    def kernel(xo_ref, xs_ref, wo_ref, ws_ref, stat_ref, got_ref, own_ref, send_ref, rows):
        load_rows(rows, xo_ref, xs_ref)
        center = stat_ref[:, 0:1] / CHIP
        for n in range(6):
            columns = slice(n * HD, (n + 1) * HD)
            if n % 2 == 0:
                pair, _ = partial_tile(rows, wo_ref, ws_ref, slice(n * HD, (n + 2) * HD), center)
            tile = pair[:, (n % 2) * HD : (n % 2 + 1) * HD] + got_ref[:, columns].astype(F32)
            if n < 3:
                own_ref[:, columns] = tile
            else:
                send_ref[:, (n - 3) * HD : (n - 2) * HD] = tile.astype(BF16)

    return call(
        kernel, [((SH, HEAD), F32), ((SH, HEAD), BF16)], [VMEM] * 6, [ROWS_SCRATCH], PART_FLOPS
    )(xo, xs, wo, ws, stat, got)


def whole_part(xo, xs, weights, stats):
    def kernel(xo_ref, xs_ref, ko_ref, ks_ref, so_ref, ss_ref, t0_ref, t1_ref, t2_ref, *refs):
        own_ref, p1_ref, p2_ref, p3_ref = refs[0:4]
        notes, rows = refs[4:8], refs[8]
        load_rows(rows, xo_ref, xs_ref)
        stat = row_stats(xo_ref, xs_ref)
        center = stat[:, 0:1] / CHIP
        for wo_ref, ws_ref, outs, js in ((so_ref, ss_ref, (p1_ref, p3_ref), (1, 3)), (ko_ref, ks_ref, (own_ref, p2_ref), (0, 2))):
            for n in range(6):
                if n % 2 == 0:
                    pair, sums = partial_tile(rows, wo_ref, ws_ref, slice(n * HD, (n + 2) * HD), center)
                half = slice((n % 2) * HD, (n % 2 + 1) * HD)
                columns = slice((n % 3) * HD, (n % 3 + 1) * HD)
                out_ref = outs[n // 3]
                out_ref[:, columns] = pair[:, half].astype(out_ref.dtype)
                notes[js[n // 3]][:, R + (n % 3) * HD : R + (n % 3 + 1) * HD] = sums[:, half]
        for k, one in enumerate((t0_ref[...], t1_ref[...], t2_ref[...], stat)):
            turned = one.T[0:8, :]
            for note in notes:
                note[:, k * SH : (k + 1) * SH] = turned

    part = ((SH, HEAD), BF16)
    note = ((8, NOTE), F32)
    return call(
        kernel, [((SH, HEAD), F32), part, part, part] + [note] * 4, [VMEM] * 9, [ROWS_SCRATCH], 2 * PART_FLOPS
    )(xo, xs, *weights, *stats)


def coefficients(notes):
    def kernel(n0_ref, n1_ref, n2_ref, n3_ref, coef_ref, cs_ref):
        refs = (n0_ref, n1_ref, n2_ref, n3_ref)
        sums = [n[0:1, 0:R] for n in refs]
        mean = (sums[0] + sums[1] + sums[2] + sums[3]) / D
        squares = n0_ref[1:2, 0:R] + n1_ref[1:2, 0:R] + n2_ref[1:2, 0:R] + n3_ref[1:2, 0:R]
        var = squares / D - mean * mean
        scale = lax.rsqrt(var + 1e-06)
        lines = [scale] + [s / CHIP - mean for s in sums] + [jnp.zeros((HD - 5, R), F32)]
        coef_ref[...] = jnp.concatenate(lines, axis=0).T
        for c, n in enumerate(refs):
            cs_ref[c : c + 1, :] = n[0:1, R:NOTE]
        cs_ref[4:8, :] = jnp.zeros((4, HEAD), F32)

    return call(kernel, [((R, HD), F32), ((8, HEAD), F32)], [VMEM] * 4)(*notes)


def attention(places, coef, cs, parts):
    flat = [p for chunk in parts for p in chunk]

    def kernel(places_ref, coef_ref, cs_ref, *refs):
        out_ref, qkv = refs[len(flat)], refs[len(flat) + 1]
        my = lax.axis_index("my")
        at = 0
        for k, offset in enumerate((0, 1, 3, 2)):
            coef = coef_ref[k * SH : (k + 1) * SH, :]
            total = refs[at][...]
            for more in range(1, len(parts[k])):
                total = total + refs[at + more][...].astype(F32)
            at += len(parts[k])
            for c in range(4):
                total = total + coef[:, c + 1 : c + 2] * cs_ref[c : c + 1, :]
            total = total * coef[:, 0:1]
            shard = (my + offset) & 3
            qkv[pl.ds(pl.multiple_of(shard * SH, SH), SH), :] = total.astype(BF16)
        first, second = places_ref[8], places_ref[9]
        for image in range(2):
            start = pl.multiple_of(first * BLK, BLK) if image else 0
            live = (second if image else first) * BLK
            q = qkv[pl.ds(start, IMG_ROWS), 0:HD]
            key = qkv[pl.ds(start, IMG_ROWS), HD : 2 * HD]
            value = qkv[pl.ds(start, IMG_ROWS), 2 * HD : 3 * HD]
            rows = lax.broadcasted_iota(jnp.int32, (IMG_ROWS, HD), 0)
            value = jnp.where(rows < live, value, jnp.zeros_like(value))
            scores = lax.dot_general(q, key, (((1,), (1,)), ((), ())), preferred_element_type=F32)
            columns = lax.broadcasted_iota(jnp.int32, (IMG_ROWS, IMG_ROWS), 1)
            scores = jnp.where(columns < live, scores * HD ** (-0.5), F32(-1e30))
            top = jnp.max(scores, axis=1, keepdims=True)
            powers = jnp.exp(scores - top)
            weights = (powers / jnp.sum(powers, axis=1, keepdims=True)).astype(BF16)
            mixture = jnp.dot(weights, value, preferred_element_type=F32)
            out_ref[image * IMG_ROWS : (image + 1) * IMG_ROWS, :] = mixture.astype(BF16)

    (out,) = call(
        kernel,
        [((R, HD), BF16)],
        [SMEM] + [VMEM] * (2 + len(flat)),
        [pltpu.VMEM((R, HEAD), BF16)],
        8 * IMG_ROWS * IMG_ROWS * HD,
        4 << 20,
        2 * IMG_ROWS * IMG_ROWS,
        24,
    )(places, coef, cs, *flat)
    return out


def route(places, mine, other):
    def kernel(places_ref, mine_ref, other_ref, *outs):
        for n in range(GRP):
            out_ref, at = ((outs[0], 0), (outs[1], 2), (outs[2], 6))[(0, 0, 1, 1, 1, 1, 2, 2)[n]]
            place = slice((n - at) * BLK, (n - at + 1) * BLK)
            src = places_ref[n]
            row = pl.multiple_of((src & 7) * BLK, BLK)

            @pl.when(src < 0)
            def _():
                out_ref[place, :] = jnp.zeros((BLK, HD), BF16)

            @pl.when((src >= 0) & (src < GRP))
            def _():
                out_ref[place, :] = mine_ref[pl.ds(row, BLK), :]

            @pl.when(src >= GRP)
            def _():
                out_ref[place, :] = other_ref[pl.ds(row, BLK), :]

    outs = [((SH, HD), BF16), ((2 * SH, HD), BF16), ((SH, HD), BF16)]
    return call(kernel, outs, [SMEM, VMEM, VMEM])(places, mine, other)


def project(block, wo, dtype):
    lane = [block] + [swap(block, "mx", 2 * j) for j in (1, 2, 3)]
    heads = lane + [swap(one, "mx", 1) for one in lane]
    count = block.shape[0] // SH

    def kernel(*refs):
        w_ref, outs, rows = refs[8], refs[9 : 9 + count], refs[9 + count]
        for h in range(8):
            rows[:, h * HD : (h + 1) * HD] = refs[h][...]
        for i, out_ref in enumerate(outs):
            for n in range(3):
                columns = slice(n * 256, (n + 1) * 256)
                tile = jnp.dot(rows[i * SH : (i + 1) * SH, :], w_ref[:, columns], preferred_element_type=F32)
                out_ref[:, columns] = tile.astype(out_ref.dtype)

    return call(
        kernel,
        [((SH, DL), dtype)] * count,
        [VMEM] * 9,
        [pltpu.VMEM((count * SH, R), BF16)],
        2 * count * SH * R * DL,
    )(*heads, wo)


def shards(patches, tile_counts, image_owner, block_target, qkv_weight, out_weight):
    rows = [patches, shift(patches, "my", 1), shift(patches, "my", -1), shift(patches, "my", 2)]
    w3 = jnp.transpose(qkv_weight, (1, 0, 2))
    theirs_keep, theirs_send = weight_heads(w3, True)
    sib_send = swap(theirs_send, "mx", 1)
    sib_keep = swap(theirs_keep, "mx", 1)
    own_keep, own_send = weight_heads(w3, False)
    wo = out_weight_heads(out_weight)
    places = table(tile_counts, image_owner, block_target)
    sibs = [swap(x, "mx", 1) for x in rows]

    parts, stats = [], []
    for k in range(3):
        part, stat = send_part(rows[k], sibs[k], own_send, sib_send)
        stats.append(stat)
        got = swap(part, "mx", 2)
        own, second = keep_part(rows[k], sibs[k], own_keep, sib_keep, stat, got)
        parts.append((own, swap(second, "mx", 4)))
    weights = (own_keep, sib_keep, own_send, sib_send)
    own, p1, p2, p3, n0, n1, n2, n3 = whole_part(rows[3], sibs[3], weights, stats)
    parts.append((own, swap(p2, "mx", 4), swap(p3, "mx", 6), swap(p1, "mx", 2)))
    coef, cs = coefficients([n0, swap(n1, "mx", 2), swap(n2, "mx", 4), swap(n3, "mx", 6)])

    attended = attention(places, coef, cs, parts)
    other = swap(attended, "img", 1)
    across, beside, here = route(places, attended, other)

    (far,) = project(across, wo, BF16)
    up, down = project(beside, wo, BF16)
    (mine,) = project(here, wo, F32)
    from_far = shift(far, "my", 2)
    from_up = shift(up, "my", -1)
    from_down = shift(down, "my", 1)
    out = mine + from_far.astype(F32) + from_up.astype(F32) + from_down.astype(F32)
    return out.astype(BF16)


def solution(mesh):
    in_specs = (
        P(("img", "my"), "mx"),
        P(),
        P(),
        P("img", None),
        P("mx", None, "my"),
        P("my", "mx"),
    )
    out_specs = P(("img", "my"), "mx")
    return jax.shard_map(shards, mesh=mesh, in_specs=in_specs, out_specs=out_specs, check_vma=False)
```

```python
import jax
import jax.numpy as jnp
from jax import lax
from jax.experimental import pallas as pl
from jax.experimental.pallas import tpu as pltpu
from jax.sharding import PartitionSpec as P

D = 6144
HD = 128
BLK = 128
GRP = 8
R = 1024
SH = 256
DL = 768
CHIP = 2 * DL
HEAD = 3 * HD
IMG_ROWS = 512
ORDER = (0, 2, 1, 3)
NOTE = R + HEAD
F32 = jnp.float32
BF16 = jnp.bfloat16

VMEM = pl.BlockSpec(memory_space=pltpu.VMEM)
SMEM = pl.BlockSpec(memory_space=pltpu.SMEM)
ANY = pl.BlockSpec(memory_space=pl.ANY)
HBM = pl.BlockSpec(memory_space=pltpu.HBM)
LONG = 8 << 30


def call(kernel, outs, ins, scratch=(), flops=0, moved=1 << 20, exps=0, limit=16, out_specs=None, after=(), aliases=None):
    out_shape = [jax.ShapeDtypeStruct(s, d) for s, d in outs]
    count = len(ins)

    def ordered(*refs):
        kernel(*refs[:count], *refs[count + len(after) :])

    made = pl.pallas_call(
        ordered,
        out_shape=out_shape,
        in_specs=list(ins) + [ANY] * len(after),
        out_specs=out_specs or [VMEM] * len(outs),
        scratch_shapes=list(scratch),
        input_output_aliases=aliases or {},
        compiler_params=pltpu.CompilerParams(vmem_limit_bytes=limit << 20),
        cost_estimate=pl.CostEstimate(flops=flops, bytes_accessed=moved, transcendentals=exps),
    )
    return lambda *args: made(*args, *after)


def gate(blocks, after):
    def kernel(*refs):
        pass

    outs = [(b.shape, b.dtype) for b in blocks]
    ins = [ANY] * len(blocks)
    same = {i: i for i in range(len(blocks))}
    return call(kernel, outs, ins, moved=1 << 10, limit=4, out_specs=ins, after=after, aliases=same)(*blocks)


def swap(block, axis, bits):
    count = lax.axis_size(axis)
    return lax.ppermute(block, axis, [(i, i ^ bits) for i in range(count)])


def shift(block, axis, step):
    count = lax.axis_size(axis)
    return lax.ppermute(block, axis, [((i + step) % count, i) for i in range(count)])


def weight_heads(w3, sibling):
    def kernel(w_ref, keep_ref, send_ref, sems):
        mx = lax.axis_index("mx")
        z = mx >> 1
        lane = (mx & 1) ^ (1 if sibling else 0)
        copies = []
        for place in (2, 3, 0, 1):
            head = lane * 4 + (z ^ ORDER[place])
            dst = keep_ref if place < 2 else send_ref
            for s in range(3):
                copies.append(
                    pltpu.make_async_copy(
                        w_ref.at[s, :, pl.ds(pl.multiple_of(head * HD, HD), HD)],
                        dst.at[:, pl.ds((place % 2) * HEAD + s * HD, HD)],
                        sems.at[len(copies)],
                    )
                )
        for copy in copies:
            copy.start()
        for copy in copies:
            copy.wait()

    shape = ((DL, 2 * HEAD), BF16)
    return call(kernel, [shape, shape], [HBM], [pltpu.SemaphoreType.DMA((12,))], moved=8 * DL * HEAD)(w3)


def out_weight_heads(w):
    def kernel(w_ref, out_ref, sems):
        mx = lax.axis_index("mx")
        z = mx >> 1
        copies = []
        for side in range(2):
            lane = (mx & 1) ^ side
            for j in range(4):
                head = lane * 4 + (z ^ j)
                copies.append(
                    pltpu.make_async_copy(
                        w_ref.at[pl.ds(pl.multiple_of(head * HD, HD), HD), :],
                        out_ref.at[pl.ds((side * 4 + j) * HD, HD), :],
                        sems.at[len(copies)],
                    )
                )
        for copy in copies:
            copy.start()
        for copy in copies:
            copy.wait()

    (out,) = call(kernel, [(w.shape, BF16)], [HBM], [pltpu.SemaphoreType.DMA((8,))], moved=4 * R * DL)(w)
    return out


def table(counts, owner, target):
    def kernel(counts_ref, owner_ref, target_ref, out_ref, source):
        group = lax.axis_index("img")
        my = lax.axis_index("my")
        for t in range(GRP):
            source[t] = -1
        base = (group >> 1) * 4
        offset = jnp.int32(0)
        for i in range(4):
            image = base + i
            count = counts_ref[image]
            owned = owner_ref[image] == group
            side = jnp.where((image >> 1) == group, 0, GRP)
            for b in range(4):

                @pl.when(owned & (b < count))
                def _():
                    place = target_ref[0, jnp.minimum(offset + b, GRP - 1)]
                    source[place] = side + (i & 1) * 4 + b

            offset = offset + jnp.where(owned, count, 0)
        for n, step in enumerate((2, 1, 3, 0)):
            shard = (my + step) & 3
            out_ref[2 * n] = source[2 * shard]
            out_ref[2 * n + 1] = source[2 * shard + 1]
        out_ref[8] = counts_ref[2 * group]
        out_ref[9] = counts_ref[2 * group + 1]

    (out,) = call(
        kernel,
        [((16,), jnp.int32)],
        [SMEM] * 3,
        [pltpu.SMEM((GRP,), jnp.int32)],
        moved=1 << 10,
        limit=4,
        out_specs=[SMEM],
    )(counts, owner, target)
    return out


def load_rows(rows, xo_ref, xs_ref):
    rows[0:SH, 0:DL] = xo_ref[...]
    rows[0:SH, DL:CHIP] = xs_ref[...]
    rows[SH : SH + 16, :] = jnp.ones((16, CHIP), BF16)


def row_stats(xo_ref, xs_ref):
    fo, fs = xo_ref[...].astype(F32), xs_ref[...].astype(F32)
    s1 = jnp.sum(fo, axis=1, keepdims=True) + jnp.sum(fs, axis=1, keepdims=True)
    s2 = jnp.sum(fo * fo, axis=1, keepdims=True) + jnp.sum(fs * fs, axis=1, keepdims=True)
    lane = lax.broadcasted_iota(jnp.int32, (SH, HD), 1)
    return jnp.where(lane == 0, s1, jnp.where(lane == 1, s2, F32(0.0)))


def partial_tile(rows, wo_ref, ws_ref, columns, center):
    acc = jnp.dot(rows[:, 0:DL], wo_ref[:, columns], preferred_element_type=F32)
    acc = acc + jnp.dot(rows[:, DL:CHIP], ws_ref[:, columns], preferred_element_type=F32)
    sums = acc[SH : SH + 8, :]
    return acc[0:SH, :] - center * sums[0:1, :], sums


ROWS_SCRATCH = pltpu.VMEM((SH + 16, CHIP), BF16)
PART_FLOPS = 2 * SH * CHIP * 2 * HEAD


def send_part(xo, xs, wo, ws, after):
    def kernel(xo_ref, xs_ref, wo_ref, ws_ref, out_ref, stat_ref, copy_ref, rows):
        load_rows(rows, xo_ref, xs_ref)
        copy_ref[...] = xo_ref[...]
        stat = row_stats(xo_ref, xs_ref)
        stat_ref[...] = stat
        center = stat[:, 0:1] / CHIP
        for n in range(3):
            columns = slice(n * 256, (n + 1) * 256)
            tile, _ = partial_tile(rows, wo_ref, ws_ref, columns, center)
            out_ref[:, columns] = tile.astype(BF16)

    outs = [((SH, 2 * HEAD), BF16), ((SH, HD), F32), ((SH, DL), BF16)]
    return call(kernel, outs, [VMEM] * 4, [ROWS_SCRATCH], PART_FLOPS, after=after)(xo, xs, wo, ws)


def keep_part(xo, xs, wo, ws, stat, got, after):
    def kernel(xo_ref, xs_ref, wo_ref, ws_ref, stat_ref, got_ref, own_ref, send_ref, rows):
        load_rows(rows, xo_ref, xs_ref)
        center = stat_ref[:, 0:1] / CHIP
        for n in range(6):
            columns = slice(n * HD, (n + 1) * HD)
            if n % 2 == 0:
                pair, _ = partial_tile(rows, wo_ref, ws_ref, slice(n * HD, (n + 2) * HD), center)
            tile = pair[:, (n % 2) * HD : (n % 2 + 1) * HD] + got_ref[:, columns].astype(F32)
            if n < 3:
                own_ref[:, columns] = tile
            else:
                send_ref[:, (n - 3) * HD : (n - 2) * HD] = tile.astype(BF16)

    outs = [((SH, HEAD), F32), ((SH, HEAD), BF16)]
    return call(kernel, outs, [VMEM] * 6, [ROWS_SCRATCH], LONG, after=after)(xo, xs, wo, ws, stat, got)


def whole_part(xo, xs, weights, stats, after):
    def kernel(xo_ref, xs_ref, ko_ref, ks_ref, so_ref, ss_ref, t0_ref, t1_ref, t2_ref, *refs):
        own_ref, p1_ref, p2_ref, p3_ref = refs[0:4]
        notes, rows = refs[4:8], refs[8]
        load_rows(rows, xo_ref, xs_ref)
        stat = row_stats(xo_ref, xs_ref)
        center = stat[:, 0:1] / CHIP
        for wo_ref, ws_ref, outs, js in ((so_ref, ss_ref, (p1_ref, p3_ref), (1, 3)), (ko_ref, ks_ref, (own_ref, p2_ref), (0, 2))):
            for n in range(6):
                if n % 2 == 0:
                    pair, sums = partial_tile(rows, wo_ref, ws_ref, slice(n * HD, (n + 2) * HD), center)
                half = slice((n % 2) * HD, (n % 2 + 1) * HD)
                columns = slice((n % 3) * HD, (n % 3 + 1) * HD)
                out_ref = outs[n // 3]
                out_ref[:, columns] = pair[:, half].astype(out_ref.dtype)
                notes[js[n // 3]][:, R + (n % 3) * HD : R + (n % 3 + 1) * HD] = sums[:, half]
        for k, one in enumerate((t0_ref[...], t1_ref[...], t2_ref[...], stat)):
            turned = one.T[0:8, :]
            for note in notes:
                note[:, k * SH : (k + 1) * SH] = turned

    part = ((SH, HEAD), BF16)
    note = ((8, NOTE), F32)
    outs = [((SH, HEAD), F32), part, part, part] + [note] * 4
    return call(kernel, outs, [VMEM] * 9, [ROWS_SCRATCH], LONG, after=after)(xo, xs, *weights, *stats)


def coefficients(notes):
    def kernel(n0_ref, n1_ref, n2_ref, n3_ref, coef_ref, cs_ref):
        refs = (n0_ref, n1_ref, n2_ref, n3_ref)
        sums = [n[0:1, 0:R] for n in refs]
        mean = (sums[0] + sums[1] + sums[2] + sums[3]) / D
        squares = n0_ref[1:2, 0:R] + n1_ref[1:2, 0:R] + n2_ref[1:2, 0:R] + n3_ref[1:2, 0:R]
        var = squares / D - mean * mean
        scale = lax.rsqrt(var + 1e-06)
        lines = [scale] + [s / CHIP - mean for s in sums] + [jnp.zeros((HD - 5, R), F32)]
        coef_ref[...] = jnp.concatenate(lines, axis=0).T
        for c, n in enumerate(refs):
            cs_ref[c : c + 1, :] = n[0:1, R:NOTE]
        cs_ref[4:8, :] = jnp.zeros((4, HEAD), F32)

    return call(kernel, [((R, HD), F32), ((8, HEAD), F32)], [VMEM] * 4)(*notes)


def attention(places, coef, cs, parts):
    flat = [p for chunk in parts for p in chunk]

    def kernel(places_ref, coef_ref, cs_ref, *refs):
        out_ref, qkv = refs[len(flat)], refs[len(flat) + 1]
        my = lax.axis_index("my")
        at = 0
        for k, offset in enumerate((0, 1, 3, 2)):
            coef = coef_ref[k * SH : (k + 1) * SH, :]
            total = refs[at][...]
            for more in range(1, len(parts[k])):
                total = total + refs[at + more][...].astype(F32)
            at += len(parts[k])
            for c in range(4):
                total = total + coef[:, c + 1 : c + 2] * cs_ref[c : c + 1, :]
            total = total * coef[:, 0:1]
            shard = (my + offset) & 3
            qkv[pl.ds(pl.multiple_of(shard * SH, SH), SH), :] = total.astype(BF16)
        first, second = places_ref[8], places_ref[9]
        for image in range(2):
            start = pl.multiple_of(first * BLK, BLK) if image else 0
            live = (second if image else first) * BLK
            q = qkv[pl.ds(start, IMG_ROWS), 0:HD]
            key = qkv[pl.ds(start, IMG_ROWS), HD : 2 * HD]
            value = qkv[pl.ds(start, IMG_ROWS), 2 * HD : 3 * HD]
            rows = lax.broadcasted_iota(jnp.int32, (IMG_ROWS, HD), 0)
            value = jnp.where(rows < live, value, jnp.zeros_like(value))
            scores = lax.dot_general(q, key, (((1,), (1,)), ((), ())), preferred_element_type=F32)
            columns = lax.broadcasted_iota(jnp.int32, (IMG_ROWS, IMG_ROWS), 1)
            scores = jnp.where(columns < live, scores * HD ** (-0.5), F32(-1e30))
            top = jnp.max(scores, axis=1, keepdims=True)
            powers = jnp.exp(scores - top)
            weights = (powers / jnp.sum(powers, axis=1, keepdims=True)).astype(BF16)
            mixture = jnp.dot(weights, value, preferred_element_type=F32)
            out_ref[image * IMG_ROWS : (image + 1) * IMG_ROWS, :] = mixture.astype(BF16)

    (out,) = call(
        kernel,
        [((R, HD), BF16)],
        [SMEM] + [VMEM] * (2 + len(flat)),
        [pltpu.VMEM((R, HEAD), BF16)],
        8 * IMG_ROWS * IMG_ROWS * HD,
        4 << 20,
        2 * IMG_ROWS * IMG_ROWS,
        24,
    )(places, coef, cs, *flat)
    return out


def route(places, mine, other):
    def kernel(places_ref, mine_ref, other_ref, *outs):
        for n in range(GRP):
            out_ref, at = ((outs[0], 0), (outs[1], 2), (outs[2], 6))[(0, 0, 1, 1, 1, 1, 2, 2)[n]]
            place = slice((n - at) * BLK, (n - at + 1) * BLK)
            src = places_ref[n]
            row = pl.multiple_of((src & 7) * BLK, BLK)

            @pl.when(src < 0)
            def _():
                out_ref[place, :] = jnp.zeros((BLK, HD), BF16)

            @pl.when((src >= 0) & (src < GRP))
            def _():
                out_ref[place, :] = mine_ref[pl.ds(row, BLK), :]

            @pl.when(src >= GRP)
            def _():
                out_ref[place, :] = other_ref[pl.ds(row, BLK), :]

    outs = [((SH, HD), BF16), ((2 * SH, HD), BF16), ((SH, HD), BF16)]
    return call(kernel, outs, [SMEM, VMEM, VMEM])(places, mine, other)


def project(block, wo, dtype, after):
    lane = [block] + [swap(block, "mx", 2 * j) for j in (1, 2, 3)]
    heads = lane + [swap(one, "mx", 1) for one in lane]
    count = block.shape[0] // SH

    def kernel(*refs):
        w_ref, outs, rows = refs[8], refs[9 : 9 + count], refs[9 + count]
        for h in range(8):
            rows[:, h * HD : (h + 1) * HD] = refs[h][...]
        for i, out_ref in enumerate(outs):
            for n in range(3):
                columns = slice(n * 256, (n + 1) * 256)
                tile = jnp.dot(rows[i * SH : (i + 1) * SH, :], w_ref[:, columns], preferred_element_type=F32)
                out_ref[:, columns] = tile.astype(out_ref.dtype)

    return call(
        kernel,
        [((SH, DL), dtype)] * count,
        [VMEM] * 9,
        [pltpu.VMEM((count * SH, R), BF16)],
        LONG,
        after=after,
    )(*heads, wo)


def shards(patches, tile_counts, image_owner, block_target, qkv_weight, out_weight):
    next_rows, last_rows = shift(patches, "my", 1), shift(patches, "my", -1)
    w3 = jnp.transpose(qkv_weight, (1, 0, 2))
    theirs_keep, theirs_send = weight_heads(w3, True)
    sib_send = swap(theirs_send, "mx", 1)
    sib_keep = swap(theirs_keep, "mx", 1)
    own_keep, own_send = weight_heads(w3, False)
    wo = out_weight_heads(out_weight)
    places = table(tile_counts, image_owner, block_target)

    x0, s0 = patches, swap(patches, "mx", 1)
    part0, stat0, again = send_part(x0, s0, own_send, sib_send, ())
    got0 = swap(part0, "mx", 2)
    x3 = shift(again, "my", 2)
    x1, x2 = gate([next_rows, last_rows], (part0,))
    s1, s2 = swap(x1, "mx", 1), swap(x2, "mx", 1)
    part1, stat1, _ = send_part(x1, s1, own_send, sib_send, (part0,))
    got1 = swap(part1, "mx", 2)
    part2, stat2, _ = send_part(x2, s2, own_send, sib_send, (part1,))
    got2 = swap(part2, "mx", 2)
    own0, next0 = keep_part(x0, s0, own_keep, sib_keep, stat0, got0, (part2,))
    end0 = swap(next0, "mx", 4)
    (x3,) = gate([x3], (next0,))
    s3 = swap(x3, "mx", 1)
    own1, next1 = keep_part(x1, s1, own_keep, sib_keep, stat1, got1, (next0,))
    end1 = swap(next1, "mx", 4)
    weights = (own_keep, sib_keep, own_send, sib_send)
    own3, p1, p2, p3, n0, n1, n2, n3 = whole_part(x3, s3, weights, (stat0, stat1, stat2), (next1, end0))
    end3 = (own3, swap(p2, "mx", 4), swap(p3, "mx", 6), swap(p1, "mx", 2))
    own2, next2 = keep_part(x2, s2, own_keep, sib_keep, stat2, got2, (p1,))
    end2 = swap(next2, "mx", 4)
    coef, cs = coefficients([n0, swap(n1, "mx", 2), swap(n2, "mx", 4), swap(n3, "mx", 6)])

    parts = [(own0, end0), (own1, end1), (own2, end2), end3]
    attended = attention(places, coef, cs, parts)
    other = swap(attended, "img", 1)
    across, beside, here = route(places, attended, other)

    (far,) = project(across, wo, BF16, ())
    from_far = shift(far, "my", 2)
    up, down = project(beside, wo, BF16, (far,))
    from_up, from_down = shift(up, "my", -1), shift(down, "my", 1)
    (mine,) = project(here, wo, F32, (up,))
    out = mine + from_far.astype(F32) + from_up.astype(F32) + from_down.astype(F32)
    return out.astype(BF16)


def solution(mesh):
    in_specs = (
        P(("img", "my"), "mx"),
        P(),
        P(),
        P("img", None),
        P("mx", None, "my"),
        P("my", "mx"),
    )
    out_specs = P(("img", "my"), "mx")
    return jax.shard_map(shards, mesh=mesh, in_specs=in_specs, out_specs=out_specs, check_vma=False)
```

```python
import jax
import jax.numpy as jnp
from jax import lax
from jax.experimental import pallas as pl
from jax.experimental.pallas import tpu as pltpu
from jax.sharding import PartitionSpec as P

D = 6144
HD = 128
BLK = 128
GRP = 8
R = 1024
SH = 256
DL = 768
CHIP = 2 * DL
HEAD = 3 * HD
IMG_ROWS = 512
ORDER = (0, 2, 1, 3)
EXTRA = 32
F32 = jnp.float32
BF16 = jnp.bfloat16

VMEM = pl.BlockSpec(memory_space=pltpu.VMEM)
SMEM = pl.BlockSpec(memory_space=pltpu.SMEM)
ANY = pl.BlockSpec(memory_space=pl.ANY)
HBM = pl.BlockSpec(memory_space=pltpu.HBM)


def call(kernel, outs, ins, scratch=(), limit=16, out_specs=None, after=(), aliases=None):
    out_shape = [jax.ShapeDtypeStruct(s, d) for s, d in outs]
    count = len(ins)

    def ordered(*refs):
        kernel(*refs[:count], *refs[count + len(after) :])

    made = pl.pallas_call(
        ordered,
        out_shape=out_shape,
        in_specs=list(ins) + [ANY] * len(after),
        out_specs=out_specs or [VMEM] * len(outs),
        scratch_shapes=list(scratch),
        input_output_aliases=aliases or {},
        compiler_params=pltpu.CompilerParams(vmem_limit_bytes=limit << 20),
        cost_estimate=pl.CostEstimate(flops=0, bytes_accessed=1024, transcendentals=0),
    )
    return lambda *args: made(*args, *after)


def gate(blocks, after):
    def kernel(*refs):
        pass

    outs = [(b.shape, b.dtype) for b in blocks]
    ins = [ANY] * len(blocks)
    same = {i: i for i in range(len(blocks))}
    return call(kernel, outs, ins, limit=4, out_specs=ins, after=after, aliases=same)(*blocks)


def swap(block, axis, bits):
    count = lax.axis_size(axis)
    return lax.ppermute(block, axis, [(i, i ^ bits) for i in range(count)])


def shift(block, axis, step):
    count = lax.axis_size(axis)
    return lax.ppermute(block, axis, [((i + step) % count, i) for i in range(count)])


def weight_heads(w3, sibling):
    def kernel(w_ref, keep_ref, send_ref, sems):
        mx = lax.axis_index("mx")
        z = mx >> 1
        lane = (mx & 1) ^ (1 if sibling else 0)
        copies = []
        for place in (2, 3, 0, 1):
            head = lane * 4 + (z ^ ORDER[place])
            dst = keep_ref if place < 2 else send_ref
            for s in range(3):
                copies.append(
                    pltpu.make_async_copy(
                        w_ref.at[s, :, pl.ds(pl.multiple_of(head * HD, HD), HD)],
                        dst.at[:, pl.ds((place % 2) * HEAD + s * HD, HD)],
                        sems.at[len(copies)],
                    )
                )
        for copy in copies:
            copy.start()
        for copy in copies:
            copy.wait()

    shape = ((DL, 2 * HEAD), BF16)
    return call(kernel, [shape, shape], [HBM], [pltpu.SemaphoreType.DMA((12,))])(w3)


def out_weight_heads(w):
    def kernel(w_ref, out_ref, sems):
        mx = lax.axis_index("mx")
        z = mx >> 1
        copies = []
        for side in range(2):
            lane = (mx & 1) ^ side
            for j in range(4):
                head = lane * 4 + (z ^ j)
                copies.append(
                    pltpu.make_async_copy(
                        w_ref.at[pl.ds(pl.multiple_of(head * HD, HD), HD), :],
                        out_ref.at[pl.ds((side * 4 + j) * HD, HD), :],
                        sems.at[len(copies)],
                    )
                )
        for copy in copies:
            copy.start()
        for copy in copies:
            copy.wait()

    (out,) = call(kernel, [(w.shape, BF16)], [HBM], [pltpu.SemaphoreType.DMA((8,))])(w)
    return out


def table(counts, owner, target):
    def kernel(counts_ref, owner_ref, target_ref, out_ref, source):
        group = lax.axis_index("img")
        my = lax.axis_index("my")
        for t in range(GRP):
            source[t] = -1
        base = (group >> 1) * 4
        offset = jnp.int32(0)
        for i in range(4):
            image = base + i
            count = counts_ref[image]
            owned = owner_ref[image] == group
            side = jnp.where((image >> 1) == group, 0, GRP)
            for b in range(4):

                @pl.when(owned & (b < count))
                def _():
                    place = target_ref[0, jnp.minimum(offset + b, GRP - 1)]
                    source[place] = side + (i & 1) * 4 + b

            offset = offset + jnp.where(owned, count, 0)
        for n, step in enumerate((2, 1, 3, 0)):
            shard = (my + step) & 3
            out_ref[2 * n] = source[2 * shard]
            out_ref[2 * n + 1] = source[2 * shard + 1]
        out_ref[8] = counts_ref[2 * group]
        out_ref[9] = counts_ref[2 * group + 1]

    (out,) = call(
        kernel,
        [((16,), jnp.int32)],
        [SMEM] * 3,
        [pltpu.SMEM((GRP,), jnp.int32)],
        limit=4,
        out_specs=[SMEM],
    )(counts, owner, target)
    return out


def load_rows(rows, xo_ref, xs_ref):
    count = xo_ref.shape[0]
    rows[0:count, 0:DL] = xo_ref[...]
    rows[0:count, DL:CHIP] = xs_ref[...]
    rows[count : count + 16, :] = jnp.ones((16, CHIP), BF16)


def row_stats(xo_ref, xs_ref):
    fo, fs = xo_ref[...].astype(F32), xs_ref[...].astype(F32)
    s1 = jnp.sum(fo, axis=1, keepdims=True) + jnp.sum(fs, axis=1, keepdims=True)
    s2 = jnp.sum(fo * fo, axis=1, keepdims=True) + jnp.sum(fs * fs, axis=1, keepdims=True)
    lane = lax.broadcasted_iota(jnp.int32, (xo_ref.shape[0], HD), 1)
    return jnp.where(lane == 0, s1, jnp.where(lane == 1, s2, F32(0.0)))


def partial_tile(rows, wo_ref, ws_ref, columns, center):
    count = center.shape[0]
    acc = jnp.dot(rows[:, 0:DL], wo_ref[:, columns], preferred_element_type=F32)
    acc = acc + jnp.dot(rows[:, DL:CHIP], ws_ref[:, columns], preferred_element_type=F32)
    sums = acc[count : count + 8, :]
    return acc[0:count, :] - center * sums[0:1, :], sums


def rows_scratch(count):
    return pltpu.VMEM((count + 16, CHIP), BF16)


def send_part(xo, xs, wo, ws, after=()):
    count = xo.shape[0]

    def kernel(xo_ref, xs_ref, wo_ref, ws_ref, out_ref, stat_ref, copy_ref, rows):
        load_rows(rows, xo_ref, xs_ref)
        copy_ref[...] = xo_ref[...]
        stat = row_stats(xo_ref, xs_ref)
        stat_ref[...] = stat
        center = stat[:, 0:1] / CHIP
        for n in range(3):
            columns = slice(n * 256, (n + 1) * 256)
            tile, _ = partial_tile(rows, wo_ref, ws_ref, columns, center)
            out_ref[:, columns] = tile.astype(BF16)

    outs = [((count, 2 * HEAD), BF16), ((count, HD), F32), ((count, DL), BF16)]
    return call(kernel, outs, [VMEM] * 4, [rows_scratch(count)], after=after)(xo, xs, wo, ws)


def keep_part(xo, xs, wo, ws, stat, got, more=None, pieces=1, after=()):
    count = xo.shape[0]
    size = count // pieces
    extra = list(more or ())

    def kernel(xo_ref, xs_ref, wo_ref, ws_ref, stat_ref, got_ref, *refs):
        refs, rows = refs[:-1], refs[-1]
        own_ref, sends = refs[len(extra)], refs[len(extra) + 1 : len(extra) + 1 + pieces]
        load_rows(rows, xo_ref, xs_ref)
        center = stat_ref[:, 0:1] / CHIP
        for n in reversed(range(6)):
            columns = slice(n * HD, (n + 1) * HD)
            if n % 2 == 1:
                pair, _ = partial_tile(rows, wo_ref, ws_ref, slice((n - 1) * HD, (n + 1) * HD), center)
            tile = pair[:, (n % 2) * HD : (n % 2 + 1) * HD] + got_ref[:, columns].astype(F32)
            if n < 3:
                own_ref[:, columns] = tile
            else:
                for i, send_ref in enumerate(sends):
                    send_ref[:, (n - 3) * HD : (n - 2) * HD] = tile[i * size : (i + 1) * size, :].astype(BF16)
        if extra:
            refs[-1][...] = refs[0][...] + refs[1][...].astype(F32)

    outs = [((count, HEAD), F32)] + [((size, HEAD), BF16)] * pieces
    outs += [((SH, HEAD), F32)] if extra else []
    ins = [VMEM] * (6 + len(extra))
    return call(kernel, outs, ins, [rows_scratch(count)], after=after)(xo, xs, wo, ws, stat, got, *extra)


def whole_tiles(refs, sends, own_ref, rows, center, done):
    ko_ref, ks_ref, so_ref, ss_ref = refs
    p1_ref, p2_ref, p3_ref = sends
    count = center.shape[0]
    for wo_ref, ws_ref, outs, js in ((so_ref, ss_ref, (p1_ref, p3_ref), (1, 3)), (ko_ref, ks_ref, (own_ref, p2_ref), (0, 2))):
        for n in range(0, 6, 2):
            pair, sums = partial_tile(rows, wo_ref, ws_ref, slice(n * HD, (n + 2) * HD), center)
            for h in range(2):
                half = slice(h * HD, (h + 1) * HD)
                side, place = divmod(n + h, 3)
                out_ref = outs[side]
                out_ref[0:count, place * HD : (place + 1) * HD] = pair[:, half].astype(out_ref.dtype)
                done(js[side], place, sums[:, half])


def last_part(xo, xs, weights, stats, after):
    def kernel(xo_ref, xs_ref, *refs):
        ws, (t0_ref, t12_ref) = refs[0:4], refs[4:6]
        own_ref, p1_ref, p2_ref, p3_ref, note_ref, rows = refs[6:]
        load_rows(rows, xo_ref, xs_ref)
        stat = row_stats(xo_ref, xs_ref)
        turned = [one[k * SH : (k + 1) * SH, :].T for one, k in ((t0_ref, 0), (t12_ref, 0), (t12_ref, 1), (stat, 0))]
        sums = jnp.concatenate([t[0:1, :] for t in turned] + [t[1:2, :] for t in turned], axis=0)
        column_sums = {}

        def done(j, place, tile_sums):
            column_sums[j, place] = tile_sums[0:1, :]

        whole_tiles(ws, (p1_ref, p2_ref, p3_ref), own_ref, rows, stat[:, 0:1] / CHIP, done)
        for j, ref in enumerate((note_ref, p1_ref, p2_ref, p3_ref)):
            heads = [column_sums[j, place] for place in range(3)] + [jnp.zeros((5, HD), F32)]
            note = jnp.concatenate([sums, jnp.concatenate(heads, axis=0)], axis=1)
            if j == 0:
                ref[...] = note
                continue
            terms = []
            for _ in range(3):
                terms.append(note.astype(BF16).astype(F32))
                note = note - terms[-1]
            terms.append(jnp.zeros((8, HEAD), F32))
            ref[SH : SH + EXTRA, :] = jnp.concatenate(terms, axis=0).astype(BF16)

    part = ((SH + EXTRA, HEAD), BF16)
    outs = [((SH, HEAD), F32), part, part, part, ((8, HEAD), F32)]
    return call(kernel, outs, [VMEM] * 8, [rows_scratch(SH)], after=after)(xo, xs, *weights, *stats)


def last_sum(own, got, note):
    def kernel(own_ref, g1_ref, g2_ref, g3_ref, note_ref, out_ref, coef_ref, cs_ref):
        total = own_ref[...]
        notes = [note_ref[...]]
        for ref in (g1_ref, g2_ref, g3_ref):
            total = total + ref[0:SH, :].astype(F32)
            terms = ref[SH : SH + EXTRA, :].astype(F32)
            notes.append(terms[0:8, :] + terms[8:16, :] + terms[16:24, :])
        out_ref[...] = total
        for k in range(4):
            sums = [n[k : k + 1, 0:SH] for n in notes]
            squares = [n[4 + k : 5 + k, 0:SH] for n in notes]
            mean = (sums[0] + sums[1] + sums[2] + sums[3]) / D
            var = (squares[0] + squares[1] + squares[2] + squares[3]) / D - mean * mean
            lines = [lax.rsqrt(var + 1e-06)] + [s / CHIP - mean for s in sums] + [jnp.zeros((HD - 5, SH), F32)]
            coef_ref[k * SH : (k + 1) * SH, :] = jnp.concatenate(lines, axis=0).T
        for c, n in enumerate(notes):
            for place in range(3):
                cs_ref[c : c + 1, place * HD : (place + 1) * HD] = n[place : place + 1, SH:HEAD]
        cs_ref[4:8, :] = jnp.zeros((4, HEAD), F32)

    outs = [((SH, HEAD), F32), ((R, HD), F32), ((8, HEAD), F32)]
    return call(kernel, outs, [VMEM] * 5)(own, *got, note)


def join(blocks, axis, after=()):
    size = blocks[0].shape[axis]

    def kernel(*refs):
        for i, ref in enumerate(refs[:-1]):
            at = slice(i * size, (i + 1) * size)
            if axis == 0:
                refs[-1][at, :] = ref[...]
            else:
                refs[-1][:, at] = ref[...]

    shape = list(blocks[0].shape)
    shape[axis] *= len(blocks)
    (out,) = call(kernel, [(tuple(shape), BF16)], [VMEM] * len(blocks), after=after)(*blocks)
    return out


def attention(places, coef, cs, tot0, own12, ends, tot3):
    def kernel(places_ref, coef_ref, cs_ref, tot0_ref, own12_ref, end1_ref, end2_ref, tot3_ref, out_ref, qkv):
        my = lax.axis_index("my")
        for k, offset in enumerate((0, 1, 3, 2)):
            if k in (1, 2):
                end_ref = end1_ref if k == 1 else end2_ref
                total = own12_ref[(k - 1) * SH : k * SH, :] + end_ref[...].astype(F32)
            else:
                total = (tot3_ref if k else tot0_ref)[...]
            coef = coef_ref[k * SH : (k + 1) * SH, :]
            for c in range(4):
                total = total + coef[:, c + 1 : c + 2] * cs_ref[c : c + 1, :]
            total = total * coef[:, 0:1]
            shard = (my + offset) & 3
            qkv[pl.ds(pl.multiple_of(shard * SH, SH), SH), :] = total.astype(BF16)
        first, second = places_ref[8], places_ref[9]
        for image in range(2):
            start = pl.multiple_of(first * BLK, BLK) if image else 0
            live = (second if image else first) * BLK
            q = qkv[pl.ds(start, IMG_ROWS), 0:HD]
            key = qkv[pl.ds(start, IMG_ROWS), HD : 2 * HD]
            value = qkv[pl.ds(start, IMG_ROWS), 2 * HD : 3 * HD]
            rows = lax.broadcasted_iota(jnp.int32, (IMG_ROWS, HD), 0)
            value = jnp.where(rows < live, value, jnp.zeros_like(value))
            scores = lax.dot_general(q, key, (((1,), (1,)), ((), ())), preferred_element_type=F32)
            columns = lax.broadcasted_iota(jnp.int32, (IMG_ROWS, IMG_ROWS), 1)
            scores = jnp.where(columns < live, scores * HD ** (-0.5), F32(-1e30))
            top = jnp.max(scores, axis=1, keepdims=True)
            powers = jnp.exp(scores - top)
            weights = (powers / jnp.sum(powers, axis=1, keepdims=True)).astype(BF16)
            mixture = jnp.dot(weights, value, preferred_element_type=F32)
            out_ref[image * IMG_ROWS : (image + 1) * IMG_ROWS, :] = mixture.astype(BF16)

    (out,) = call(
        kernel, [((R, HD), BF16)], [SMEM] + [VMEM] * 7, [pltpu.VMEM((R, HEAD), BF16)], limit=24
    )(places, coef, cs, tot0, own12, *ends, tot3)
    return out


def route(places, mine, other):
    def kernel(places_ref, mine_ref, other_ref, *outs):
        for n in range(GRP):
            out_ref, at = (outs[0], n) if n < 6 else (outs[1], n - 6)
            place = slice(at * BLK, (at + 1) * BLK)
            src = places_ref[n]
            row = pl.multiple_of((src & 7) * BLK, BLK)

            @pl.when(src < 0)
            def _():
                out_ref[place, :] = jnp.zeros((BLK, HD), BF16)

            @pl.when((src >= 0) & (src < GRP))
            def _():
                out_ref[place, :] = mine_ref[pl.ds(row, BLK), :]

            @pl.when(src >= GRP)
            def _():
                out_ref[place, :] = other_ref[pl.ds(row, BLK), :]

    outs = [((3 * SH, HD), BF16), ((SH, HD), BF16)]
    return call(kernel, outs, [SMEM, VMEM, VMEM])(places, mine, other)


def project(block, wo, dtype, after=()):
    lane = join([block] + [swap(block, "mx", 2 * j) for j in (1, 2, 3)], 1, after)
    sib = swap(lane, "mx", 1)
    count = block.shape[0] // SH

    def kernel(lane_ref, sib_ref, w_ref, *outs):
        for i, out_ref in enumerate(outs):
            at = slice(i * SH, (i + 1) * SH)
            for n in range(3):
                columns = slice(n * 256, (n + 1) * 256)
                tile = jnp.dot(lane_ref[at, :], w_ref[0 : 4 * HD, columns], preferred_element_type=F32)
                tile = tile + jnp.dot(sib_ref[at, :], w_ref[4 * HD :, columns], preferred_element_type=F32)
                out_ref[:, columns] = tile.astype(dtype)

    return call(kernel, [((SH, DL), dtype)] * count, [VMEM] * 3)(lane, sib, wo)


def shards(patches, tile_counts, image_owner, block_target, qkv_weight, out_weight):
    scope = jax.named_scope
    with scope("rows_near"):
        next_rows, last_rows = shift(patches, "my", 1), shift(patches, "my", -1)
    w3 = jnp.transpose(qkv_weight, (1, 0, 2))
    with scope("weights"):
        theirs_keep, theirs_send = weight_heads(w3, True)
        sib_send = swap(theirs_send, "mx", 1)
        sib_keep = swap(theirs_keep, "mx", 1)
        own_keep, own_send = weight_heads(w3, False)
        wo = out_weight_heads(out_weight)
        places = table(tile_counts, image_owner, block_target)
    weights = (own_keep, sib_keep, own_send, sib_send)

    with scope("chunk0"):
        s0 = swap(patches, "mx", 1)
        part0, stat0, again = send_part(patches, s0, own_send, sib_send)
        got0 = swap(part0, "mx", 2)
    with scope("rows_far"):
        x3 = shift(again, "my", 2)
    with scope("chunk12"):
        x12 = join([next_rows, last_rows], 0, (got0,))
        s12 = swap(x12, "mx", 1)
    with scope("sum0"):
        own0, next0 = keep_part(patches, s0, own_keep, sib_keep, stat0, got0)
        end0 = swap(next0, "mx", 4)
    with scope("chunk12"):
        part12, stat12, _ = send_part(x12, s12, own_send, sib_send, (next0,))
        got12 = swap(part12, "mx", 2)
    with scope("chunk3"):
        (x3,) = gate([x3], (part12,))
        s3 = swap(x3, "mx", 1)
        own3, p1, p2, p3, note = last_part(x3, s3, weights, (stat0, stat12), (part12, wo, places))
        got3 = [swap(p1, "mx", 2), swap(p2, "mx", 4), swap(p3, "mx", 6)]
    with scope("sum12"):
        own12, next1, next2, tot0 = keep_part(x12, s12, own_keep, sib_keep, stat12, got12, (own0, end0), 2, (own3,))
        ends = [swap(next1, "mx", 4), swap(next2, "mx", 4)]
    with scope("sum3"):
        tot3, coef, cs = last_sum(own3, got3, note)

    with scope("attention"):
        attended = attention(places, coef, cs, tot0, own12, ends, tot3)
        other = swap(attended, "img", 1)
        across, here = route(places, attended, other)

    with scope("out"):
        far, up, down = project(across, wo, BF16)
        arrived = [shift(far, "my", 2), shift(up, "my", -1), shift(down, "my", 1)]
    with scope("own_out"):
        (mine,) = project(here, wo, F32)
    for one in arrived:
        mine = mine + one.astype(F32)
    return mine.astype(BF16)


def solution(mesh):
    in_specs = (
        P(("img", "my"), "mx"),
        P(),
        P(),
        P("img", None),
        P("mx", None, "my"),
        P("my", "mx"),
    )
    out_specs = P(("img", "my"), "mx")
    return jax.shard_map(shards, mesh=mesh, in_specs=in_specs, out_specs=out_specs, check_vma=False)
```

```python
import jax
import jax.numpy as jnp
from jax import lax
from jax.experimental import pallas as pl
from jax.experimental.pallas import tpu as pltpu
from jax.sharding import PartitionSpec as P

D = 6144
HD = 128
BLK = 128
GRP = 8
R = 1024
SH = 256
DL = 768
CHIP = 2 * DL
HEAD = 3 * HD
IMG_ROWS = 512
ORDER = (0, 2, 1, 3)
EXTRA = 32
F32 = jnp.float32
BF16 = jnp.bfloat16

VMEM = pl.BlockSpec(memory_space=pltpu.VMEM)
SMEM = pl.BlockSpec(memory_space=pltpu.SMEM)
ANY = pl.BlockSpec(memory_space=pl.ANY)
HBM = pl.BlockSpec(memory_space=pltpu.HBM)


def call(kernel, outs, ins, scratch=(), limit=16, out_specs=None, after=(), aliases=None):
    out_shape = [jax.ShapeDtypeStruct(s, d) for s, d in outs]
    count = len(ins)

    def ordered(*refs):
        kernel(*refs[:count], *refs[count + len(after) :])

    made = pl.pallas_call(
        ordered,
        out_shape=out_shape,
        in_specs=list(ins) + [ANY] * len(after),
        out_specs=out_specs or [VMEM] * len(outs),
        scratch_shapes=list(scratch),
        input_output_aliases=aliases or {},
        compiler_params=pltpu.CompilerParams(vmem_limit_bytes=limit << 20),
        cost_estimate=pl.CostEstimate(flops=0, bytes_accessed=1024, transcendentals=0),
    )
    return lambda *args: made(*args, *after)


def gate(blocks, after):
    def kernel(*refs):
        pass

    outs = [(b.shape, b.dtype) for b in blocks]
    ins = [ANY] * len(blocks)
    same = {i: i for i in range(len(blocks))}
    return call(kernel, outs, ins, limit=4, out_specs=ins, after=after, aliases=same)(*blocks)


def swap(block, axis, bits):
    count = lax.axis_size(axis)
    return lax.ppermute(block, axis, [(i, i ^ bits) for i in range(count)])


def shift(block, axis, step):
    count = lax.axis_size(axis)
    return lax.ppermute(block, axis, [((i + step) % count, i) for i in range(count)])


def weight_heads(w3, sibling):
    def kernel(w_ref, keep_ref, send_ref, sems):
        mx = lax.axis_index("mx")
        z = mx >> 1
        lane = (mx & 1) ^ (1 if sibling else 0)
        copies = []
        for place in (2, 3, 0, 1):
            head = lane * 4 + (z ^ ORDER[place])
            dst = keep_ref if place < 2 else send_ref
            for s in range(3):
                copies.append(
                    pltpu.make_async_copy(
                        w_ref.at[s, :, pl.ds(pl.multiple_of(head * HD, HD), HD)],
                        dst.at[:, pl.ds((place % 2) * HEAD + s * HD, HD)],
                        sems.at[len(copies)],
                    )
                )
        for copy in copies:
            copy.start()
        for copy in copies:
            copy.wait()

    shape = ((DL, 2 * HEAD), BF16)
    return call(kernel, [shape, shape], [HBM], [pltpu.SemaphoreType.DMA((12,))])(w3)


def table(counts, owner, target):
    def kernel(counts_ref, owner_ref, target_ref, out_ref, source):
        group = lax.axis_index("img")
        my = lax.axis_index("my")
        for t in range(GRP):
            source[t] = -1
        base = (group >> 1) * 4
        offset = jnp.int32(0)
        for i in range(4):
            image = base + i
            count = counts_ref[image]
            owned = owner_ref[image] == group
            side = jnp.where((image >> 1) == group, 0, GRP)
            for b in range(4):

                @pl.when(owned & (b < count))
                def _():
                    place = target_ref[0, jnp.minimum(offset + b, GRP - 1)]
                    source[place] = side + (i & 1) * 4 + b

            offset = offset + jnp.where(owned, count, 0)
        for n, step in enumerate((2, 1, 3, 0)):
            shard = (my + step) & 3
            out_ref[2 * n] = source[2 * shard]
            out_ref[2 * n + 1] = source[2 * shard + 1]
        out_ref[8] = counts_ref[2 * group]
        out_ref[9] = counts_ref[2 * group + 1]

    (out,) = call(
        kernel,
        [((16,), jnp.int32)],
        [SMEM] * 3,
        [pltpu.SMEM((GRP,), jnp.int32)],
        limit=4,
        out_specs=[SMEM],
    )(counts, owner, target)
    return out


def load_rows(rows, xo_ref, xs_ref):
    count = xo_ref.shape[0]
    rows[0:count, 0:DL] = xo_ref[...]
    rows[0:count, DL:CHIP] = xs_ref[...]
    rows[count : count + 16, :] = jnp.ones((16, CHIP), BF16)


def row_stats(xo_ref, xs_ref):
    fo, fs = xo_ref[...].astype(F32), xs_ref[...].astype(F32)
    s1 = jnp.sum(fo, axis=1, keepdims=True) + jnp.sum(fs, axis=1, keepdims=True)
    s2 = jnp.sum(fo * fo, axis=1, keepdims=True) + jnp.sum(fs * fs, axis=1, keepdims=True)
    lane = lax.broadcasted_iota(jnp.int32, (xo_ref.shape[0], HD), 1)
    return jnp.where(lane == 0, s1, jnp.where(lane == 1, s2, F32(0.0)))


def partial_tile(rows, wo_ref, ws_ref, columns, center):
    count = center.shape[0]
    acc = jnp.dot(rows[:, 0:DL], wo_ref[:, columns], preferred_element_type=F32)
    acc = acc + jnp.dot(rows[:, DL:CHIP], ws_ref[:, columns], preferred_element_type=F32)
    sums = acc[count : count + 8, :]
    return acc[0:count, :] - center * sums[0:1, :], sums


def rows_scratch(count):
    return pltpu.VMEM((count + 16, CHIP), BF16)


def send_part(xo, xs, wo, ws, after=()):
    count = xo.shape[0]

    def kernel(xo_ref, xs_ref, wo_ref, ws_ref, out_ref, stat_ref, copy_ref, rows):
        load_rows(rows, xo_ref, xs_ref)
        copy_ref[...] = xo_ref[...]
        stat = row_stats(xo_ref, xs_ref)
        stat_ref[...] = stat
        center = stat[:, 0:1] / CHIP
        for n in range(3):
            columns = slice(n * 256, (n + 1) * 256)
            tile, _ = partial_tile(rows, wo_ref, ws_ref, columns, center)
            out_ref[:, columns] = tile.astype(BF16)

    outs = [((count, 2 * HEAD), BF16), ((count, HD), F32), ((count, DL), BF16)]
    return call(kernel, outs, [VMEM] * 4, [rows_scratch(count)], after=after)(xo, xs, wo, ws)


def keep_part(xo, xs, wo, ws, stat, got, more=None, pieces=1, after=()):
    count = xo.shape[0]
    size = count // pieces
    extra = list(more or ())

    def kernel(xo_ref, xs_ref, wo_ref, ws_ref, stat_ref, got_ref, *refs):
        refs, rows = refs[:-1], refs[-1]
        own_ref, sends = refs[len(extra)], refs[len(extra) + 1 : len(extra) + 1 + pieces]
        load_rows(rows, xo_ref, xs_ref)
        center = stat_ref[:, 0:1] / CHIP
        for n in reversed(range(6)):
            columns = slice(n * HD, (n + 1) * HD)
            if n % 2 == 1:
                pair, _ = partial_tile(rows, wo_ref, ws_ref, slice((n - 1) * HD, (n + 1) * HD), center)
            tile = pair[:, (n % 2) * HD : (n % 2 + 1) * HD] + got_ref[:, columns].astype(F32)
            if n < 3:
                own_ref[:, columns] = tile
            else:
                for i, send_ref in enumerate(sends):
                    send_ref[:, (n - 3) * HD : (n - 2) * HD] = tile[i * size : (i + 1) * size, :].astype(BF16)
        if extra:
            refs[-1][...] = refs[0][...] + refs[1][...].astype(F32)

    outs = [((count, HEAD), F32)] + [((size, HEAD), BF16)] * pieces
    outs += [((SH, HEAD), F32)] if extra else []
    ins = [VMEM] * (6 + len(extra))
    return call(kernel, outs, ins, [rows_scratch(count)], after=after)(xo, xs, wo, ws, stat, got, *extra)


def whole_tiles(refs, sends, own_ref, rows, center, done):
    ko_ref, ks_ref, so_ref, ss_ref = refs
    p1_ref, p2_ref, p3_ref = sends
    count = center.shape[0]
    for wo_ref, ws_ref, outs, js in ((so_ref, ss_ref, (p1_ref, p3_ref), (1, 3)), (ko_ref, ks_ref, (own_ref, p2_ref), (0, 2))):
        for n in range(0, 6, 2):
            pair, sums = partial_tile(rows, wo_ref, ws_ref, slice(n * HD, (n + 2) * HD), center)
            for h in range(2):
                half = slice(h * HD, (h + 1) * HD)
                side, place = divmod(n + h, 3)
                out_ref = outs[side]
                out_ref[0:count, place * HD : (place + 1) * HD] = pair[:, half].astype(out_ref.dtype)
                done(js[side], place, sums[:, half])


def last_part(xo, xs, weights, stats, after):
    def kernel(xo_ref, xs_ref, *refs):
        ws, (t0_ref, t12_ref) = refs[0:4], refs[4:6]
        own_ref, p1_ref, p2_ref, p3_ref, note_ref, rows = refs[6:]
        load_rows(rows, xo_ref, xs_ref)
        stat = row_stats(xo_ref, xs_ref)
        turned = [one[k * SH : (k + 1) * SH, :].T for one, k in ((t0_ref, 0), (t12_ref, 0), (t12_ref, 1), (stat, 0))]
        sums = jnp.concatenate([t[0:1, :] for t in turned] + [t[1:2, :] for t in turned], axis=0)
        column_sums = {}

        def done(j, place, tile_sums):
            column_sums[j, place] = tile_sums[0:1, :]

        whole_tiles(ws, (p1_ref, p2_ref, p3_ref), own_ref, rows, stat[:, 0:1] / CHIP, done)
        for j, ref in enumerate((note_ref, p1_ref, p2_ref, p3_ref)):
            heads = [column_sums[j, place] for place in range(3)] + [jnp.zeros((5, HD), F32)]
            note = jnp.concatenate([sums, jnp.concatenate(heads, axis=0)], axis=1)
            if j == 0:
                ref[...] = note
                continue
            terms = []
            for _ in range(3):
                terms.append(note.astype(BF16).astype(F32))
                note = note - terms[-1]
            terms.append(jnp.zeros((8, HEAD), F32))
            ref[SH : SH + EXTRA, :] = jnp.concatenate(terms, axis=0).astype(BF16)

    part = ((SH + EXTRA, HEAD), BF16)
    outs = [((SH, HEAD), F32), part, part, part, ((8, HEAD), F32)]
    return call(kernel, outs, [VMEM] * 8, [rows_scratch(SH)], after=after)(xo, xs, *weights, *stats)


def last_sum(own, got, note):
    def kernel(own_ref, g1_ref, g2_ref, g3_ref, note_ref, out_ref, coef_ref, cs_ref):
        total = own_ref[...]
        notes = [note_ref[...]]
        for ref in (g1_ref, g2_ref, g3_ref):
            total = total + ref[0:SH, :].astype(F32)
            terms = ref[SH : SH + EXTRA, :].astype(F32)
            notes.append(terms[0:8, :] + terms[8:16, :] + terms[16:24, :])
        out_ref[...] = total
        for k in range(4):
            sums = [n[k : k + 1, 0:SH] for n in notes]
            squares = [n[4 + k : 5 + k, 0:SH] for n in notes]
            mean = (sums[0] + sums[1] + sums[2] + sums[3]) / D
            var = (squares[0] + squares[1] + squares[2] + squares[3]) / D - mean * mean
            lines = [lax.rsqrt(var + 1e-06)] + [s / CHIP - mean for s in sums] + [jnp.zeros((HD - 5, SH), F32)]
            coef_ref[k * SH : (k + 1) * SH, :] = jnp.concatenate(lines, axis=0).T
        for c, n in enumerate(notes):
            for place in range(3):
                cs_ref[c : c + 1, place * HD : (place + 1) * HD] = n[place : place + 1, SH:HEAD]
        cs_ref[4:8, :] = jnp.zeros((4, HEAD), F32)

    outs = [((SH, HEAD), F32), ((R, HD), F32), ((8, HEAD), F32)]
    return call(kernel, outs, [VMEM] * 5)(own, *got, note)


def join(blocks, axis, after=()):
    size = blocks[0].shape[axis]

    def kernel(*refs):
        for i, ref in enumerate(refs[:-1]):
            at = slice(i * size, (i + 1) * size)
            if axis == 0:
                refs[-1][at, :] = ref[...]
            else:
                refs[-1][:, at] = ref[...]

    shape = list(blocks[0].shape)
    shape[axis] *= len(blocks)
    (out,) = call(kernel, [(tuple(shape), BF16)], [VMEM] * len(blocks), after=after)(*blocks)
    return out


def attention(places, coef, cs, tot0, own12, ends, tot3):
    def kernel(places_ref, coef_ref, cs_ref, tot0_ref, own12_ref, end1_ref, end2_ref, tot3_ref, out_ref, qkv):
        my = lax.axis_index("my")
        for k, offset in enumerate((0, 1, 3, 2)):
            if k in (1, 2):
                end_ref = end1_ref if k == 1 else end2_ref
                total = own12_ref[(k - 1) * SH : k * SH, :] + end_ref[...].astype(F32)
            else:
                total = (tot3_ref if k else tot0_ref)[...]
            coef = coef_ref[k * SH : (k + 1) * SH, :]
            for c in range(4):
                total = total + coef[:, c + 1 : c + 2] * cs_ref[c : c + 1, :]
            total = total * coef[:, 0:1]
            shard = (my + offset) & 3
            qkv[pl.ds(pl.multiple_of(shard * SH, SH), SH), :] = total.astype(BF16)
        first, second = places_ref[8], places_ref[9]
        for image in range(2):
            start = pl.multiple_of(first * BLK, BLK) if image else 0
            live = (second if image else first) * BLK
            q = qkv[pl.ds(start, IMG_ROWS), 0:HD]
            key = qkv[pl.ds(start, IMG_ROWS), HD : 2 * HD]
            value = qkv[pl.ds(start, IMG_ROWS), 2 * HD : 3 * HD]
            rows = lax.broadcasted_iota(jnp.int32, (IMG_ROWS, HD), 0)
            value = jnp.where(rows < live, value, jnp.zeros_like(value))
            scores = lax.dot_general(q, key, (((1,), (1,)), ((), ())), preferred_element_type=F32)
            columns = lax.broadcasted_iota(jnp.int32, (IMG_ROWS, IMG_ROWS), 1)
            scores = jnp.where(columns < live, scores * HD ** (-0.5), F32(-1e30))
            top = jnp.max(scores, axis=1, keepdims=True)
            powers = jnp.exp(scores - top)
            weights = (powers / jnp.sum(powers, axis=1, keepdims=True)).astype(BF16)
            mixture = jnp.dot(weights, value, preferred_element_type=F32)
            out_ref[image * IMG_ROWS : (image + 1) * IMG_ROWS, :] = mixture.astype(BF16)

    (out,) = call(
        kernel, [((R, HD), BF16)], [SMEM] + [VMEM] * 7, [pltpu.VMEM((R, HEAD), BF16)], limit=24
    )(places, coef, cs, tot0, own12, *ends, tot3)
    return out


def route(places, mine, other):
    def kernel(places_ref, mine_ref, other_ref, *outs):
        for n in range(GRP):
            out_ref = outs[n // 2]
            place = slice((n % 2) * BLK, (n % 2 + 1) * BLK)
            src = places_ref[n]
            row = pl.multiple_of((src & 7) * BLK, BLK)

            @pl.when(src < 0)
            def _():
                out_ref[place, :] = jnp.zeros((BLK, HD), BF16)

            @pl.when((src >= 0) & (src < GRP))
            def _():
                out_ref[place, :] = mine_ref[pl.ds(row, BLK), :]

            @pl.when(src >= GRP)
            def _():
                out_ref[place, :] = other_ref[pl.ds(row, BLK), :]

    return call(kernel, [((SH, HD), BF16)] * 4, [SMEM, VMEM, VMEM])(places, mine, other)


def lane_rows(blocks):
    def kernel(*refs):
        z = lax.axis_index("mx") >> 1
        for j, ref in enumerate(refs[:-1]):
            for d in range(4):
                at = pl.multiple_of((d * 4 + (z ^ j)) * HD, HD)
                refs[-1][:, pl.ds(at, HD)] = ref[:, d * HD : (d + 1) * HD]

    (out,) = call(kernel, [((SH, 16 * HD), BF16)], [VMEM] * 4)(*blocks)
    return out


def project(lane, sib, weight):
    def kernel(lane_ref, sib_ref, w_ref, out_ref):
        my = lax.axis_index("my")
        side = lax.axis_index("mx") & 1
        for n in range(3):
            columns = slice(n * 256, (n + 1) * 256)
            total = jnp.zeros((SH, 256), F32)
            for d, offset in enumerate((0, 1, 3, 2)):
                base = ((my + offset) & 3) * R
                for ref, lane_side in ((lane_ref, side), (sib_ref, 1 - side)):
                    row = pl.multiple_of(base + lane_side * 4 * HD, 4 * HD)
                    part = ref[:, d * 4 * HD : (d + 1) * 4 * HD]
                    total = total + jnp.dot(part, w_ref[pl.ds(row, 4 * HD), columns], preferred_element_type=F32)
            out_ref[:, columns] = total.astype(BF16)

    (out,) = call(kernel, [((SH, DL), BF16)], [VMEM] * 3, limit=24)(lane, sib, weight)
    return out


def shards(patches, tile_counts, image_owner, block_target, qkv_weight, out_weight):
    scope = jax.named_scope
    with scope("rows_near"):
        next_rows, last_rows = shift(patches, "my", 1), shift(patches, "my", -1)
    w3 = jnp.transpose(qkv_weight, (1, 0, 2))
    with scope("weights"):
        theirs_keep, theirs_send = weight_heads(w3, True)
        sib_send = swap(theirs_send, "mx", 1)
        sib_keep = swap(theirs_keep, "mx", 1)
        own_keep, own_send = weight_heads(w3, False)
        places = table(tile_counts, image_owner, block_target)
    weights = (own_keep, sib_keep, own_send, sib_send)

    with scope("chunk0"):
        s0 = swap(patches, "mx", 1)
        part0, stat0, again = send_part(patches, s0, own_send, sib_send)
        got0 = swap(part0, "mx", 2)
    with scope("rows_far"):
        x3 = shift(again, "my", 2)
    with scope("chunk12"):
        x12 = join([next_rows, last_rows], 0, (got0,))
        s12 = swap(x12, "mx", 1)
    with scope("out_weight"):
        (held,) = gate([out_weight], (x12,))
        whole_weight = lax.all_gather(held, "my", axis=0, tiled=True)
    with scope("sum0"):
        own0, next0 = keep_part(patches, s0, own_keep, sib_keep, stat0, got0)
        end0 = swap(next0, "mx", 4)
    with scope("chunk12"):
        part12, stat12, _ = send_part(x12, s12, own_send, sib_send, (next0,))
        got12 = swap(part12, "mx", 2)
    with scope("chunk3"):
        (x3,) = gate([x3], (part12, end0))
        s3 = swap(x3, "mx", 1)
        own3, p1, p2, p3, note = last_part(x3, s3, weights, (stat0, stat12), (part12, places))
        got3 = [swap(p1, "mx", 2), swap(p2, "mx", 4), swap(p3, "mx", 6)]
    with scope("sum12"):
        own12, next1, next2, tot0 = keep_part(x12, s12, own_keep, sib_keep, stat12, got12, (own0, end0), 2, (own3,))
        ends = [swap(next1, "mx", 4), swap(next2, "mx", 4)]
    with scope("sum3"):
        tot3, coef, cs = last_sum(own3, got3, note)

    with scope("attention"):
        attended = attention(places, coef, cs, tot0, own12, ends, tot3)
        other = swap(attended, "img", 1)
        far, up, down, own = route(places, attended, other)
        near = [own, shift(down, "my", 1), shift(up, "my", -1), shift(far, "my", 2)]

    with scope("out"):
        block = join(near, 1)
        lane = lane_rows([block] + [swap(block, "mx", 2 * j) for j in (1, 2, 3)])
        return project(lane, swap(lane, "mx", 1), whole_weight)


def solution(mesh):
    in_specs = (
        P(("img", "my"), "mx"),
        P(),
        P(),
        P("img", None),
        P("mx", None, "my"),
        P("my", "mx"),
    )
    out_specs = P(("img", "my"), "mx")
    return jax.shard_map(shards, mesh=mesh, in_specs=in_specs, out_specs=out_specs, check_vma=False)
```

```python
import jax
import jax.numpy as jnp
from jax import lax
from jax.experimental import pallas as pl
from jax.experimental.pallas import tpu as pltpu
from jax.sharding import PartitionSpec as P

D = 6144
HD = 128
BLK = 128
GRP = 8
R = 1024
SH = 256
DL = 768
CHIP = 2 * DL
HEAD = 3 * HD
IMG_ROWS = 512
ORDER = (0, 2, 1, 3)
FIRST = 160
EXTRA = 32
F32 = jnp.float32
BF16 = jnp.bfloat16

VMEM = pl.BlockSpec(memory_space=pltpu.VMEM)
SMEM = pl.BlockSpec(memory_space=pltpu.SMEM)
ANY = pl.BlockSpec(memory_space=pl.ANY)
HBM = pl.BlockSpec(memory_space=pltpu.HBM)


def call(kernel, outs, ins, scratch=(), limit=16, out_specs=None, after=(), aliases=None):
    out_shape = [jax.ShapeDtypeStruct(s, d) for s, d in outs]
    count = len(ins)

    def ordered(*refs):
        kernel(*refs[:count], *refs[count + len(after) :])

    made = pl.pallas_call(
        ordered,
        out_shape=out_shape,
        in_specs=list(ins) + [ANY] * len(after),
        out_specs=out_specs or [VMEM] * len(outs),
        scratch_shapes=list(scratch),
        input_output_aliases=aliases or {},
        compiler_params=pltpu.CompilerParams(vmem_limit_bytes=limit << 20),
        cost_estimate=pl.CostEstimate(flops=0, bytes_accessed=1024, transcendentals=0),
    )
    return lambda *args: made(*args, *after)


def gate(blocks, after):
    def kernel(*refs):
        pass

    outs = [(b.shape, b.dtype) for b in blocks]
    ins = [ANY] * len(blocks)
    same = {i: i for i in range(len(blocks))}
    return call(kernel, outs, ins, limit=4, out_specs=ins, after=after, aliases=same)(*blocks)


def swap(block, axis, bits):
    count = lax.axis_size(axis)
    return lax.ppermute(block, axis, [(i, i ^ bits) for i in range(count)])


def shift(block, axis, step):
    count = lax.axis_size(axis)
    return lax.ppermute(block, axis, [((i + step) % count, i) for i in range(count)])


def weight_heads(w3, sibling):
    def kernel(w_ref, keep_ref, send_ref, sems):
        mx = lax.axis_index("mx")
        z = mx >> 1
        lane = (mx & 1) ^ (1 if sibling else 0)
        copies = []
        for place in (2, 3, 0, 1):
            head = lane * 4 + (z ^ ORDER[place])
            dst = keep_ref if place < 2 else send_ref
            for s in range(3):
                copies.append(
                    pltpu.make_async_copy(
                        w_ref.at[s, :, pl.ds(pl.multiple_of(head * HD, HD), HD)],
                        dst.at[:, pl.ds((place % 2) * HEAD + s * HD, HD)],
                        sems.at[len(copies)],
                    )
                )
        for copy in copies:
            copy.start()
        for copy in copies:
            copy.wait()

    shape = ((DL, 2 * HEAD), BF16)
    return call(kernel, [shape, shape], [HBM], [pltpu.SemaphoreType.DMA((12,))])(w3)


def fetch(block, after):
    rows = block.shape[0] // 4

    def kernel(block_ref, out_ref, sems):
        parts = [pl.ds(i * rows, rows) for i in range(4)]
        copies = [pltpu.make_async_copy(block_ref.at[p, :], out_ref.at[p, :], sems.at[i]) for i, p in enumerate(parts)]
        for copy in copies:
            copy.start()
        for copy in copies:
            copy.wait()

    (out,) = call(kernel, [(block.shape, BF16)], [HBM], [pltpu.SemaphoreType.DMA((4,))], after=after)(block)
    return out


def table(counts, owner, target):
    def kernel(counts_ref, owner_ref, target_ref, out_ref, source):
        group = lax.axis_index("img")
        my = lax.axis_index("my")
        for t in range(GRP):
            source[t] = -1
        base = (group >> 1) * 4
        offset = jnp.int32(0)
        for i in range(4):
            image = base + i
            count = counts_ref[image]
            owned = owner_ref[image] == group
            side = jnp.where((image >> 1) == group, 0, GRP)
            for b in range(4):

                @pl.when(owned & (b < count))
                def _():
                    place = target_ref[0, jnp.minimum(offset + b, GRP - 1)]
                    source[place] = side + (i & 1) * 4 + b

            offset = offset + jnp.where(owned, count, 0)
        for n, step in enumerate((2, 1, 3, 0)):
            shard = (my + step) & 3
            out_ref[2 * n] = source[2 * shard]
            out_ref[2 * n + 1] = source[2 * shard + 1]
        out_ref[8] = counts_ref[2 * group]
        out_ref[9] = counts_ref[2 * group + 1]

    (out,) = call(
        kernel,
        [((16,), jnp.int32)],
        [SMEM] * 3,
        [pltpu.SMEM((GRP,), jnp.int32)],
        limit=4,
        out_specs=[SMEM],
    )(counts, owner, target)
    return out


def load_rows(rows, xo_ref, xs_ref):
    count = xo_ref.shape[0]
    rows[0:count, 0:DL] = xo_ref[...]
    rows[0:count, DL:CHIP] = xs_ref[...]
    rows[count : count + 16, :] = jnp.ones((16, CHIP), BF16)


def row_stats(xo_ref, xs_ref):
    fo, fs = xo_ref[...].astype(F32), xs_ref[...].astype(F32)
    s1 = jnp.sum(fo, axis=1, keepdims=True) + jnp.sum(fs, axis=1, keepdims=True)
    s2 = jnp.sum(fo * fo, axis=1, keepdims=True) + jnp.sum(fs * fs, axis=1, keepdims=True)
    lane = lax.broadcasted_iota(jnp.int32, (xo_ref.shape[0], HD), 1)
    return jnp.where(lane == 0, s1, jnp.where(lane == 1, s2, F32(0.0)))


def partial_tile(rows, wo_ref, ws_ref, columns, center):
    count = center.shape[0]
    acc = jnp.dot(rows[:, 0:DL], wo_ref[:, columns], preferred_element_type=F32)
    acc = acc + jnp.dot(rows[:, DL:CHIP], ws_ref[:, columns], preferred_element_type=F32)
    sums = acc[count : count + 8, :]
    return acc[0:count, :] - center * sums[0:1, :], sums


def rows_scratch(count):
    return pltpu.VMEM((count + 16, CHIP), BF16)


def note_terms(note):
    terms = []
    for _ in range(3):
        terms.append(note.astype(BF16).astype(F32))
        note = note - terms[-1]
    return jnp.concatenate(terms + [jnp.zeros_like(note)], axis=0).astype(BF16)


def read_note(rows):
    terms = rows.astype(F32)
    return terms[0:8, :] + terms[8:16, :] + terms[16:24, :]


def head_note(sums, columns):
    return jnp.concatenate([sums, jnp.concatenate(columns + [jnp.zeros((5, HD), F32)], axis=0)], axis=1)


def send_part(xo, xs, wo, ws, earlier=(), after=()):
    count = xo.shape[0]
    last = len(earlier) > 0

    def kernel(xo_ref, xs_ref, wo_ref, ws_ref, *refs):
        others, (out_ref, stat_ref, copy_ref, rows) = refs[: len(earlier)], refs[len(earlier) :]
        load_rows(rows, xo_ref, xs_ref)
        copy_ref[...] = xo_ref[...]
        stat = row_stats(xo_ref, xs_ref)
        center = stat[:, 0:1] / CHIP
        column_sums = []
        for n in range(3):
            columns = slice(n * 256, (n + 1) * 256)
            tile, sums = partial_tile(rows, wo_ref, ws_ref, columns, center)
            out_ref[0:count, columns] = tile.astype(BF16)
            column_sums += [sums[0:1, 0:HD], sums[0:1, HD:256]]
        if not last:
            stat_ref[...] = stat
            return
        turned = [ref[k * SH : (k + 1) * SH, :].T for ref in others for k in range(ref.shape[0] // SH)] + [stat.T]
        lines = jnp.concatenate([t[0:1, :] for t in turned] + [t[1:2, :] for t in turned], axis=0)
        stat_ref[...] = lines
        for half in range(2):
            note = head_note(lines, column_sums[3 * half : 3 * half + 3])
            out_ref[count : count + EXTRA, half * HEAD : (half + 1) * HEAD] = note_terms(note)

    outs = [((count + EXTRA if last else count, 2 * HEAD), BF16), ((8, SH) if last else (count, HD), F32), ((count, DL), BF16)]
    ins = [VMEM] * (4 + len(earlier))
    return call(kernel, outs, ins, [rows_scratch(count)], after=after)(xo, xs, wo, ws, *earlier)


def keep_part(xo, xs, wo, ws, stat, got, more=None, last=False, after=()):
    count = xo.shape[0]
    extra = list(more or ())

    def kernel(xo_ref, xs_ref, wo_ref, ws_ref, stat_ref, got_ref, *refs):
        refs, rows = refs[:-1], refs[-1]
        own_ref, send_ref = refs[len(extra)], refs[len(extra) + 1]
        load_rows(rows, xo_ref, xs_ref)
        stat = row_stats(xo_ref, xs_ref) if last else stat_ref[...]
        center = stat[:, 0:1] / CHIP
        column_sums = {}
        for n in reversed(range(6)):
            columns = slice(n * HD, (n + 1) * HD)
            if n % 2 == 1:
                pair, sums = partial_tile(rows, wo_ref, ws_ref, slice((n - 1) * HD, (n + 1) * HD), center)
            half = slice((n % 2) * HD, (n % 2 + 1) * HD)
            tile = pair[:, half] + got_ref[0:count, columns].astype(F32)
            column_sums[n] = sums[0:1, half]
            if n < 3:
                own_ref[:, columns] = tile
            else:
                send_ref[0:count, (n - 3) * HD : (n - 2) * HD] = tile.astype(BF16)
        if extra:
            refs[-1][...] = refs[0][...] + refs[1][...].astype(F32)
        if last:
            under = slice(count, count + EXTRA)
            send_ref[under, :] = note_terms(head_note(stat_ref[...], [column_sums[n] for n in (3, 4, 5)]))
            send_ref[count + EXTRA : count + 2 * EXTRA, :] = got_ref[under, HEAD : 2 * HEAD]
            refs[-2][...] = head_note(stat_ref[...], [column_sums[n] for n in (0, 1, 2)])
            refs[-1][...] = read_note(got_ref[under, 0:HEAD])

    outs = [((count, HEAD), F32), ((count + 2 * EXTRA if last else count, HEAD), BF16)]
    outs += [((SH, HEAD), F32)] if extra else []
    outs += [((8, HEAD), F32)] * 2 if last else []
    ins = [VMEM] * (6 + len(extra))
    return call(kernel, outs, ins, [rows_scratch(count)], after=after)(xo, xs, wo, ws, stat, got, *extra)


def last_sum(own, got, mine, near):
    def kernel(own_ref, got_ref, mine_ref, near_ref, out_ref, coef_ref, cs_ref):
        out_ref[...] = own_ref[...] + got_ref[0:SH, :].astype(F32)
        notes = [mine_ref[...], near_ref[...]]
        for at in (SH, SH + EXTRA):
            notes.append(read_note(got_ref[at : at + EXTRA, :]))
        for k in range(4):
            sums = [n[k : k + 1, 0:SH] for n in notes]
            squares = [n[4 + k : 5 + k, 0:SH] for n in notes]
            mean = (sums[0] + sums[1] + sums[2] + sums[3]) / D
            var = (squares[0] + squares[1] + squares[2] + squares[3]) / D - mean * mean
            lines = [lax.rsqrt(var + 1e-06)] + [s / CHIP - mean for s in sums] + [jnp.zeros((HD - 5, SH), F32)]
            coef_ref[k * SH : (k + 1) * SH, :] = jnp.concatenate(lines, axis=0).T
        for c, n in enumerate(notes):
            for place in range(3):
                cs_ref[c : c + 1, place * HD : (place + 1) * HD] = n[place : place + 1, SH:HEAD]
        cs_ref[4:8, :] = jnp.zeros((4, HEAD), F32)

    outs = [((SH, HEAD), F32), ((R, HD), F32), ((8, HEAD), F32)]
    return call(kernel, outs, [VMEM] * 4)(own, got, mine, near)


def join(blocks, axis, after=()):
    size = blocks[0].shape[axis]

    def kernel(*refs):
        for i, ref in enumerate(refs[:-1]):
            at = slice(i * size, (i + 1) * size)
            if axis == 0:
                refs[-1][at, :] = ref[...]
            else:
                refs[-1][:, at] = ref[...]

    shape = list(blocks[0].shape)
    shape[axis] *= len(blocks)
    (out,) = call(kernel, [(tuple(shape), BF16)], [VMEM] * len(blocks), after=after)(*blocks)
    return out


def attention(places, coef, cs, tot0, own12, end12, tot3):
    def kernel(places_ref, coef_ref, cs_ref, tot0_ref, own12_ref, end12_ref, tot3_ref, out_ref, qkv):
        my = lax.axis_index("my")
        for k, offset in enumerate((0, 1, 3, 2)):
            if k in (1, 2):
                at = slice((k - 1) * SH, k * SH)
                total = own12_ref[at, :] + end12_ref[at, :].astype(F32)
            else:
                total = (tot3_ref if k else tot0_ref)[...]
            coef = coef_ref[k * SH : (k + 1) * SH, :]
            for c in range(4):
                total = total + coef[:, c + 1 : c + 2] * cs_ref[c : c + 1, :]
            total = total * coef[:, 0:1]
            shard = (my + offset) & 3
            qkv[pl.ds(pl.multiple_of(shard * SH, SH), SH), :] = total.astype(BF16)
        first, second = places_ref[8], places_ref[9]
        for image in range(2):
            start = pl.multiple_of(first * BLK, BLK) if image else 0
            live = (second if image else first) * BLK
            q = qkv[pl.ds(start, IMG_ROWS), 0:HD]
            key = qkv[pl.ds(start, IMG_ROWS), HD : 2 * HD]
            value = qkv[pl.ds(start, IMG_ROWS), 2 * HD : 3 * HD]
            rows = lax.broadcasted_iota(jnp.int32, (IMG_ROWS, HD), 0)
            value = jnp.where(rows < live, value, jnp.zeros_like(value))
            scores = lax.dot_general(q, key, (((1,), (1,)), ((), ())), preferred_element_type=F32)
            columns = lax.broadcasted_iota(jnp.int32, (IMG_ROWS, IMG_ROWS), 1)
            scores = jnp.where(columns < live, scores * HD ** (-0.5), F32(-1e30))
            top = jnp.max(scores, axis=1, keepdims=True)
            powers = jnp.exp(scores - top)
            weights = (powers / jnp.sum(powers, axis=1, keepdims=True)).astype(BF16)
            mixture = jnp.dot(weights, value, preferred_element_type=F32)
            out_ref[image * IMG_ROWS : (image + 1) * IMG_ROWS, :] = mixture.astype(BF16)

    (out,) = call(
        kernel, [((R, HD), BF16)], [SMEM] + [VMEM] * 6, [pltpu.VMEM((R, HEAD), BF16)], limit=24
    )(places, coef, cs, tot0, own12, end12, tot3)
    return out


def route(places, mine, other):
    def kernel(places_ref, mine_ref, other_ref, *outs):
        for n in range(GRP):
            out_ref = outs[n // 2]
            place = slice((n % 2) * BLK, (n % 2 + 1) * BLK)
            src = places_ref[n]
            row = pl.multiple_of((src & 7) * BLK, BLK)

            @pl.when(src < 0)
            def _():
                out_ref[place, :] = jnp.zeros((BLK, HD), BF16)

            @pl.when((src >= 0) & (src < GRP))
            def _():
                out_ref[place, :] = mine_ref[pl.ds(row, BLK), :]

            @pl.when(src >= GRP)
            def _():
                out_ref[place, :] = other_ref[pl.ds(row, BLK), :]

    return call(kernel, [((SH, HD), BF16)] * 4, [SMEM, VMEM, VMEM])(places, mine, other)


def lane_rows(blocks):
    def kernel(*refs):
        z = lax.axis_index("mx") >> 1
        for j, ref in enumerate(refs[:4]):
            for d in range(4):
                at = pl.multiple_of((d * 4 + (z ^ j)) * HD, HD)
                refs[4][:, pl.ds(at, HD)] = ref[0:FIRST, d * HD : (d + 1) * HD]
                refs[5][:, pl.ds(at, HD)] = ref[FIRST:SH, d * HD : (d + 1) * HD]

    return call(kernel, [((FIRST, 16 * HD), BF16), ((SH - FIRST, 16 * HD), BF16)], [VMEM] * 4)(*blocks)


def project(lanes, sibs, weights):
    def kernel(lane0_ref, lane1_ref, sib0_ref, sib1_ref, w0_ref, w1_ref, w2_ref, top_ref, bottom_ref, out_ref, low, high):
        side = lax.axis_index("mx") & 1
        for at, lane_ref, sib_ref in ((slice(0, FIRST), lane0_ref, sib0_ref), (slice(FIRST, SH), lane1_ref, sib1_ref)):
            one, two = lane_ref[...], sib_ref[...]
            low[at, :] = jnp.where(side == 0, one, two)
            high[at, :] = jnp.where(side == 0, two, one)
        for n in range(3):
            columns = slice(n * 256, (n + 1) * 256)
            total = jnp.zeros((SH, 256), F32)
            for d, ref in enumerate((w0_ref, w1_ref, w2_ref, None)):
                heads = slice(d * 4 * HD, (d + 1) * 4 * HD)
                upper = top_ref[:, columns] if ref is None else ref[0 : 4 * HD, columns]
                lower = bottom_ref[:, columns] if ref is None else ref[4 * HD : R, columns]
                total = total + jnp.dot(low[:, heads], upper, preferred_element_type=F32)
                total = total + jnp.dot(high[:, heads], lower, preferred_element_type=F32)
            out_ref[:, columns] = total.astype(BF16)

    scratch = [pltpu.VMEM((SH, 16 * HD), BF16)] * 2
    (out,) = call(kernel, [((SH, DL), BF16)], [VMEM] * 9, scratch, limit=24)(*lanes, *sibs, *weights)
    return out


def shards(patches, tile_counts, image_owner, block_target, qkv_weight, out_weight):
    scope = jax.named_scope
    with scope("rows_near"):
        next_rows, last_rows = shift(patches, "my", 1), shift(patches, "my", -1)
    w3 = jnp.transpose(qkv_weight, (1, 0, 2))
    with scope("weights"):
        theirs_keep, theirs_send = weight_heads(w3, True)
        sib_send = swap(theirs_send, "mx", 1)
        sib_keep = swap(theirs_keep, "mx", 1)
        own_keep, own_send = weight_heads(w3, False)
        places = table(tile_counts, image_owner, block_target)
    weights = (own_keep, sib_keep, own_send, sib_send)

    with scope("chunk0"):
        s0 = swap(patches, "mx", 1)
        part0, stat0, again = send_part(patches, s0, own_send, sib_send)
        got0 = swap(part0, "mx", 2)
    with scope("rows_far"):
        x3 = shift(again, "my", 2)
    with scope("chunk12"):
        x12 = join([next_rows, last_rows], 0, (got0,))
        s12 = swap(x12, "mx", 1)
    with scope("sum0"):
        own0, next0 = keep_part(patches, s0, own_keep, sib_keep, stat0, got0)
        end0 = swap(next0, "mx", 4)
    with scope("chunk12"):
        part12, stat12, _ = send_part(x12, s12, own_send, sib_send, after=(next0,))
        got12 = swap(part12, "mx", 2)
    with scope("chunk3"):
        (x3,) = gate([x3], (part12, end0))
        s3 = swap(x3, "mx", 1)
        part3, stat3, _ = send_part(x3, s3, own_send, sib_send, (stat0, stat12), (part12, places))
        got3 = swap(part3, "mx", 2)
    with scope("sum12"):
        own12, next12, tot0 = keep_part(x12, s12, own_keep, sib_keep, stat12, got12, (own0, end0), after=(part3,))
        end12 = swap(next12, "mx", 4)
    with scope("sum3"):
        own3, next3, mine, near = keep_part(x3, s3, own_keep, sib_keep, stat3, got3, last=True, after=(next12,))
        tot3, coef, cs = last_sum(own3, swap(next3, "mx", 4), mine, near)
    with scope("out_weight"):
        held = fetch(out_weight, (x3,))
        w_next, w_last = shift(held, "my", 1), shift(held, "my", -1)
        w_far = [shift(w_next[: 4 * HD], "my", 1), shift(w_last[4 * HD :], "my", -1)]

    with scope("attention"):
        attended = attention(places, coef, cs, tot0, own12, end12, tot3)
        other = swap(attended, "img", 1)
        far, up, down, own = route(places, attended, other)
        near = [own, shift(down, "my", 1), shift(up, "my", -1), shift(far, "my", 2)]

    with scope("out"):
        block = join(near, 1)
        lanes = lane_rows([block] + [swap(block, "mx", 2 * j) for j in (1, 2, 3)])
        return project(lanes, [swap(lane, "mx", 1) for lane in lanes], [held, w_next, w_last] + w_far)


def solution(mesh):
    in_specs = (
        P(("img", "my"), "mx"),
        P(),
        P(),
        P("img", None),
        P("mx", None, "my"),
        P("my", "mx"),
    )
    out_specs = P(("img", "my"), "mx")
    return jax.shard_map(shards, mesh=mesh, in_specs=in_specs, out_specs=out_specs, check_vma=False)
```

```python
import jax
import jax.numpy as jnp
from jax import lax
from jax.experimental import pallas as pl
from jax.experimental.pallas import tpu as pltpu
from jax.sharding import PartitionSpec as P

D = 6144
HD = 128
BLK = 128
GRP = 8
R = 1024
SH = 256
DL = 768
CHIP = 2 * DL
HEAD = 3 * HD
IMG_ROWS = 512
ORDER = (0, 2, 1, 3)
FIRST = 160
EXTRA = 32
F32 = jnp.float32
BF16 = jnp.bfloat16

VMEM = pl.BlockSpec(memory_space=pltpu.VMEM)
SMEM = pl.BlockSpec(memory_space=pltpu.SMEM)
ANY = pl.BlockSpec(memory_space=pl.ANY)
HBM = pl.BlockSpec(memory_space=pltpu.HBM)


def call(kernel, outs, ins, scratch=(), limit=16, out_specs=None, after=(), aliases=None):
    out_shape = [jax.ShapeDtypeStruct(s, d) for s, d in outs]
    count = len(ins)

    def ordered(*refs):
        kernel(*refs[:count], *refs[count + len(after) :])

    made = pl.pallas_call(
        ordered,
        out_shape=out_shape,
        in_specs=list(ins) + [ANY] * len(after),
        out_specs=out_specs or [VMEM] * len(outs),
        scratch_shapes=list(scratch),
        input_output_aliases=aliases or {},
        compiler_params=pltpu.CompilerParams(vmem_limit_bytes=limit << 20),
        cost_estimate=pl.CostEstimate(flops=0, bytes_accessed=1024, transcendentals=0),
    )
    return lambda *args: made(*args, *after)


def gate(blocks, after):
    def kernel(*refs):
        pass

    outs = [(b.shape, b.dtype) for b in blocks]
    ins = [ANY] * len(blocks)
    same = {i: i for i in range(len(blocks))}
    return call(kernel, outs, ins, limit=4, out_specs=ins, after=after, aliases=same)(*blocks)


def swap(block, axis, bits):
    count = lax.axis_size(axis)
    return lax.ppermute(block, axis, [(i, i ^ bits) for i in range(count)])


def shift(block, axis, step):
    count = lax.axis_size(axis)
    return lax.ppermute(block, axis, [((i + step) % count, i) for i in range(count)])


def weight_heads(w3, sibling):
    def kernel(w_ref, keep_ref, send_ref, sems):
        mx = lax.axis_index("mx")
        z = mx >> 1
        lane = (mx & 1) ^ (1 if sibling else 0)
        copies = []
        for place in (2, 3, 0, 1):
            head = lane * 4 + (z ^ ORDER[place])
            dst = keep_ref if place < 2 else send_ref
            for s in range(3):
                copies.append(
                    pltpu.make_async_copy(
                        w_ref.at[s, :, pl.ds(pl.multiple_of(head * HD, HD), HD)],
                        dst.at[:, pl.ds((place % 2) * HEAD + s * HD, HD)],
                        sems.at[len(copies)],
                    )
                )
        for copy in copies:
            copy.start()
        for copy in copies:
            copy.wait()

    shape = ((DL, 2 * HEAD), BF16)
    return call(kernel, [shape, shape], [HBM], [pltpu.SemaphoreType.DMA((12,))])(w3)


def table(counts, owner, target):
    def kernel(counts_ref, owner_ref, target_ref, out_ref, source):
        group = lax.axis_index("img")
        my = lax.axis_index("my")
        for t in range(GRP):
            source[t] = -1
        base = (group >> 1) * 4
        offset = jnp.int32(0)
        for i in range(4):
            image = base + i
            count = counts_ref[image]
            owned = owner_ref[image] == group
            side = jnp.where((image >> 1) == group, 0, GRP)
            for b in range(4):

                @pl.when(owned & (b < count))
                def _():
                    place = target_ref[0, jnp.minimum(offset + b, GRP - 1)]
                    source[place] = side + (i & 1) * 4 + b

            offset = offset + jnp.where(owned, count, 0)
        for n, step in enumerate((2, 1, 3, 0)):
            shard = (my + step) & 3
            out_ref[2 * n] = source[2 * shard]
            out_ref[2 * n + 1] = source[2 * shard + 1]
        out_ref[8] = counts_ref[2 * group]
        out_ref[9] = counts_ref[2 * group + 1]

    (out,) = call(
        kernel,
        [((16,), jnp.int32)],
        [SMEM] * 3,
        [pltpu.SMEM((GRP,), jnp.int32)],
        limit=4,
        out_specs=[SMEM],
    )(counts, owner, target)
    return out


def load_rows(rows, xo_refs, xs_refs):
    at = 0
    for xo_ref, xs_ref in zip(xo_refs, xs_refs):
        size = xo_ref.shape[0]
        rows[at : at + size, 0:DL] = xo_ref[...]
        rows[at : at + size, DL:CHIP] = xs_ref[...]
        at += size
    rows[at : at + 16, :] = jnp.ones((16, CHIP), BF16)


def row_stats(xo_refs, xs_refs):
    stats = []
    for xo_ref, xs_ref in zip(xo_refs, xs_refs):
        fo, fs = xo_ref[...].astype(F32), xs_ref[...].astype(F32)
        s1 = jnp.sum(fo, axis=1, keepdims=True) + jnp.sum(fs, axis=1, keepdims=True)
        s2 = jnp.sum(fo * fo, axis=1, keepdims=True) + jnp.sum(fs * fs, axis=1, keepdims=True)
        lane = lax.broadcasted_iota(jnp.int32, (xo_ref.shape[0], HD), 1)
        stats.append(jnp.where(lane == 0, s1, jnp.where(lane == 1, s2, F32(0.0))))
    return stats[0] if len(stats) == 1 else jnp.concatenate(stats, axis=0)


def partial_tile(rows, wo_ref, ws_ref, columns, center):
    count = center.shape[0]
    acc = jnp.dot(rows[:, 0:DL], wo_ref[:, columns], preferred_element_type=F32)
    acc = acc + jnp.dot(rows[:, DL:CHIP], ws_ref[:, columns], preferred_element_type=F32)
    sums = acc[count : count + 8, :]
    return acc[0:count, :] - center * sums[0:1, :], sums


def rows_scratch(count):
    return pltpu.VMEM((count + 16, CHIP), BF16)


def note_terms(note):
    terms = []
    for _ in range(3):
        terms.append(note.astype(BF16).astype(F32))
        note = note - terms[-1]
    return jnp.concatenate(terms + [jnp.zeros_like(note)], axis=0).astype(BF16)


def read_note(rows):
    terms = rows.astype(F32)
    return terms[0:8, :] + terms[8:16, :] + terms[16:24, :]


def head_note(sums, columns):
    return jnp.concatenate([sums, jnp.concatenate(columns + [jnp.zeros((5, HD), F32)], axis=0)], axis=1)


def send_part(xo, xs, wo, ws, earlier=(), after=()):
    count = xo.shape[0]
    last = len(earlier) > 0

    def kernel(xo_ref, xs_ref, wo_ref, ws_ref, *refs):
        others, (out_ref, stat_ref, copy_ref, rows) = refs[: len(earlier)], refs[len(earlier) :]
        load_rows(rows, [xo_ref], [xs_ref])
        copy_ref[...] = xo_ref[...]
        stat = row_stats([xo_ref], [xs_ref])
        center = stat[:, 0:1] / CHIP
        column_sums = []
        for n in range(3):
            columns = slice(n * 256, (n + 1) * 256)
            tile, sums = partial_tile(rows, wo_ref, ws_ref, columns, center)
            out_ref[0:count, columns] = tile.astype(BF16)
            column_sums += [sums[0:1, 0:HD], sums[0:1, HD:256]]
        if not last:
            stat_ref[...] = stat
            return
        turned = [ref[k * SH : (k + 1) * SH, :].T for ref in others for k in range(ref.shape[0] // SH)] + [stat.T]
        lines = jnp.concatenate([t[0:1, :] for t in turned] + [t[1:2, :] for t in turned], axis=0)
        stat_ref[...] = lines
        for half in range(2):
            note = head_note(lines, column_sums[3 * half : 3 * half + 3])
            out_ref[count : count + EXTRA, half * HEAD : (half + 1) * HEAD] = note_terms(note)

    outs = [((count + EXTRA if last else count, 2 * HEAD), BF16), ((8, SH) if last else (count, HD), F32), ((count, DL), BF16)]
    ins = [VMEM] * (4 + len(earlier))
    return call(kernel, outs, ins, [rows_scratch(count)], after=after)(xo, xs, wo, ws, *earlier)


def own_product(blocks, weight, after):
    size = blocks[0].shape[0]
    count = len(blocks) * size

    def kernel(*refs):
        w_ref, out_ref, rows = refs[len(blocks) :]
        for i in range(len(blocks)):
            rows[i * size : (i + 1) * size, :] = refs[i][...]
        rows[count : count + 16, :] = jnp.ones((16, DL), BF16)
        for n in range(3):
            columns = slice(n * 256, (n + 1) * 256)
            out_ref[:, columns] = jnp.dot(rows[...], w_ref[:, columns], preferred_element_type=F32)

    outs = [((count + 16, 2 * HEAD), F32)]
    scratch = [pltpu.VMEM((count + 16, DL), BF16)]
    (out,) = call(kernel, outs, [VMEM] * (1 + len(blocks)), scratch, after=after)(*blocks, weight)
    return out


def rest_part(xo, xs, weight, product, after):
    size, blocks = xo[0].shape[0], len(xo)
    count = blocks * size

    def kernel(*refs):
        xo_refs, xs_refs = refs[:blocks], refs[blocks : 2 * blocks]
        w_ref, product_ref, out_ref, stat_ref, rows = refs[2 * blocks :]
        for i, ref in enumerate(xs_refs):
            rows[i * size : (i + 1) * size, :] = ref[...]
        rows[count : count + 16, :] = jnp.ones((16, DL), BF16)
        stat = row_stats(xo_refs, xs_refs)
        stat_ref[...] = stat
        center = stat[:, 0:1] / CHIP
        for n in range(3):
            columns = slice(n * 256, (n + 1) * 256)
            acc = product_ref[:, columns] + jnp.dot(rows[...], w_ref[:, columns], preferred_element_type=F32)
            out_ref[:, columns] = (acc[0:count, :] - center * acc[count : count + 1, :]).astype(BF16)

    outs = [((count, 2 * HEAD), BF16), ((count, HD), F32)]
    scratch = [pltpu.VMEM((count + 16, DL), BF16)]
    return call(kernel, outs, [VMEM] * (2 * blocks + 2), scratch, after=after)(*xo, *xs, weight, product)


def kept_part(xo, xs, wo, ws, stat, last=False, after=()):
    blocks = len(xo)
    count = sum(block.shape[0] for block in xo)

    def kernel(*refs):
        xo_refs, xs_refs = refs[:blocks], refs[blocks : 2 * blocks]
        wo_ref, ws_ref, stat_ref, kept_ref = refs[2 * blocks : 2 * blocks + 4]
        refs, rows = refs[2 * blocks + 4 : -1], refs[-1]
        load_rows(rows, xo_refs, xs_refs)
        stat = row_stats(xo_refs, xs_refs) if last else stat_ref[...]
        center = stat[:, 0:1] / CHIP
        column_sums = []
        for n in range(3):
            columns = slice(n * 256, (n + 1) * 256)
            tile, sums = partial_tile(rows, wo_ref, ws_ref, columns, center)
            kept_ref[:, columns] = tile
            column_sums += [sums[0:1, 0:HD], sums[0:1, HD:256]]
        if last:
            refs[0][...] = head_note(stat_ref[...], column_sums[0:3])
            refs[1][...] = note_terms(head_note(stat_ref[...], column_sums[3:6]))

    outs = [((count, 2 * HEAD), F32)] + ([((8, HEAD), F32), ((EXTRA, HEAD), BF16)] if last else [])
    return call(kernel, outs, [VMEM] * (2 * blocks + 3), [rows_scratch(count)], after=after)(*xo, *xs, wo, ws, stat)


def add_part(kept, got, more=None, note=None, after=()):
    count = kept.shape[0]
    extra = list(more or ())
    last = note is not None
    ins = [kept, got] + extra + ([note] if last else [])

    def kernel(kept_ref, got_ref, *refs):
        own_ref, send_ref = refs[len(ins) - 2], refs[len(ins) - 1]
        own_ref[...] = kept_ref[:, 0:HEAD] + got_ref[0:count, 0:HEAD].astype(F32)
        send_ref[0:count, :] = (kept_ref[:, HEAD:] + got_ref[0:count, HEAD:].astype(F32)).astype(BF16)
        if extra:
            refs[len(ins)][...] = refs[0][...] + refs[1][...].astype(F32)
        if last:
            under = slice(count, count + EXTRA)
            send_ref[under, :] = refs[len(ins) - 3][...]
            send_ref[count + EXTRA : count + 2 * EXTRA, :] = got_ref[under, HEAD:]
            refs[-1][...] = read_note(got_ref[under, 0:HEAD])

    outs = [((count, HEAD), F32), ((count + 2 * EXTRA if last else count, HEAD), BF16)]
    outs += [((SH, HEAD), F32)] if extra else []
    outs += [((8, HEAD), F32)] if last else []
    return call(kernel, outs, [VMEM] * len(ins), after=after)(*ins)


def last_sum(own, got, mine, near):
    def kernel(own_ref, got_ref, mine_ref, near_ref, out_ref, coef_ref, cs_ref):
        out_ref[...] = own_ref[...] + got_ref[0:SH, :].astype(F32)
        notes = [mine_ref[...], near_ref[...]]
        for at in (SH, SH + EXTRA):
            notes.append(read_note(got_ref[at : at + EXTRA, :]))
        for k in range(4):
            sums = [n[k : k + 1, 0:SH] for n in notes]
            squares = [n[4 + k : 5 + k, 0:SH] for n in notes]
            mean = (sums[0] + sums[1] + sums[2] + sums[3]) / D
            var = (squares[0] + squares[1] + squares[2] + squares[3]) / D - mean * mean
            lines = [lax.rsqrt(var + 1e-06)] + [s / CHIP - mean for s in sums] + [jnp.zeros((HD - 5, SH), F32)]
            coef_ref[k * SH : (k + 1) * SH, :] = jnp.concatenate(lines, axis=0).T
        for c, n in enumerate(notes):
            for place in range(3):
                cs_ref[c : c + 1, place * HD : (place + 1) * HD] = n[place : place + 1, SH:HEAD]
        cs_ref[4:8, :] = jnp.zeros((4, HEAD), F32)

    outs = [((SH, HEAD), F32), ((R, HD), F32), ((8, HEAD), F32)]
    return call(kernel, outs, [VMEM] * 4)(own, got, mine, near)


def join(blocks, axis, after=()):
    size = blocks[0].shape[axis]

    def kernel(*refs):
        for i, ref in enumerate(refs[:-1]):
            at = slice(i * size, (i + 1) * size)
            if axis == 0:
                refs[-1][at, :] = ref[...]
            else:
                refs[-1][:, at] = ref[...]

    shape = list(blocks[0].shape)
    shape[axis] *= len(blocks)
    (out,) = call(kernel, [(tuple(shape), BF16)], [VMEM] * len(blocks), after=after)(*blocks)
    return out


def attention(places, coef, cs, tot0, own12, end12, tot3):
    def kernel(places_ref, coef_ref, cs_ref, tot0_ref, own12_ref, end12_ref, tot3_ref, out_ref, qkv):
        my = lax.axis_index("my")
        for k, offset in enumerate((0, 1, 3, 2)):
            if k in (1, 2):
                at = slice((k - 1) * SH, k * SH)
                total = own12_ref[at, :] + end12_ref[at, :].astype(F32)
            else:
                total = (tot3_ref if k else tot0_ref)[...]
            coef = coef_ref[k * SH : (k + 1) * SH, :]
            for c in range(4):
                total = total + coef[:, c + 1 : c + 2] * cs_ref[c : c + 1, :]
            total = total * coef[:, 0:1]
            shard = (my + offset) & 3
            qkv[pl.ds(pl.multiple_of(shard * SH, SH), SH), :] = total.astype(BF16)
        first, second = places_ref[8], places_ref[9]
        for image in range(2):
            start = pl.multiple_of(first * BLK, BLK) if image else 0
            live = (second if image else first) * BLK
            q = qkv[pl.ds(start, IMG_ROWS), 0:HD]
            key = qkv[pl.ds(start, IMG_ROWS), HD : 2 * HD]
            value = qkv[pl.ds(start, IMG_ROWS), 2 * HD : 3 * HD]
            rows = lax.broadcasted_iota(jnp.int32, (IMG_ROWS, HD), 0)
            value = jnp.where(rows < live, value, jnp.zeros_like(value))
            scores = lax.dot_general(q, key, (((1,), (1,)), ((), ())), preferred_element_type=F32)
            columns = lax.broadcasted_iota(jnp.int32, (IMG_ROWS, IMG_ROWS), 1)
            scores = jnp.where(columns < live, scores, F32(-1e30))
            top = jnp.max(scores, axis=1, keepdims=True)
            powers = jnp.exp((scores - top) * HD ** (-0.5))
            mixture = jnp.dot(powers.astype(BF16), value, preferred_element_type=F32)
            mixture = mixture / jnp.sum(powers, axis=1, keepdims=True)
            out_ref[image * IMG_ROWS : (image + 1) * IMG_ROWS, :] = mixture.astype(BF16)

    (out,) = call(
        kernel, [((R, HD), BF16)], [SMEM] + [VMEM] * 6, [pltpu.VMEM((R, HEAD), BF16)], limit=24
    )(places, coef, cs, tot0, own12, end12, tot3)
    return out


def route(places, mine, other):
    def kernel(places_ref, mine_ref, other_ref, *outs):
        for n in range(GRP):
            out_ref = outs[n // 2]
            place = slice((n % 2) * BLK, (n % 2 + 1) * BLK)
            src = places_ref[n]
            row = pl.multiple_of((src & 7) * BLK, BLK)

            @pl.when(src < 0)
            def _():
                out_ref[place, :] = jnp.zeros((BLK, HD), BF16)

            @pl.when((src >= 0) & (src < GRP))
            def _():
                out_ref[place, :] = mine_ref[pl.ds(row, BLK), :]

            @pl.when(src >= GRP)
            def _():
                out_ref[place, :] = other_ref[pl.ds(row, BLK), :]

    return call(kernel, [((SH, HD), BF16)] * 4, [SMEM, VMEM, VMEM])(places, mine, other)


def lane_rows(blocks):
    def kernel(*refs):
        z = lax.axis_index("mx") >> 1
        for j, ref in enumerate(refs[:4]):
            for d in range(4):
                at = pl.multiple_of((d * 4 + (z ^ j)) * HD, HD)
                refs[4][:, pl.ds(at, HD)] = ref[0:FIRST, d * HD : (d + 1) * HD]
                refs[5][:, pl.ds(at, HD)] = ref[FIRST:SH, d * HD : (d + 1) * HD]

    return call(kernel, [((FIRST, 16 * HD), BF16), ((SH - FIRST, 16 * HD), BF16)], [VMEM] * 4)(*blocks)


def project_lane(lanes, weights):
    def kernel(lane0_ref, lane1_ref, w0_ref, w1_ref, w2_ref, out_ref, rows):
        side = lax.axis_index("mx") & 1
        rows[0:FIRST, :] = lane0_ref[:, 0 : 12 * HD]
        rows[FIRST:SH, :] = lane1_ref[:, 0 : 12 * HD]
        at = pl.ds(pl.multiple_of(side * 4 * HD, 4 * HD), 4 * HD)
        for n in range(3):
            columns = slice(n * 256, (n + 1) * 256)
            total = jnp.zeros((SH, 256), F32)
            for d, ref in enumerate((w0_ref, w1_ref, w2_ref)):
                heads = slice(d * 4 * HD, (d + 1) * 4 * HD)
                total = total + jnp.dot(rows[:, heads], ref[at, columns], preferred_element_type=F32)
            out_ref[:, columns] = total

    scratch = [pltpu.VMEM((SH, 12 * HD), BF16)]
    (out,) = call(kernel, [((SH, DL), F32)], [VMEM] * 5, scratch, limit=24)(*lanes, *weights)
    return out


def project(so_far, lanes, sibs, weights):
    def kernel(far_ref, lane0_ref, lane1_ref, sib0_ref, sib1_ref, w0_ref, w1_ref, w2_ref, top_ref, bottom_ref, out_ref, rows, low, high):
        side = lax.axis_index("mx") & 1
        last = slice(12 * HD, 16 * HD)
        for at, lane_ref, sib_ref in ((slice(0, FIRST), lane0_ref, sib0_ref), (slice(FIRST, SH), lane1_ref, sib1_ref)):
            rows[at, :] = sib_ref[:, 0 : 12 * HD]
            one, two = lane_ref[:, last], sib_ref[:, last]
            low[at, :] = jnp.where(side == 0, one, two)
            high[at, :] = jnp.where(side == 0, two, one)
        place = pl.ds(pl.multiple_of((1 - side) * 4 * HD, 4 * HD), 4 * HD)
        for n in range(3):
            columns = slice(n * 256, (n + 1) * 256)
            total = far_ref[:, columns]
            for d, ref in enumerate((w0_ref, w1_ref, w2_ref)):
                heads = slice(d * 4 * HD, (d + 1) * 4 * HD)
                total = total + jnp.dot(rows[:, heads], ref[place, columns], preferred_element_type=F32)
            total = total + jnp.dot(low[...], top_ref[:, columns], preferred_element_type=F32)
            total = total + jnp.dot(high[...], bottom_ref[:, columns], preferred_element_type=F32)
            out_ref[:, columns] = total.astype(BF16)

    scratch = [pltpu.VMEM((SH, 12 * HD), BF16)] + [pltpu.VMEM((SH, 4 * HD), BF16)] * 2
    (out,) = call(kernel, [((SH, DL), BF16)], [VMEM] * 10, scratch, limit=24)(so_far, *lanes, *sibs, *weights)
    return out


def shards(patches, tile_counts, image_owner, block_target, qkv_weight, out_weight):
    scope = jax.named_scope
    with scope("rows_near"):
        next_rows, last_rows = shift(patches, "my", 1), shift(patches, "my", -1)
    w3 = jnp.transpose(qkv_weight, (1, 0, 2))
    with scope("weights"):
        theirs_keep, theirs_send = weight_heads(w3, True)
        sib_send = swap(theirs_send, "mx", 1)
        sib_keep = swap(theirs_keep, "mx", 1)
        own_keep, own_send = weight_heads(w3, False)
        places = table(tile_counts, image_owner, block_target)
    weights = (own_keep, sib_keep, own_send, sib_send)

    with scope("chunk0"):
        s0 = swap(patches, "mx", 1)
        part0, stat0, again = send_part(patches, s0, own_send, sib_send)
        got0 = swap(part0, "mx", 2)
    with scope("rows_far"):
        x3 = shift(again, "my", 2)
    with scope("sum0"):
        (kept0,) = kept_part([patches], [s0], own_keep, sib_keep, stat0)
    with scope("chunk12"):
        x12 = [next_rows, last_rows]
        s12 = [swap(x, "mx", 1) for x in x12]
        product = own_product(x12, own_send, (kept0,))
        own0, next0 = add_part(kept0, got0, after=(product,))
        end0 = swap(next0, "mx", 4)
        part12, stat12 = rest_part(x12, s12, sib_send, product, (next0,))
        got12 = swap(part12, "mx", 2)
    with scope("chunk3"):
        (x3,) = gate([x3], (part12, end0))
        s3 = swap(x3, "mx", 1)
        part3, stat3, _ = send_part(x3, s3, own_send, sib_send, (stat0, stat12), (part12, places))
        got3 = swap(part3, "mx", 2)
    with scope("sum12"):
        (kept12,) = kept_part(x12, s12, own_keep, sib_keep, stat12, after=(part3,))
        own12, next12, tot0 = add_part(kept12, got12, (own0, end0))
        end12 = swap(next12, "mx", 4)
    with scope("sum3"):
        kept3, mine, note = kept_part([x3], [s3], own_keep, sib_keep, stat3, True, (part3,))
        own3, next3, near = add_part(kept3, got3, note=note, after=(next12,))
        tot3, coef, cs = last_sum(own3, swap(next3, "mx", 4), mine, near)
    with scope("out_weight"):
        w_next, w_last = shift(out_weight, "my", 1), shift(out_weight, "my", -1)
        w_far = [shift(w_next[: 4 * HD], "my", 1), shift(w_last[4 * HD :], "my", -1)]

    with scope("attention"):
        attended = attention(places, coef, cs, tot0, own12, end12, tot3)
        other = swap(attended, "img", 1)
        far, up, down, own = route(places, attended, other)
        near = [own, shift(down, "my", 1), shift(up, "my", -1), shift(far, "my", 2)]

    with scope("out"):
        block = join(near, 1)
        lanes = lane_rows([block] + [swap(block, "mx", 2 * j) for j in (1, 2, 3)])
        sibs = [swap(lane, "mx", 1) for lane in lanes]
        so_far = project_lane(lanes, [out_weight, w_next, w_last])
        return project(so_far, lanes, sibs, [out_weight, w_next, w_last] + w_far)


def solution(mesh):
    in_specs = (
        P(("img", "my"), "mx"),
        P(),
        P(),
        P("img", None),
        P("mx", None, "my"),
        P("my", "mx"),
    )
    out_specs = P(("img", "my"), "mx")
    return jax.shard_map(shards, mesh=mesh, in_specs=in_specs, out_specs=out_specs, check_vma=False)
```

```python
import jax
import jax.numpy as jnp
from jax import lax
from jax.experimental import pallas as pl
from jax.experimental.pallas import tpu as pltpu
from jax.sharding import PartitionSpec as P

D = 6144
HD = 128
BLK = 128
GRP = 8
R = 1024
SH = 256
DL = 768
CHIP = 2 * DL
HEAD = 3 * HD
IMG_ROWS = 512
ORDER = (0, 2, 1, 3)
FIRST = 160
EXTRA = 32
TERMS = 24
SENT = (2, 1, 3)
F32 = jnp.float32
BF16 = jnp.bfloat16

VMEM = pl.BlockSpec(memory_space=pltpu.VMEM)
SMEM = pl.BlockSpec(memory_space=pltpu.SMEM)
ANY = pl.BlockSpec(memory_space=pl.ANY)
HBM = pl.BlockSpec(memory_space=pltpu.HBM)


def call(kernel, outs, ins, scratch=(), limit=16, out_specs=None, after=(), aliases=None):
    out_shape = [jax.ShapeDtypeStruct(s, d) for s, d in outs]
    count = len(ins)

    def ordered(*refs):
        kernel(*refs[:count], *refs[count + len(after) :])

    made = pl.pallas_call(
        ordered,
        out_shape=out_shape,
        in_specs=list(ins) + [ANY] * len(after),
        out_specs=out_specs or [VMEM] * len(outs),
        scratch_shapes=list(scratch),
        input_output_aliases=aliases or {},
        compiler_params=pltpu.CompilerParams(vmem_limit_bytes=limit << 20),
        cost_estimate=pl.CostEstimate(flops=0, bytes_accessed=1024, transcendentals=0),
    )
    return lambda *args: made(*args, *after)


def gate(blocks, after):
    def kernel(*refs):
        pass

    outs = [(b.shape, b.dtype) for b in blocks]
    ins = [ANY] * len(blocks)
    same = {i: i for i in range(len(blocks))}
    return call(kernel, outs, ins, limit=4, out_specs=ins, after=after, aliases=same)(*blocks)


def swap(block, axis, bits):
    count = lax.axis_size(axis)
    return lax.ppermute(block, axis, [(i, i ^ bits) for i in range(count)])


def shift(block, axis, step):
    count = lax.axis_size(axis)
    return lax.ppermute(block, axis, [((i + step) % count, i) for i in range(count)])


def weight_heads(w3, sibling):
    def kernel(w_ref, keep_ref, send_ref, sems):
        mx = lax.axis_index("mx")
        z = mx >> 1
        lane = (mx & 1) ^ (1 if sibling else 0)
        copies = []
        for place in (2, 3, 0, 1):
            head = lane * 4 + (z ^ ORDER[place])
            dst = keep_ref if place < 2 else send_ref
            for s in range(3):
                copies.append(
                    pltpu.make_async_copy(
                        w_ref.at[s, :, pl.ds(pl.multiple_of(head * HD, HD), HD)],
                        dst.at[:, pl.ds((place % 2) * HEAD + s * HD, HD)],
                        sems.at[len(copies)],
                    )
                )
        for copy in copies:
            copy.start()
        for copy in copies:
            copy.wait()

    shape = ((DL, 2 * HEAD), BF16)
    return call(kernel, [shape, shape], [HBM], [pltpu.SemaphoreType.DMA((12,))])(w3)


def table(counts, owner, target):
    def kernel(counts_ref, owner_ref, target_ref, out_ref, source):
        group = lax.axis_index("img")
        my = lax.axis_index("my")
        for t in range(GRP):
            source[t] = -1
        base = (group >> 1) * 4
        offset = jnp.int32(0)
        for i in range(4):
            image = base + i
            count = counts_ref[image]
            owned = owner_ref[image] == group
            side = jnp.where((image >> 1) == group, 0, GRP)
            for b in range(4):

                @pl.when(owned & (b < count))
                def _():
                    place = target_ref[0, jnp.minimum(offset + b, GRP - 1)]
                    source[place] = side + (i & 1) * 4 + b

            offset = offset + jnp.where(owned, count, 0)
        for n, step in enumerate((2, 1, 3, 0)):
            shard = (my + step) & 3
            out_ref[2 * n] = source[2 * shard]
            out_ref[2 * n + 1] = source[2 * shard + 1]
        out_ref[8] = counts_ref[2 * group]
        out_ref[9] = counts_ref[2 * group + 1]

    (out,) = call(
        kernel,
        [((16,), jnp.int32)],
        [SMEM] * 3,
        [pltpu.SMEM((GRP,), jnp.int32)],
        limit=4,
        out_specs=[SMEM],
    )(counts, owner, target)
    return out


def load_rows(rows, xo_refs, xs_refs):
    at = 0
    for xo_ref, xs_ref in zip(xo_refs, xs_refs):
        size = xo_ref.shape[0]
        rows[at : at + size, 0:DL] = xo_ref[...]
        rows[at : at + size, DL:CHIP] = xs_ref[...]
        at += size
    rows[at : at + 16, :] = jnp.ones((16, CHIP), BF16)


def row_stats(xo_refs, xs_refs):
    stats = []
    for xo_ref, xs_ref in zip(xo_refs, xs_refs):
        fo, fs = xo_ref[...].astype(F32), xs_ref[...].astype(F32)
        s1 = jnp.sum(fo, axis=1, keepdims=True) + jnp.sum(fs, axis=1, keepdims=True)
        s2 = jnp.sum(fo * fo, axis=1, keepdims=True) + jnp.sum(fs * fs, axis=1, keepdims=True)
        lane = lax.broadcasted_iota(jnp.int32, (xo_ref.shape[0], HD), 1)
        stats.append(jnp.where(lane == 0, s1, jnp.where(lane == 1, s2, F32(0.0))))
    return stats[0] if len(stats) == 1 else jnp.concatenate(stats, axis=0)


def partial_tile(rows, wo_ref, ws_ref, columns, center):
    count = center.shape[0]
    acc = jnp.dot(rows[:, 0:DL], wo_ref[:, columns], preferred_element_type=F32)
    acc = acc + jnp.dot(rows[:, DL:CHIP], ws_ref[:, columns], preferred_element_type=F32)
    sums = acc[count : count + 8, :]
    return acc[0:count, :] - center * sums[0:1, :], sums


def rows_scratch(count):
    return pltpu.VMEM((count + 16, CHIP), BF16)


def note_terms(note):
    terms = []
    for _ in range(3):
        terms.append(note.astype(BF16).astype(F32))
        note = note - terms[-1]
    return jnp.concatenate(terms + [jnp.zeros_like(note)], axis=0).astype(BF16)


def read_note(rows):
    terms = rows.astype(F32)
    return terms[0:8, :] + terms[8:16, :] + terms[16:24, :]


def head_note(sums, columns):
    return jnp.concatenate([sums, jnp.concatenate(columns + [jnp.zeros((5, HD), F32)], axis=0)], axis=1)


def send_part(xo, xs, wo, ws, earlier=(), after=()):
    count = xo.shape[0]
    last = len(earlier) > 0

    def kernel(xo_ref, xs_ref, wo_ref, ws_ref, *refs):
        others, (out_ref, stat_ref, copy_ref, rows) = refs[: len(earlier)], refs[len(earlier) :]
        load_rows(rows, [xo_ref], [xs_ref])
        copy_ref[...] = xo_ref[...]
        stat = row_stats([xo_ref], [xs_ref])
        center = stat[:, 0:1] / CHIP
        column_sums = []
        for n in range(3):
            columns = slice(n * 256, (n + 1) * 256)
            tile, sums = partial_tile(rows, wo_ref, ws_ref, columns, center)
            out_ref[0:count, columns] = tile.astype(BF16)
            column_sums += [sums[0:1, 0:HD], sums[0:1, HD:256]]
        if not last:
            stat_ref[...] = stat
            return
        turned = [ref[k * SH : (k + 1) * SH, :].T for ref in others for k in range(ref.shape[0] // SH)] + [stat.T]
        lines = jnp.concatenate([t[0:1, :] for t in turned] + [t[1:2, :] for t in turned], axis=0)
        stat_ref[...] = lines
        for half in range(2):
            note = head_note(lines, column_sums[3 * half : 3 * half + 3])
            out_ref[count : count + EXTRA, half * HEAD : (half + 1) * HEAD] = note_terms(note)

    outs = [((count + EXTRA if last else count, 2 * HEAD), BF16), ((8, SH) if last else (count, HD), F32), ((count, DL), BF16)]
    ins = [VMEM] * (4 + len(earlier))
    return call(kernel, outs, ins, [rows_scratch(count)], after=after)(xo, xs, wo, ws, *earlier)


def own_product(blocks, weight, after):
    size = blocks[0].shape[0]
    count = len(blocks) * size

    def kernel(*refs):
        w_ref, out_ref, rows = refs[len(blocks) :]
        for i in range(len(blocks)):
            rows[i * size : (i + 1) * size, :] = refs[i][...]
        rows[count : count + 16, :] = jnp.ones((16, DL), BF16)
        for n in range(3):
            columns = slice(n * 256, (n + 1) * 256)
            out_ref[:, columns] = jnp.dot(rows[...], w_ref[:, columns], preferred_element_type=F32)

    outs = [((count + 16, 2 * HEAD), F32)]
    scratch = [pltpu.VMEM((count + 16, DL), BF16)]
    (out,) = call(kernel, outs, [VMEM] * (1 + len(blocks)), scratch, after=after)(*blocks, weight)
    return out


def rest_part(xo, xs, weight, product, after):
    size, blocks = xo[0].shape[0], len(xo)
    count = blocks * size

    def kernel(*refs):
        xo_refs, xs_refs = refs[:blocks], refs[blocks : 2 * blocks]
        w_ref, product_ref, out_ref, stat_ref, rows = refs[2 * blocks :]
        for i, ref in enumerate(xs_refs):
            rows[i * size : (i + 1) * size, :] = ref[...]
        rows[count : count + 16, :] = jnp.ones((16, DL), BF16)
        stat = row_stats(xo_refs, xs_refs)
        stat_ref[...] = stat
        center = stat[:, 0:1] / CHIP
        for n in range(3):
            columns = slice(n * 256, (n + 1) * 256)
            acc = product_ref[:, columns] + jnp.dot(rows[...], w_ref[:, columns], preferred_element_type=F32)
            out_ref[:, columns] = (acc[0:count, :] - center * acc[count : count + 1, :]).astype(BF16)

    outs = [((count, 2 * HEAD), BF16), ((count, HD), F32)]
    scratch = [pltpu.VMEM((count + 16, DL), BF16)]
    return call(kernel, outs, [VMEM] * (2 * blocks + 2), scratch, after=after)(*xo, *xs, weight, product)


def kept_part(xo, xs, wo, ws, stat, last=False, after=()):
    blocks = len(xo)
    count = sum(block.shape[0] for block in xo)

    def kernel(*refs):
        xo_refs, xs_refs = refs[:blocks], refs[blocks : 2 * blocks]
        wo_ref, ws_ref, stat_ref, kept_ref = refs[2 * blocks : 2 * blocks + 4]
        refs, rows = refs[2 * blocks + 4 : -1], refs[-1]
        load_rows(rows, xo_refs, xs_refs)
        stat = row_stats(xo_refs, xs_refs) if last else stat_ref[...]
        center = stat[:, 0:1] / CHIP
        column_sums = []
        for n in range(3):
            columns = slice(n * 256, (n + 1) * 256)
            tile, sums = partial_tile(rows, wo_ref, ws_ref, columns, center)
            kept_ref[:, columns] = tile
            column_sums += [sums[0:1, 0:HD], sums[0:1, HD:256]]
        if last:
            refs[0][...] = head_note(stat_ref[...], column_sums[0:3])
            refs[1][...] = note_terms(head_note(stat_ref[...], column_sums[3:6]))

    outs = [((count, 2 * HEAD), F32)] + ([((8, HEAD), F32), ((EXTRA, HEAD), BF16)] if last else [])
    return call(kernel, outs, [VMEM] * (2 * blocks + 3), [rows_scratch(count)], after=after)(*xo, *xs, wo, ws, stat)


def add_part(kept, got, more=None, note=None, after=()):
    count = kept.shape[0]
    extra = list(more or ())
    last = note is not None
    ins = [kept, got] + extra + ([note] if last else [])

    def kernel(kept_ref, got_ref, *refs):
        own_ref, send_ref = refs[len(ins) - 2], refs[len(ins) - 1]
        own_ref[...] = kept_ref[:, 0:HEAD] + got_ref[0:count, 0:HEAD].astype(F32)
        send_ref[0:count, :] = (kept_ref[:, HEAD:] + got_ref[0:count, HEAD:].astype(F32)).astype(BF16)
        if extra:
            refs[len(ins)][...] = refs[0][...] + refs[1][...].astype(F32)
        if last:
            under = slice(count, count + EXTRA)
            terms = [refs[len(ins) - 3][...], got_ref[under, HEAD:]]
            terms = jnp.concatenate([rows.astype(F32)[0:TERMS, :] for rows in terms], axis=0)
            send_ref[count : count + 2 * TERMS, :] = terms.astype(BF16)
            refs[-1][...] = read_note(got_ref[under, 0:HEAD])

    outs = [((count, HEAD), F32), ((count + 2 * TERMS if last else count, HEAD), BF16)]
    outs += [((SH, HEAD), F32)] if extra else []
    outs += [((8, HEAD), F32)] if last else []
    return call(kernel, outs, [VMEM] * len(ins), after=after)(*ins)


def last_sum(own, got, mine, near):
    def kernel(own_ref, got_ref, mine_ref, near_ref, out_ref, coef_ref, cs_ref):
        out_ref[...] = own_ref[...] + got_ref[0:SH, :].astype(F32)
        notes = [mine_ref[...], near_ref[...]]
        terms = got_ref[SH : SH + 2 * TERMS, :].astype(F32)
        notes += [read_note(terms[at : at + TERMS, :]) for at in (0, TERMS)]
        for k in range(4):
            sums = [n[k : k + 1, 0:SH] for n in notes]
            squares = [n[4 + k : 5 + k, 0:SH] for n in notes]
            mean = (sums[0] + sums[1] + sums[2] + sums[3]) / D
            var = (squares[0] + squares[1] + squares[2] + squares[3]) / D - mean * mean
            lines = [lax.rsqrt(var + 1e-06)] + [s / CHIP - mean for s in sums] + [jnp.zeros((HD - 5, SH), F32)]
            coef_ref[k * SH : (k + 1) * SH, :] = jnp.concatenate(lines, axis=0).T
        for c, n in enumerate(notes):
            for place in range(3):
                cs_ref[c : c + 1, place * HD : (place + 1) * HD] = n[place : place + 1, SH:HEAD]
        cs_ref[4:8, :] = jnp.zeros((4, HEAD), F32)

    outs = [((SH, HEAD), F32), ((R, HD), F32), ((8, HEAD), F32)]
    return call(kernel, outs, [VMEM] * 4)(own, got, mine, near)


def join(blocks, axis, after=()):
    size = blocks[0].shape[axis]

    def kernel(*refs):
        for i, ref in enumerate(refs[:-1]):
            at = slice(i * size, (i + 1) * size)
            if axis == 0:
                refs[-1][at, :] = ref[...]
            else:
                refs[-1][:, at] = ref[...]

    shape = list(blocks[0].shape)
    shape[axis] *= len(blocks)
    (out,) = call(kernel, [(tuple(shape), BF16)], [VMEM] * len(blocks), after=after)(*blocks)
    return out


def attention(places, coef, cs, tot0, own12, end12, tot3):
    def kernel(places_ref, coef_ref, cs_ref, tot0_ref, own12_ref, end12_ref, tot3_ref, out_ref, qkv):
        my = lax.axis_index("my")
        for k, offset in enumerate((0, 1, 3, 2)):
            if k in (1, 2):
                at = slice((k - 1) * SH, k * SH)
                total = own12_ref[at, :] + end12_ref[at, :].astype(F32)
            else:
                total = (tot3_ref if k else tot0_ref)[...]
            coef = coef_ref[k * SH : (k + 1) * SH, :]
            for c in range(4):
                total = total + coef[:, c + 1 : c + 2] * cs_ref[c : c + 1, :]
            total = total * coef[:, 0:1]
            shard = (my + offset) & 3
            qkv[pl.ds(pl.multiple_of(shard * SH, SH), SH), :] = total.astype(BF16)
        first, second = places_ref[8], places_ref[9]
        for image in range(2):
            start = pl.multiple_of(first * BLK, BLK) if image else 0
            live = (second if image else first) * BLK
            q = qkv[pl.ds(start, IMG_ROWS), 0:HD]
            key = qkv[pl.ds(start, IMG_ROWS), HD : 2 * HD]
            value = qkv[pl.ds(start, IMG_ROWS), 2 * HD : 3 * HD]
            rows = lax.broadcasted_iota(jnp.int32, (IMG_ROWS, HD), 0)
            value = jnp.where(rows < live, value, jnp.zeros_like(value))
            scores = lax.dot_general(q, key, (((1,), (1,)), ((), ())), preferred_element_type=F32)
            columns = lax.broadcasted_iota(jnp.int32, (IMG_ROWS, IMG_ROWS), 1)
            scores = jnp.where(columns < live, scores, F32(-1e30))
            top = jnp.max(scores, axis=1, keepdims=True)
            powers = jnp.exp((scores - top) * HD ** (-0.5))
            mixture = jnp.dot(powers.astype(BF16), value, preferred_element_type=F32)
            mixture = mixture / jnp.sum(powers, axis=1, keepdims=True)
            out_ref[image * IMG_ROWS : (image + 1) * IMG_ROWS, :] = mixture.astype(BF16)

    (out,) = call(
        kernel, [((R, HD), BF16)], [SMEM] + [VMEM] * 6, [pltpu.VMEM((R, HEAD), BF16)], limit=24
    )(places, coef, cs, tot0, own12, end12, tot3)
    return out


def route(places, mine, other):
    def kernel(places_ref, mine_ref, other_ref, *outs):
        for n in range(GRP):
            out_ref = outs[n // 2]
            place = slice((n % 2) * BLK, (n % 2 + 1) * BLK)
            src = places_ref[n]
            row = pl.multiple_of((src & 7) * BLK, BLK)

            @pl.when(src < 0)
            def _():
                out_ref[place, :] = jnp.zeros((BLK, HD), BF16)

            @pl.when((src >= 0) & (src < GRP))
            def _():
                out_ref[place, :] = mine_ref[pl.ds(row, BLK), :]

            @pl.when(src >= GRP)
            def _():
                out_ref[place, :] = other_ref[pl.ds(row, BLK), :]

    return call(kernel, [((SH, HD), BF16)] * 4, [SMEM, VMEM, VMEM])(places, mine, other)


def lane_rows(blocks):
    def kernel(*refs):
        z = lax.axis_index("mx") >> 1
        for j, ref in zip((0,) + SENT, refs[:4]):
            for d in range(4):
                at = pl.multiple_of((d * 4 + (z ^ j)) * HD, HD)
                refs[4][:, pl.ds(at, HD)] = ref[0:FIRST, d * HD : (d + 1) * HD]
                refs[5][:, pl.ds(at, HD)] = ref[FIRST:SH, d * HD : (d + 1) * HD]

    return call(kernel, [((FIRST, 16 * HD), BF16), ((SH - FIRST, 16 * HD), BF16)], [VMEM] * 4)(*blocks)


def project_lane(lanes, weights):
    def kernel(lane0_ref, lane1_ref, w0_ref, w1_ref, w2_ref, out_ref, rows):
        side = lax.axis_index("mx") & 1
        rows[0:FIRST, :] = lane0_ref[:, 0 : 12 * HD]
        rows[FIRST:SH, :] = lane1_ref[:, 0 : 12 * HD]
        at = pl.ds(pl.multiple_of(side * 4 * HD, 4 * HD), 4 * HD)
        for n in range(3):
            columns = slice(n * 256, (n + 1) * 256)
            total = jnp.zeros((SH, 256), F32)
            for d, ref in enumerate((w0_ref, w1_ref, w2_ref)):
                heads = slice(d * 4 * HD, (d + 1) * 4 * HD)
                total = total + jnp.dot(rows[:, heads], ref[at, columns], preferred_element_type=F32)
            out_ref[:, columns] = total

    scratch = [pltpu.VMEM((SH, 12 * HD), BF16)]
    (out,) = call(kernel, [((SH, DL), F32)], [VMEM] * 5, scratch, limit=24)(*lanes, *weights)
    return out


def project(so_far, lanes, sibs, weights):
    def kernel(far_ref, lane0_ref, lane1_ref, sib0_ref, sib1_ref, w0_ref, w1_ref, w2_ref, top_ref, bottom_ref, out_ref, rows, low, high):
        side = lax.axis_index("mx") & 1
        last = slice(12 * HD, 16 * HD)
        for at, lane_ref, sib_ref in ((slice(0, FIRST), lane0_ref, sib0_ref), (slice(FIRST, SH), lane1_ref, sib1_ref)):
            rows[at, :] = sib_ref[:, 0 : 12 * HD]
            one, two = lane_ref[:, last], sib_ref[:, last]
            low[at, :] = jnp.where(side == 0, one, two)
            high[at, :] = jnp.where(side == 0, two, one)
        place = pl.ds(pl.multiple_of((1 - side) * 4 * HD, 4 * HD), 4 * HD)
        for n in range(3):
            columns = slice(n * 256, (n + 1) * 256)
            total = far_ref[:, columns]
            for d, ref in enumerate((w0_ref, w1_ref, w2_ref)):
                heads = slice(d * 4 * HD, (d + 1) * 4 * HD)
                total = total + jnp.dot(rows[:, heads], ref[place, columns], preferred_element_type=F32)
            total = total + jnp.dot(low[...], top_ref[:, columns], preferred_element_type=F32)
            total = total + jnp.dot(high[...], bottom_ref[:, columns], preferred_element_type=F32)
            out_ref[:, columns] = total.astype(BF16)

    scratch = [pltpu.VMEM((SH, 12 * HD), BF16)] + [pltpu.VMEM((SH, 4 * HD), BF16)] * 2
    (out,) = call(kernel, [((SH, DL), BF16)], [VMEM] * 10, scratch, limit=24)(so_far, *lanes, *sibs, *weights)
    return out


def shards(patches, tile_counts, image_owner, block_target, qkv_weight, out_weight):
    scope = jax.named_scope
    with scope("rows_near"):
        next_rows, last_rows = shift(patches, "my", 1), shift(patches, "my", -1)
    w3 = jnp.transpose(qkv_weight, (1, 0, 2))
    with scope("weights"):
        theirs_keep, theirs_send = weight_heads(w3, True)
        sib_send = swap(theirs_send, "mx", 1)
        sib_keep = swap(theirs_keep, "mx", 1)
        own_keep, own_send = weight_heads(w3, False)
        places = table(tile_counts, image_owner, block_target)
    weights = (own_keep, sib_keep, own_send, sib_send)

    with scope("chunk0"):
        s0 = swap(patches, "mx", 1)
        part0, stat0, again = send_part(patches, s0, own_send, sib_send)
        got0 = swap(part0, "mx", 2)
    with scope("rows_far"):
        x3 = shift(again, "my", 2)
    with scope("sum0"):
        (kept0,) = kept_part([patches], [s0], own_keep, sib_keep, stat0)
    with scope("chunk12"):
        x12 = [next_rows, last_rows]
        s12 = [swap(x, "mx", 1) for x in x12]
        product = own_product(x12, own_send, (kept0,))
        own0, next0 = add_part(kept0, got0, after=(product,))
        end0 = swap(next0, "mx", 4)
        part12, stat12 = rest_part(x12, s12, sib_send, product, (next0,))
        got12 = swap(part12, "mx", 2)
    with scope("chunk3"):
        (x3,) = gate([x3], (part12, end0))
        s3 = swap(x3, "mx", 1)
        (kept12,) = kept_part(x12, s12, own_keep, sib_keep, stat12, after=(part12,))
        part3, stat3, _ = send_part(x3, s3, own_send, sib_send, (stat0, stat12), (kept12, places))
        kept3, mine, note = kept_part([x3], [s3], own_keep, sib_keep, stat3, True, (part3,))
        (held3,) = gate([part3], (kept3, kept12))
        got3 = swap(held3, "mx", 2)
    with scope("sum12"):

        own12, next12, tot0 = add_part(kept12, got12, (own0, end0))
        end12 = swap(next12, "mx", 4)
    with scope("sum3"):
        own3, next3, near = add_part(kept3, got3, note=note, after=(next12,))
        tot3, coef, cs = last_sum(own3, swap(next3, "mx", 4), mine, near)
    with scope("out_weight"):
        w_next, w_last = shift(out_weight, "my", 1), shift(out_weight, "my", -1)
        w_far = [shift(w_next[: 4 * HD], "my", 1), shift(w_last[4 * HD :], "my", -1)]

    with scope("attention"):
        attended = attention(places, coef, cs, tot0, own12, end12, tot3)
        other = swap(attended, "img", 1)
        far, up, down, own = route(places, attended, other)
        near = [own, shift(down, "my", 1), shift(up, "my", -1), shift(far, "my", 2)]

    with scope("out"):
        block = join(near, 1)
        lanes = lane_rows([block] + [swap(block, "mx", 2 * j) for j in SENT])
        sibs = [swap(lane, "mx", 1) for lane in lanes]
        so_far = project_lane(lanes, [out_weight, w_next, w_last])
        return project(so_far, lanes, sibs, [out_weight, w_next, w_last] + w_far)


def solution(mesh):
    in_specs = (
        P(("img", "my"), "mx"),
        P(),
        P(),
        P("img", None),
        P("mx", None, "my"),
        P("my", "mx"),
    )
    out_specs = P(("img", "my"), "mx")
    return jax.shard_map(shards, mesh=mesh, in_specs=in_specs, out_specs=out_specs, check_vma=False)
```

```python
import jax
import jax.numpy as jnp
from jax import lax
from jax.experimental import pallas as pl
from jax.experimental.pallas import tpu as pltpu
from jax.sharding import PartitionSpec as P

D = 6144
HD = 128
BLK = 128
GRP = 8
R = 1024
SH = 256
DL = 768
CHIP = 2 * DL
HEAD = 3 * HD
IMG_ROWS = 512
ORDER = (0, 2, 1, 3)
FIRST = 160
EXTRA = 32
TERMS = 24
SENT = (2, 1, 3)
F32 = jnp.float32
BF16 = jnp.bfloat16

VMEM = pl.BlockSpec(memory_space=pltpu.VMEM)
SMEM = pl.BlockSpec(memory_space=pltpu.SMEM)
ANY = pl.BlockSpec(memory_space=pl.ANY)
HBM = pl.BlockSpec(memory_space=pltpu.HBM)


def call(kernel, outs, ins, scratch=(), limit=16, out_specs=None, after=(), aliases=None):
    out_shape = [jax.ShapeDtypeStruct(s, d) for s, d in outs]
    count = len(ins)

    def ordered(*refs):
        kernel(*refs[:count], *refs[count + len(after) :])

    made = pl.pallas_call(
        ordered,
        out_shape=out_shape,
        in_specs=list(ins) + [ANY] * len(after),
        out_specs=out_specs or [VMEM] * len(outs),
        scratch_shapes=list(scratch),
        input_output_aliases=aliases or {},
        compiler_params=pltpu.CompilerParams(vmem_limit_bytes=limit << 20),
        cost_estimate=pl.CostEstimate(flops=0, bytes_accessed=1024, transcendentals=0),
    )
    return lambda *args: made(*args, *after)


def gate(blocks, after):
    def kernel(*refs):
        pass

    outs = [(b.shape, b.dtype) for b in blocks]
    ins = [ANY] * len(blocks)
    same = {i: i for i in range(len(blocks))}
    return call(kernel, outs, ins, limit=4, out_specs=ins, after=after, aliases=same)(*blocks)


def swap(block, axis, bits):
    count = lax.axis_size(axis)
    return lax.ppermute(block, axis, [(i, i ^ bits) for i in range(count)])


def shift(block, axis, step):
    count = lax.axis_size(axis)
    return lax.ppermute(block, axis, [((i + step) % count, i) for i in range(count)])


def weight_heads(w3, sibling):
    def kernel(w_ref, keep_ref, send_ref, sems):
        mx = lax.axis_index("mx")
        z = mx >> 1
        lane = (mx & 1) ^ (1 if sibling else 0)
        copies = []
        for place in (2, 3, 0, 1):
            head = lane * 4 + (z ^ ORDER[place])
            dst = keep_ref if place < 2 else send_ref
            for s in range(3):
                copies.append(
                    pltpu.make_async_copy(
                        w_ref.at[s, :, pl.ds(pl.multiple_of(head * HD, HD), HD)],
                        dst.at[:, pl.ds((place % 2) * HEAD + s * HD, HD)],
                        sems.at[len(copies)],
                    )
                )
        for copy in copies:
            copy.start()
        for copy in copies:
            copy.wait()

    shape = ((DL, 2 * HEAD), BF16)
    return call(kernel, [shape, shape], [HBM], [pltpu.SemaphoreType.DMA((12,))])(w3)


def table(counts, owner, target):
    def kernel(counts_ref, owner_ref, target_ref, out_ref, source):
        group = lax.axis_index("img")
        my = lax.axis_index("my")
        for t in range(GRP):
            source[t] = -1
        base = (group >> 1) * 4
        offset = jnp.int32(0)
        for i in range(4):
            image = base + i
            count = counts_ref[image]
            owned = owner_ref[image] == group
            side = jnp.where((image >> 1) == group, 0, GRP)
            for b in range(4):

                @pl.when(owned & (b < count))
                def _():
                    place = target_ref[0, jnp.minimum(offset + b, GRP - 1)]
                    source[place] = side + (i & 1) * 4 + b

            offset = offset + jnp.where(owned, count, 0)
        for n, step in enumerate((2, 1, 3, 0)):
            shard = (my + step) & 3
            out_ref[2 * n] = source[2 * shard]
            out_ref[2 * n + 1] = source[2 * shard + 1]
        out_ref[8] = counts_ref[2 * group]
        out_ref[9] = counts_ref[2 * group + 1]

    (out,) = call(
        kernel,
        [((16,), jnp.int32)],
        [SMEM] * 3,
        [pltpu.SMEM((GRP,), jnp.int32)],
        limit=4,
        out_specs=[SMEM],
    )(counts, owner, target)
    return out


def load_rows(rows, xo_refs, xs_refs):
    at = 0
    for xo_ref, xs_ref in zip(xo_refs, xs_refs):
        size = xo_ref.shape[0]
        rows[at : at + size, 0:DL] = xo_ref[...]
        rows[at : at + size, DL:CHIP] = xs_ref[...]
        at += size
    rows[at : at + 16, :] = jnp.ones((16, CHIP), BF16)


def row_stats(xo_refs, xs_refs):
    stats = []
    for xo_ref, xs_ref in zip(xo_refs, xs_refs):
        fo, fs = xo_ref[...].astype(F32), xs_ref[...].astype(F32)
        s1 = jnp.sum(fo, axis=1, keepdims=True) + jnp.sum(fs, axis=1, keepdims=True)
        s2 = jnp.sum(fo * fo, axis=1, keepdims=True) + jnp.sum(fs * fs, axis=1, keepdims=True)
        lane = lax.broadcasted_iota(jnp.int32, (xo_ref.shape[0], HD), 1)
        stats.append(jnp.where(lane == 0, s1, jnp.where(lane == 1, s2, F32(0.0))))
    return stats[0] if len(stats) == 1 else jnp.concatenate(stats, axis=0)


def partial_tile(rows, wo_ref, ws_ref, columns, center):
    count = center.shape[0]
    acc = jnp.dot(rows[:, 0:DL], wo_ref[:, columns], preferred_element_type=F32)
    acc = acc + jnp.dot(rows[:, DL:CHIP], ws_ref[:, columns], preferred_element_type=F32)
    sums = acc[count : count + 8, :]
    return acc[0:count, :] - center * sums[0:1, :], sums


def rows_scratch(count):
    return pltpu.VMEM((count + 16, CHIP), BF16)


def note_terms(note):
    terms = []
    for _ in range(3):
        terms.append(note.astype(BF16).astype(F32))
        note = note - terms[-1]
    return jnp.concatenate(terms + [jnp.zeros_like(note)], axis=0).astype(BF16)


def read_note(rows):
    terms = rows.astype(F32)
    return terms[0:8, :] + terms[8:16, :] + terms[16:24, :]


def head_note(sums, columns):
    return jnp.concatenate([sums, jnp.concatenate(columns + [jnp.zeros((5, HD), F32)], axis=0)], axis=1)


def send_part(xo, xs, wo, ws, earlier=(), after=()):
    count = xo.shape[0]
    last = len(earlier) > 0

    def kernel(xo_ref, xs_ref, wo_ref, ws_ref, *refs):
        others, (out_ref, stat_ref, copy_ref, rows) = refs[: len(earlier)], refs[len(earlier) :]
        load_rows(rows, [xo_ref], [xs_ref])
        copy_ref[...] = xo_ref[...]
        stat = row_stats([xo_ref], [xs_ref])
        center = stat[:, 0:1] / CHIP
        column_sums = []
        for n in range(3):
            columns = slice(n * 256, (n + 1) * 256)
            tile, sums = partial_tile(rows, wo_ref, ws_ref, columns, center)
            out_ref[0:count, columns] = tile.astype(BF16)
            column_sums += [sums[0:1, 0:HD], sums[0:1, HD:256]]
        if not last:
            stat_ref[...] = stat
            return
        turned = [ref[k * SH : (k + 1) * SH, :].T for ref in others for k in range(ref.shape[0] // SH)] + [stat.T]
        lines = jnp.concatenate([t[0:1, :] for t in turned] + [t[1:2, :] for t in turned], axis=0)
        stat_ref[...] = lines
        for half in range(2):
            note = head_note(lines, column_sums[3 * half : 3 * half + 3])
            out_ref[count : count + EXTRA, half * HEAD : (half + 1) * HEAD] = note_terms(note)

    outs = [((count + EXTRA if last else count, 2 * HEAD), BF16), ((8, SH) if last else (count, HD), F32), ((count, DL), BF16)]
    ins = [VMEM] * (4 + len(earlier))
    return call(kernel, outs, ins, [rows_scratch(count)], after=after)(xo, xs, wo, ws, *earlier)


def own_product(blocks, weight, after):
    size = blocks[0].shape[0]
    count = len(blocks) * size

    def kernel(*refs):
        w_ref, out_ref, rows = refs[len(blocks) :]
        for i in range(len(blocks)):
            rows[i * size : (i + 1) * size, :] = refs[i][...]
        rows[count : count + 16, :] = jnp.ones((16, DL), BF16)
        for n in range(3):
            columns = slice(n * 256, (n + 1) * 256)
            out_ref[:, columns] = jnp.dot(rows[...], w_ref[:, columns], preferred_element_type=F32)

    outs = [((count + 16, 2 * HEAD), F32)]
    scratch = [pltpu.VMEM((count + 16, DL), BF16)]
    (out,) = call(kernel, outs, [VMEM] * (1 + len(blocks)), scratch, after=after)(*blocks, weight)
    return out


def rest_part(xo, xs, weight, product, after):
    size, blocks = xo[0].shape[0], len(xo)
    count = blocks * size

    def kernel(*refs):
        xo_refs, xs_refs = refs[:blocks], refs[blocks : 2 * blocks]
        w_ref, product_ref, out_ref, stat_ref, rows = refs[2 * blocks :]
        for i, ref in enumerate(xs_refs):
            rows[i * size : (i + 1) * size, :] = ref[...]
        rows[count : count + 16, :] = jnp.ones((16, DL), BF16)
        stat = row_stats(xo_refs, xs_refs)
        stat_ref[...] = stat
        center = stat[:, 0:1] / CHIP
        for n in range(3):
            columns = slice(n * 256, (n + 1) * 256)
            acc = product_ref[:, columns] + jnp.dot(rows[...], w_ref[:, columns], preferred_element_type=F32)
            out_ref[:, columns] = (acc[0:count, :] - center * acc[count : count + 1, :]).astype(BF16)

    outs = [((count, 2 * HEAD), BF16), ((count, HD), F32)]
    scratch = [pltpu.VMEM((count + 16, DL), BF16)]
    return call(kernel, outs, [VMEM] * (2 * blocks + 2), scratch, after=after)(*xo, *xs, weight, product)


def kept_part(xo, xs, wo, ws, stat, last=False, after=()):
    blocks = len(xo)
    count = sum(block.shape[0] for block in xo)

    def kernel(*refs):
        xo_refs, xs_refs = refs[:blocks], refs[blocks : 2 * blocks]
        wo_ref, ws_ref, stat_ref, kept_ref = refs[2 * blocks : 2 * blocks + 4]
        refs, rows = refs[2 * blocks + 4 : -1], refs[-1]
        load_rows(rows, xo_refs, xs_refs)
        stat = row_stats(xo_refs, xs_refs) if last else stat_ref[...]
        center = stat[:, 0:1] / CHIP
        column_sums = []
        for n in range(3):
            columns = slice(n * 256, (n + 1) * 256)
            tile, sums = partial_tile(rows, wo_ref, ws_ref, columns, center)
            kept_ref[:, columns] = tile
            column_sums += [sums[0:1, 0:HD], sums[0:1, HD:256]]
        if last:
            refs[0][...] = head_note(stat_ref[...], column_sums[0:3])
            refs[1][...] = note_terms(head_note(stat_ref[...], column_sums[3:6]))

    outs = [((count, 2 * HEAD), F32)] + ([((8, HEAD), F32), ((EXTRA, HEAD), BF16)] if last else [])
    return call(kernel, outs, [VMEM] * (2 * blocks + 3), [rows_scratch(count)], after=after)(*xo, *xs, wo, ws, stat)


def add_part(kept, got, more=None, note=None, after=()):
    count = kept.shape[0]
    extra = list(more or ())
    last = note is not None
    ins = [kept, got] + extra + ([note] if last else [])

    def kernel(kept_ref, got_ref, *refs):
        own_ref, send_ref = refs[len(ins) - 2], refs[len(ins) - 1]
        own_ref[...] = kept_ref[:, 0:HEAD] + got_ref[0:count, 0:HEAD].astype(F32)
        send_ref[0:count, :] = (kept_ref[:, HEAD:] + got_ref[0:count, HEAD:].astype(F32)).astype(BF16)
        if extra:
            refs[len(ins)][...] = refs[0][...] + refs[1][...].astype(F32)
        if last:
            under = slice(count, count + EXTRA)
            terms = [refs[len(ins) - 3][...], got_ref[under, HEAD:]]
            terms = jnp.concatenate([rows.astype(F32)[0:TERMS, :] for rows in terms], axis=0)
            send_ref[count : count + 2 * TERMS, :] = terms.astype(BF16)
            refs[-1][...] = read_note(got_ref[under, 0:HEAD])

    outs = [((count, HEAD), F32), ((count + 2 * TERMS if last else count, HEAD), BF16)]
    outs += [((SH, HEAD), F32)] if extra else []
    outs += [((8, HEAD), F32)] if last else []
    return call(kernel, outs, [VMEM] * len(ins), after=after)(*ins)


def last_sum(own, got, mine, near):
    def kernel(own_ref, got_ref, mine_ref, near_ref, out_ref, coef_ref, cs_ref):
        out_ref[...] = own_ref[...] + got_ref[0:SH, :].astype(F32)
        notes = [mine_ref[...], near_ref[...]]
        terms = got_ref[SH : SH + 2 * TERMS, :].astype(F32)
        notes += [read_note(terms[at : at + TERMS, :]) for at in (0, TERMS)]
        for k in range(4):
            sums = [n[k : k + 1, 0:SH] for n in notes]
            squares = [n[4 + k : 5 + k, 0:SH] for n in notes]
            mean = (sums[0] + sums[1] + sums[2] + sums[3]) / D
            var = (squares[0] + squares[1] + squares[2] + squares[3]) / D - mean * mean
            lines = [lax.rsqrt(var + 1e-06)] + [s / CHIP - mean for s in sums] + [jnp.zeros((HD - 5, SH), F32)]
            coef_ref[k * SH : (k + 1) * SH, :] = jnp.concatenate(lines, axis=0).T
        for c, n in enumerate(notes):
            for place in range(3):
                cs_ref[c : c + 1, place * HD : (place + 1) * HD] = n[place : place + 1, SH:HEAD]
        cs_ref[4:8, :] = jnp.zeros((4, HEAD), F32)

    outs = [((SH, HEAD), F32), ((R, HD), F32), ((8, HEAD), F32)]
    return call(kernel, outs, [VMEM] * 4)(own, got, mine, near)


def join(blocks, axis, places=None, after=()):
    size = blocks[0].shape[axis]
    places = places or range(len(blocks))

    def kernel(*refs):
        for i, ref in zip(places, refs[:-1]):
            at = slice(i * size, (i + 1) * size)
            if axis == 0:
                refs[-1][at, :] = ref[...]
            else:
                refs[-1][:, at] = ref[...]

    shape = list(blocks[0].shape)
    shape[axis] *= len(blocks)
    (out,) = call(kernel, [(tuple(shape), BF16)], [VMEM] * len(blocks), after=after)(*blocks)
    return out


def attention(places, coef, cs, tot0, own12, end12, tot3):
    def kernel(places_ref, coef_ref, cs_ref, tot0_ref, own12_ref, end12_ref, tot3_ref, out_ref, qkv):
        my = lax.axis_index("my")
        for k, offset in enumerate((0, 1, 3, 2)):
            if k in (1, 2):
                at = slice((k - 1) * SH, k * SH)
                total = own12_ref[at, :] + end12_ref[at, :].astype(F32)
            else:
                total = (tot3_ref if k else tot0_ref)[...]
            coef = coef_ref[k * SH : (k + 1) * SH, :]
            for c in range(4):
                total = total + coef[:, c + 1 : c + 2] * cs_ref[c : c + 1, :]
            total = total * coef[:, 0:1]
            shard = (my + offset) & 3
            qkv[pl.ds(pl.multiple_of(shard * SH, SH), SH), :] = total.astype(BF16)
        first, second = places_ref[8], places_ref[9]
        for image in range(2):
            start = pl.multiple_of(first * BLK, BLK) if image else 0
            live = (second if image else first) * BLK
            q = qkv[pl.ds(start, IMG_ROWS), 0:HD]
            key = qkv[pl.ds(start, IMG_ROWS), HD : 2 * HD]
            value = qkv[pl.ds(start, IMG_ROWS), 2 * HD : 3 * HD]
            rows = lax.broadcasted_iota(jnp.int32, (IMG_ROWS, HD), 0)
            value = jnp.where(rows < live, value, jnp.zeros_like(value))
            scores = lax.dot_general(q, key, (((1,), (1,)), ((), ())), preferred_element_type=F32)
            columns = lax.broadcasted_iota(jnp.int32, (IMG_ROWS, IMG_ROWS), 1)
            scores = jnp.where(columns < live, scores, F32(-1e30))
            top = jnp.max(scores, axis=1, keepdims=True)
            powers = jnp.exp((scores - top) * HD ** (-0.5))
            mixture = jnp.dot(powers.astype(BF16), value, preferred_element_type=F32)
            mixture = mixture / jnp.sum(powers, axis=1, keepdims=True)
            out_ref[image * IMG_ROWS : (image + 1) * IMG_ROWS, :] = mixture.astype(BF16)

    (out,) = call(
        kernel, [((R, HD), BF16)], [SMEM] + [VMEM] * 6, [pltpu.VMEM((R, HEAD), BF16)], limit=24
    )(places, coef, cs, tot0, own12, end12, tot3)
    return out


def route(places, mine, other):
    def kernel(places_ref, mine_ref, other_ref, *outs):
        for n in range(GRP):
            out_ref = outs[n // 2]
            place = slice((n % 2) * BLK, (n % 2 + 1) * BLK)
            src = places_ref[n]
            row = pl.multiple_of((src & 7) * BLK, BLK)

            @pl.when(src < 0)
            def _():
                out_ref[place, :] = jnp.zeros((BLK, HD), BF16)

            @pl.when((src >= 0) & (src < GRP))
            def _():
                out_ref[place, :] = mine_ref[pl.ds(row, BLK), :]

            @pl.when(src >= GRP)
            def _():
                out_ref[place, :] = other_ref[pl.ds(row, BLK), :]

    return call(kernel, [((SH, HD), BF16)] * 4, [SMEM, VMEM, VMEM])(places, mine, other)


def lane_rows(blocks):
    def kernel(*refs):
        z = lax.axis_index("mx") >> 1
        for j, ref in zip((0,) + SENT, refs[:4]):
            for d in range(4):
                at = pl.multiple_of((d * 4 + (z ^ j)) * HD, HD)
                refs[4][:, pl.ds(at, HD)] = ref[0:FIRST, d * HD : (d + 1) * HD]
                refs[5][:, pl.ds(at, HD)] = ref[FIRST:SH, d * HD : (d + 1) * HD]

    return call(kernel, [((FIRST, 16 * HD), BF16), ((SH - FIRST, 16 * HD), BF16)], [VMEM] * 4)(*blocks)


def project_lane(lanes, weights):
    def kernel(lane0_ref, lane1_ref, w0_ref, w1_ref, w2_ref, out_ref, rows):
        side = lax.axis_index("mx") & 1
        rows[0:FIRST, :] = lane0_ref[:, 0 : 12 * HD]
        rows[FIRST:SH, :] = lane1_ref[:, 0 : 12 * HD]
        at = pl.ds(pl.multiple_of(side * 4 * HD, 4 * HD), 4 * HD)
        for n in range(3):
            columns = slice(n * 256, (n + 1) * 256)
            total = jnp.zeros((SH, 256), F32)
            for d, ref in enumerate((w0_ref, w1_ref, w2_ref)):
                heads = slice(d * 4 * HD, (d + 1) * 4 * HD)
                total = total + jnp.dot(rows[:, heads], ref[at, columns], preferred_element_type=F32)
            out_ref[:, columns] = total

    scratch = [pltpu.VMEM((SH, 12 * HD), BF16)]
    (out,) = call(kernel, [((SH, DL), F32)], [VMEM] * 5, scratch, limit=24)(*lanes, *weights)
    return out


def project(so_far, lanes, sibs, weights):
    def kernel(far_ref, lane0_ref, lane1_ref, sib0_ref, sib1_ref, w0_ref, w1_ref, w2_ref, top_ref, bottom_ref, out_ref, rows, low, high):
        side = lax.axis_index("mx") & 1
        last = slice(12 * HD, 16 * HD)
        for at, lane_ref, sib_ref in ((slice(0, FIRST), lane0_ref, sib0_ref), (slice(FIRST, SH), lane1_ref, sib1_ref)):
            rows[at, :] = sib_ref[:, 0 : 12 * HD]
            one, two = lane_ref[:, last], sib_ref[:, last]
            low[at, :] = jnp.where(side == 0, one, two)
            high[at, :] = jnp.where(side == 0, two, one)
        place = pl.ds(pl.multiple_of((1 - side) * 4 * HD, 4 * HD), 4 * HD)
        for n in range(3):
            columns = slice(n * 256, (n + 1) * 256)
            total = far_ref[:, columns]
            for d, ref in enumerate((w0_ref, w1_ref, w2_ref)):
                heads = slice(d * 4 * HD, (d + 1) * 4 * HD)
                total = total + jnp.dot(rows[:, heads], ref[place, columns], preferred_element_type=F32)
            total = total + jnp.dot(low[...], top_ref[:, columns], preferred_element_type=F32)
            total = total + jnp.dot(high[...], bottom_ref[:, columns], preferred_element_type=F32)
            out_ref[:, columns] = total.astype(BF16)

    scratch = [pltpu.VMEM((SH, 12 * HD), BF16)] + [pltpu.VMEM((SH, 4 * HD), BF16)] * 2
    (out,) = call(kernel, [((SH, DL), BF16)], [VMEM] * 10, scratch, limit=24)(so_far, *lanes, *sibs, *weights)
    return out


def shards(patches, tile_counts, image_owner, block_target, qkv_weight, out_weight):
    scope = jax.named_scope
    with scope("rows_near"):
        next_rows, last_rows = shift(patches, "my", 1), shift(patches, "my", -1)
    w3 = jnp.transpose(qkv_weight, (1, 0, 2))
    with scope("weights"):
        theirs_keep, theirs_send = weight_heads(w3, True)
        sib_send = swap(theirs_send, "mx", 1)
        sib_keep = swap(theirs_keep, "mx", 1)
        own_keep, own_send = weight_heads(w3, False)
        places = table(tile_counts, image_owner, block_target)
    weights = (own_keep, sib_keep, own_send, sib_send)

    with scope("chunk0"):
        s0 = swap(patches, "mx", 1)
        part0, stat0, again = send_part(patches, s0, own_send, sib_send)
        got0 = swap(part0, "mx", 2)
    with scope("rows_far"):
        x3 = shift(again, "my", 2)
    with scope("sum0"):
        (kept0,) = kept_part([patches], [s0], own_keep, sib_keep, stat0)
    with scope("chunk12"):
        x12 = [next_rows, last_rows]
        s12 = [swap(x, "mx", 1) for x in x12]
        product = own_product(x12, own_send, (kept0,))
        own0, next0 = add_part(kept0, got0, after=(product,))
        end0 = swap(next0, "mx", 4)
        part12, stat12 = rest_part(x12, s12, sib_send, product, (next0,))
        got12 = swap(part12, "mx", 2)
    with scope("chunk3"):
        (x3,) = gate([x3], (part12, end0))
        s3 = swap(x3, "mx", 1)
        (kept12,) = kept_part(x12, s12, own_keep, sib_keep, stat12, after=(part12,))
        part3, stat3, _ = send_part(x3, s3, own_send, sib_send, (stat0, stat12), (kept12, places))
        kept3, mine, note = kept_part([x3], [s3], own_keep, sib_keep, stat3, True, (part3,))
        (held3,) = gate([part3], (kept3, kept12))
        got3 = swap(held3, "mx", 2)
    with scope("sum12"):

        own12, next12, tot0 = add_part(kept12, got12, (own0, end0))
        end12 = swap(next12, "mx", 4)
    with scope("sum3"):
        own3, next3, near = add_part(kept3, got3, note=note, after=(next12,))
        tot3, coef, cs = last_sum(own3, swap(next3, "mx", 4), mine, near)
    with scope("out_weight"):
        w_next, w_last = shift(out_weight, "my", 1), shift(out_weight, "my", -1)
        w_far = [shift(w_next[: 4 * HD], "my", 1), shift(w_last[4 * HD :], "my", -1)]

    with scope("attention"):
        attended = attention(places, coef, cs, tot0, own12, end12, tot3)
        other = swap(attended, "img", 1)
        far, up, down, own = route(places, attended, other)
        near = [own, shift(far, "my", 2), shift(down, "my", 1), shift(up, "my", -1)]

    with scope("out"):
        block = join(near, 1, (0, 3, 1, 2))
        lanes = lane_rows([block] + [swap(block, "mx", 2 * j) for j in SENT])
        sibs = [swap(lane, "mx", 1) for lane in lanes]
        so_far = project_lane(lanes, [out_weight, w_next, w_last])
        return project(so_far, lanes, sibs, [out_weight, w_next, w_last] + w_far)


def solution(mesh):
    in_specs = (
        P(("img", "my"), "mx"),
        P(),
        P(),
        P("img", None),
        P("mx", None, "my"),
        P("my", "mx"),
    )
    out_specs = P(("img", "my"), "mx")
    return jax.shard_map(shards, mesh=mesh, in_specs=in_specs, out_specs=out_specs, check_vma=False)
```

```python
import jax
import jax.numpy as jnp
from jax import lax
from jax.experimental import pallas as pl
from jax.experimental.pallas import tpu as pltpu
from jax.sharding import PartitionSpec as P

D = 6144
HD = 128
BLK = 128
GRP = 8
R = 1024
SH = 256
DL = 768
CHIP = 2 * DL
HEAD = 3 * HD
IMG_ROWS = 512
ORDER = (0, 2, 1, 3)
FIRST = 160
EXTRA = 32
TERMS = 24
SENT = (3, 1, 2)
F32 = jnp.float32
BF16 = jnp.bfloat16

VMEM = pl.BlockSpec(memory_space=pltpu.VMEM)
SMEM = pl.BlockSpec(memory_space=pltpu.SMEM)
ANY = pl.BlockSpec(memory_space=pl.ANY)
HBM = pl.BlockSpec(memory_space=pltpu.HBM)


def call(kernel, outs, ins, scratch=(), limit=16, out_specs=None, after=(), aliases=None):
    out_shape = [jax.ShapeDtypeStruct(s, d) for s, d in outs]
    count = len(ins)

    def ordered(*refs):
        kernel(*refs[:count], *refs[count + len(after) :])

    made = pl.pallas_call(
        ordered,
        out_shape=out_shape,
        in_specs=list(ins) + [ANY] * len(after),
        out_specs=out_specs or [VMEM] * len(outs),
        scratch_shapes=list(scratch),
        input_output_aliases=aliases or {},
        compiler_params=pltpu.CompilerParams(vmem_limit_bytes=limit << 20),
        cost_estimate=pl.CostEstimate(flops=0, bytes_accessed=1024, transcendentals=0),
    )
    return lambda *args: made(*args, *after)


def gate(blocks, after):
    def kernel(*refs):
        pass

    outs = [(b.shape, b.dtype) for b in blocks]
    ins = [ANY] * len(blocks)
    same = {i: i for i in range(len(blocks))}
    return call(kernel, outs, ins, limit=4, out_specs=ins, after=after, aliases=same)(*blocks)


def swap(block, axis, bits):
    count = lax.axis_size(axis)
    return lax.ppermute(block, axis, [(i, i ^ bits) for i in range(count)])


def shift(block, axis, step):
    count = lax.axis_size(axis)
    return lax.ppermute(block, axis, [((i + step) % count, i) for i in range(count)])


def weight_heads(w3, sibling):
    def kernel(w_ref, keep_ref, send_ref, sems):
        mx = lax.axis_index("mx")
        z = mx >> 1
        lane = (mx & 1) ^ (1 if sibling else 0)
        copies = []
        for place in (2, 3, 0, 1):
            head = lane * 4 + (z ^ ORDER[place])
            dst = keep_ref if place < 2 else send_ref
            for s in range(3):
                copies.append(
                    pltpu.make_async_copy(
                        w_ref.at[s, :, pl.ds(pl.multiple_of(head * HD, HD), HD)],
                        dst.at[:, pl.ds((place % 2) * HEAD + s * HD, HD)],
                        sems.at[len(copies)],
                    )
                )
        for copy in copies:
            copy.start()
        for copy in copies:
            copy.wait()

    shape = ((DL, 2 * HEAD), BF16)
    return call(kernel, [shape, shape], [HBM], [pltpu.SemaphoreType.DMA((12,))])(w3)


def table(counts, owner, target):
    def kernel(counts_ref, owner_ref, target_ref, out_ref, source):
        group = lax.axis_index("img")
        my = lax.axis_index("my")
        for t in range(GRP):
            source[t] = -1
        base = (group >> 1) * 4
        offset = jnp.int32(0)
        for i in range(4):
            image = base + i
            count = counts_ref[image]
            owned = owner_ref[image] == group
            side = jnp.where((image >> 1) == group, 0, GRP)
            for b in range(4):

                @pl.when(owned & (b < count))
                def _():
                    place = target_ref[0, jnp.minimum(offset + b, GRP - 1)]
                    source[place] = side + (i & 1) * 4 + b

            offset = offset + jnp.where(owned, count, 0)
        for n, step in enumerate((2, 1, 3, 0)):
            shard = (my + step) & 3
            out_ref[2 * n] = source[2 * shard]
            out_ref[2 * n + 1] = source[2 * shard + 1]
        out_ref[8] = counts_ref[2 * group]
        out_ref[9] = counts_ref[2 * group + 1]

    (out,) = call(
        kernel,
        [((16,), jnp.int32)],
        [SMEM] * 3,
        [pltpu.SMEM((GRP,), jnp.int32)],
        limit=4,
        out_specs=[SMEM],
    )(counts, owner, target)
    return out


def load_rows(rows, xo_refs, xs_refs):
    at = 0
    for xo_ref, xs_ref in zip(xo_refs, xs_refs):
        size = xo_ref.shape[0]
        rows[at : at + size, 0:DL] = xo_ref[...]
        rows[at : at + size, DL:CHIP] = xs_ref[...]
        at += size
    rows[at : at + 16, :] = jnp.ones((16, CHIP), BF16)


def row_stats(xo_refs, xs_refs):
    stats = []
    for xo_ref, xs_ref in zip(xo_refs, xs_refs):
        fo, fs = xo_ref[...].astype(F32), xs_ref[...].astype(F32)
        s1 = jnp.sum(fo, axis=1, keepdims=True) + jnp.sum(fs, axis=1, keepdims=True)
        s2 = jnp.sum(fo * fo, axis=1, keepdims=True) + jnp.sum(fs * fs, axis=1, keepdims=True)
        lane = lax.broadcasted_iota(jnp.int32, (xo_ref.shape[0], HD), 1)
        stats.append(jnp.where(lane == 0, s1, jnp.where(lane == 1, s2, F32(0.0))))
    return stats[0] if len(stats) == 1 else jnp.concatenate(stats, axis=0)


def partial_tile(rows, wo_ref, ws_ref, columns, center):
    count = center.shape[0]
    acc = jnp.dot(rows[:, 0:DL], wo_ref[:, columns], preferred_element_type=F32)
    acc = acc + jnp.dot(rows[:, DL:CHIP], ws_ref[:, columns], preferred_element_type=F32)
    sums = acc[count : count + 8, :]
    return acc[0:count, :] - center * sums[0:1, :], sums


def rows_scratch(count):
    return pltpu.VMEM((count + 16, CHIP), BF16)


def note_terms(note):
    terms = []
    for _ in range(3):
        terms.append(note.astype(BF16).astype(F32))
        note = note - terms[-1]
    return jnp.concatenate(terms + [jnp.zeros_like(note)], axis=0).astype(BF16)


def read_note(rows):
    terms = rows.astype(F32)
    return terms[0:8, :] + terms[8:16, :] + terms[16:24, :]


def head_note(sums, columns):
    return jnp.concatenate([sums, jnp.concatenate(columns + [jnp.zeros((5, HD), F32)], axis=0)], axis=1)


def send_part(xo, xs, wo, ws, earlier=(), after=()):
    count = xo.shape[0]
    last = len(earlier) > 0

    def kernel(xo_ref, xs_ref, wo_ref, ws_ref, *refs):
        others, (out_ref, stat_ref, copy_ref, rows) = refs[: len(earlier)], refs[len(earlier) :]
        load_rows(rows, [xo_ref], [xs_ref])
        copy_ref[...] = xo_ref[...]
        stat = row_stats([xo_ref], [xs_ref])
        center = stat[:, 0:1] / CHIP
        column_sums = []
        for n in range(3):
            columns = slice(n * 256, (n + 1) * 256)
            tile, sums = partial_tile(rows, wo_ref, ws_ref, columns, center)
            out_ref[0:count, columns] = tile.astype(BF16)
            column_sums += [sums[0:1, 0:HD], sums[0:1, HD:256]]
        if not last:
            stat_ref[...] = stat
            return
        turned = [ref[k * SH : (k + 1) * SH, :].T for ref in others for k in range(ref.shape[0] // SH)] + [stat.T]
        lines = jnp.concatenate([t[0:1, :] for t in turned] + [t[1:2, :] for t in turned], axis=0)
        stat_ref[...] = lines
        for half in range(2):
            note = head_note(lines, column_sums[3 * half : 3 * half + 3])
            out_ref[count : count + EXTRA, half * HEAD : (half + 1) * HEAD] = note_terms(note)

    outs = [((count + EXTRA if last else count, 2 * HEAD), BF16), ((8, SH) if last else (count, HD), F32), ((count, DL), BF16)]
    ins = [VMEM] * (4 + len(earlier))
    return call(kernel, outs, ins, [rows_scratch(count)], after=after)(xo, xs, wo, ws, *earlier)


def own_product(blocks, weight, after):
    size = blocks[0].shape[0]
    count = len(blocks) * size

    def kernel(*refs):
        w_ref, out_ref, rows = refs[len(blocks) :]
        for i in range(len(blocks)):
            rows[i * size : (i + 1) * size, :] = refs[i][...]
        rows[count : count + 16, :] = jnp.ones((16, DL), BF16)
        for n in range(3):
            columns = slice(n * 256, (n + 1) * 256)
            out_ref[:, columns] = jnp.dot(rows[...], w_ref[:, columns], preferred_element_type=F32)

    outs = [((count + 16, 2 * HEAD), F32)]
    scratch = [pltpu.VMEM((count + 16, DL), BF16)]
    (out,) = call(kernel, outs, [VMEM] * (1 + len(blocks)), scratch, after=after)(*blocks, weight)
    return out


def rest_part(xo, xs, weight, product, after):
    size, blocks = xo[0].shape[0], len(xo)
    count = blocks * size

    def kernel(*refs):
        xo_refs, xs_refs = refs[:blocks], refs[blocks : 2 * blocks]
        w_ref, product_ref, out_ref, stat_ref, rows = refs[2 * blocks :]
        for i, ref in enumerate(xs_refs):
            rows[i * size : (i + 1) * size, :] = ref[...]
        rows[count : count + 16, :] = jnp.ones((16, DL), BF16)
        stat = row_stats(xo_refs, xs_refs)
        stat_ref[...] = stat
        center = stat[:, 0:1] / CHIP
        for n in range(3):
            columns = slice(n * 256, (n + 1) * 256)
            acc = product_ref[:, columns] + jnp.dot(rows[...], w_ref[:, columns], preferred_element_type=F32)
            out_ref[:, columns] = (acc[0:count, :] - center * acc[count : count + 1, :]).astype(BF16)

    outs = [((count, 2 * HEAD), BF16), ((count, HD), F32)]
    scratch = [pltpu.VMEM((count + 16, DL), BF16)]
    return call(kernel, outs, [VMEM] * (2 * blocks + 2), scratch, after=after)(*xo, *xs, weight, product)


def kept_part(xo, xs, wo, ws, stat, last=False, after=()):
    blocks = len(xo)
    count = sum(block.shape[0] for block in xo)

    def kernel(*refs):
        xo_refs, xs_refs = refs[:blocks], refs[blocks : 2 * blocks]
        wo_ref, ws_ref, stat_ref, kept_ref = refs[2 * blocks : 2 * blocks + 4]
        refs, rows = refs[2 * blocks + 4 : -1], refs[-1]
        load_rows(rows, xo_refs, xs_refs)
        stat = row_stats(xo_refs, xs_refs) if last else stat_ref[...]
        center = stat[:, 0:1] / CHIP
        column_sums = []
        for n in range(3):
            columns = slice(n * 256, (n + 1) * 256)
            tile, sums = partial_tile(rows, wo_ref, ws_ref, columns, center)
            kept_ref[:, columns] = tile
            column_sums += [sums[0:1, 0:HD], sums[0:1, HD:256]]
        if last:
            refs[0][...] = head_note(stat_ref[...], column_sums[0:3])
            refs[1][...] = note_terms(head_note(stat_ref[...], column_sums[3:6]))

    outs = [((count, 2 * HEAD), F32)] + ([((8, HEAD), F32), ((EXTRA, HEAD), BF16)] if last else [])
    return call(kernel, outs, [VMEM] * (2 * blocks + 3), [rows_scratch(count)], after=after)(*xo, *xs, wo, ws, stat)


def add_part(kept, got, more=None, note=None, after=()):
    count = kept.shape[0]
    extra = list(more or ())
    last = note is not None
    ins = [kept, got] + extra + ([note] if last else [])

    def kernel(kept_ref, got_ref, *refs):
        own_ref, send_ref = refs[len(ins) - 2], refs[len(ins) - 1]
        own_ref[...] = kept_ref[:, 0:HEAD] + got_ref[0:count, 0:HEAD].astype(F32)
        send_ref[0:count, :] = (kept_ref[:, HEAD:] + got_ref[0:count, HEAD:].astype(F32)).astype(BF16)
        if extra:
            refs[len(ins)][...] = refs[0][...] + refs[1][...].astype(F32)
        if last:
            under = slice(count, count + EXTRA)
            terms = [refs[len(ins) - 3][...], got_ref[under, HEAD:]]
            terms = jnp.concatenate([rows.astype(F32)[0:TERMS, :] for rows in terms], axis=0)
            send_ref[count : count + 2 * TERMS, :] = terms.astype(BF16)
            refs[-1][...] = read_note(got_ref[under, 0:HEAD])

    outs = [((count, HEAD), F32), ((count + 2 * TERMS if last else count, HEAD), BF16)]
    outs += [((SH, HEAD), F32)] if extra else []
    outs += [((8, HEAD), F32)] if last else []
    return call(kernel, outs, [VMEM] * len(ins), after=after)(*ins)


def last_sum(own, got, mine, near):
    def kernel(own_ref, got_ref, mine_ref, near_ref, out_ref, coef_ref, cs_ref):
        out_ref[...] = own_ref[...] + got_ref[0:SH, :].astype(F32)
        notes = [mine_ref[...], near_ref[...]]
        terms = got_ref[SH : SH + 2 * TERMS, :].astype(F32)
        notes += [read_note(terms[at : at + TERMS, :]) for at in (0, TERMS)]
        for k in range(4):
            sums = [n[k : k + 1, 0:SH] for n in notes]
            squares = [n[4 + k : 5 + k, 0:SH] for n in notes]
            mean = (sums[0] + sums[1] + sums[2] + sums[3]) / D
            var = (squares[0] + squares[1] + squares[2] + squares[3]) / D - mean * mean
            lines = [lax.rsqrt(var + 1e-06)] + [s / CHIP - mean for s in sums] + [jnp.zeros((HD - 5, SH), F32)]
            coef_ref[k * SH : (k + 1) * SH, :] = jnp.concatenate(lines, axis=0).T
        for c, n in enumerate(notes):
            for place in range(3):
                cs_ref[c : c + 1, place * HD : (place + 1) * HD] = n[place : place + 1, SH:HEAD]
        cs_ref[4:8, :] = jnp.zeros((4, HEAD), F32)

    outs = [((SH, HEAD), F32), ((R, HD), F32), ((8, HEAD), F32)]
    return call(kernel, outs, [VMEM] * 4)(own, got, mine, near)


def join(blocks, axis, places=None, after=()):
    size = blocks[0].shape[axis]
    places = places or range(len(blocks))

    def kernel(*refs):
        for i, ref in zip(places, refs[:-1]):
            at = slice(i * size, (i + 1) * size)
            if axis == 0:
                refs[-1][at, :] = ref[...]
            else:
                refs[-1][:, at] = ref[...]

    shape = list(blocks[0].shape)
    shape[axis] *= len(blocks)
    (out,) = call(kernel, [(tuple(shape), BF16)], [VMEM] * len(blocks), after=after)(*blocks)
    return out


def attention(places, coef, cs, tot0, own12, end12, tot3):
    def kernel(places_ref, coef_ref, cs_ref, tot0_ref, own12_ref, end12_ref, tot3_ref, out_ref, qkv):
        my = lax.axis_index("my")
        for k, offset in enumerate((0, 1, 3, 2)):
            if k in (1, 2):
                at = slice((k - 1) * SH, k * SH)
                total = own12_ref[at, :] + end12_ref[at, :].astype(F32)
            else:
                total = (tot3_ref if k else tot0_ref)[...]
            coef = coef_ref[k * SH : (k + 1) * SH, :]
            for c in range(4):
                total = total + coef[:, c + 1 : c + 2] * cs_ref[c : c + 1, :]
            total = total * coef[:, 0:1]
            shard = (my + offset) & 3
            qkv[pl.ds(pl.multiple_of(shard * SH, SH), SH), :] = total.astype(BF16)
        first, second = places_ref[8], places_ref[9]
        for image in range(2):
            start = pl.multiple_of(first * BLK, BLK) if image else 0
            live = (second if image else first) * BLK
            q = qkv[pl.ds(start, IMG_ROWS), 0:HD]
            key = qkv[pl.ds(start, IMG_ROWS), HD : 2 * HD]
            value = qkv[pl.ds(start, IMG_ROWS), 2 * HD : 3 * HD]
            rows = lax.broadcasted_iota(jnp.int32, (IMG_ROWS, HD), 0)
            value = jnp.where(rows < live, value, jnp.zeros_like(value))
            scores = lax.dot_general(q, key, (((1,), (1,)), ((), ())), preferred_element_type=F32)
            columns = lax.broadcasted_iota(jnp.int32, (IMG_ROWS, IMG_ROWS), 1)
            scores = jnp.where(columns < live, scores, F32(-1e30))
            top = jnp.max(scores, axis=1, keepdims=True)
            powers = jnp.exp((scores - top) * HD ** (-0.5))
            mixture = jnp.dot(powers.astype(BF16), value, preferred_element_type=F32)
            mixture = mixture / jnp.sum(powers, axis=1, keepdims=True)
            out_ref[image * IMG_ROWS : (image + 1) * IMG_ROWS, :] = mixture.astype(BF16)

    (out,) = call(
        kernel, [((R, HD), BF16)], [SMEM] + [VMEM] * 6, [pltpu.VMEM((R, HEAD), BF16)], limit=24
    )(places, coef, cs, tot0, own12, end12, tot3)
    return out


def route(places, mine, other):
    def kernel(places_ref, mine_ref, other_ref, *outs):
        for n in range(GRP):
            out_ref = outs[n // 2]
            place = slice((n % 2) * BLK, (n % 2 + 1) * BLK)
            src = places_ref[n]
            row = pl.multiple_of((src & 7) * BLK, BLK)

            @pl.when(src < 0)
            def _():
                out_ref[place, :] = jnp.zeros((BLK, HD), BF16)

            @pl.when((src >= 0) & (src < GRP))
            def _():
                out_ref[place, :] = mine_ref[pl.ds(row, BLK), :]

            @pl.when(src >= GRP)
            def _():
                out_ref[place, :] = other_ref[pl.ds(row, BLK), :]

    return call(kernel, [((SH, HD), BF16)] * 4, [SMEM, VMEM, VMEM])(places, mine, other)


def lane_rows(blocks):
    def kernel(*refs):
        z = lax.axis_index("mx") >> 1
        for j, ref in zip((0,) + SENT, refs[:4]):
            for d in range(4):
                at = pl.multiple_of((d * 4 + (z ^ j)) * HD, HD)
                refs[4][:, pl.ds(at, HD)] = ref[0:FIRST, d * HD : (d + 1) * HD]
                refs[5][:, pl.ds(at, HD)] = ref[FIRST:SH, d * HD : (d + 1) * HD]

    return call(kernel, [((FIRST, 16 * HD), BF16), ((SH - FIRST, 16 * HD), BF16)], [VMEM] * 4)(*blocks)


def project_lane(lanes, weights):
    def kernel(lane0_ref, lane1_ref, w0_ref, w1_ref, w2_ref, out_ref, rows):
        side = lax.axis_index("mx") & 1
        rows[0:FIRST, :] = lane0_ref[:, 0 : 12 * HD]
        rows[FIRST:SH, :] = lane1_ref[:, 0 : 12 * HD]
        at = pl.ds(pl.multiple_of(side * 4 * HD, 4 * HD), 4 * HD)
        for n in range(3):
            columns = slice(n * 256, (n + 1) * 256)
            total = jnp.zeros((SH, 256), F32)
            for d, ref in enumerate((w0_ref, w1_ref, w2_ref)):
                heads = slice(d * 4 * HD, (d + 1) * 4 * HD)
                total = total + jnp.dot(rows[:, heads], ref[at, columns], preferred_element_type=F32)
            out_ref[:, columns] = total

    scratch = [pltpu.VMEM((SH, 12 * HD), BF16)]
    (out,) = call(kernel, [((SH, DL), F32)], [VMEM] * 5, scratch, limit=24)(*lanes, *weights)
    return out


def project(so_far, lanes, sibs, weights):
    def kernel(far_ref, lane0_ref, lane1_ref, sib0_ref, sib1_ref, w0_ref, w1_ref, w2_ref, top_ref, bottom_ref, out_ref, rows, low, high):
        side = lax.axis_index("mx") & 1
        last = slice(12 * HD, 16 * HD)
        for at, lane_ref, sib_ref in ((slice(0, FIRST), lane0_ref, sib0_ref), (slice(FIRST, SH), lane1_ref, sib1_ref)):
            rows[at, :] = sib_ref[:, 0 : 12 * HD]
            one, two = lane_ref[:, last], sib_ref[:, last]
            low[at, :] = jnp.where(side == 0, one, two)
            high[at, :] = jnp.where(side == 0, two, one)
        place = pl.ds(pl.multiple_of((1 - side) * 4 * HD, 4 * HD), 4 * HD)
        for n in range(3):
            columns = slice(n * 256, (n + 1) * 256)
            total = far_ref[:, columns]
            for d, ref in enumerate((w0_ref, w1_ref, w2_ref)):
                heads = slice(d * 4 * HD, (d + 1) * 4 * HD)
                total = total + jnp.dot(rows[:, heads], ref[place, columns], preferred_element_type=F32)
            total = total + jnp.dot(low[...], top_ref[:, columns], preferred_element_type=F32)
            total = total + jnp.dot(high[...], bottom_ref[:, columns], preferred_element_type=F32)
            out_ref[:, columns] = total.astype(BF16)

    scratch = [pltpu.VMEM((SH, 12 * HD), BF16)] + [pltpu.VMEM((SH, 4 * HD), BF16)] * 2
    (out,) = call(kernel, [((SH, DL), BF16)], [VMEM] * 10, scratch, limit=24)(so_far, *lanes, *sibs, *weights)
    return out


def shards(patches, tile_counts, image_owner, block_target, qkv_weight, out_weight):
    scope = jax.named_scope
    with scope("rows_near"):
        next_rows, last_rows = shift(patches, "my", 1), shift(patches, "my", -1)
    w3 = jnp.transpose(qkv_weight, (1, 0, 2))
    with scope("weights"):
        theirs_keep, theirs_send = weight_heads(w3, True)
        sib_send = swap(theirs_send, "mx", 1)
        sib_keep = swap(theirs_keep, "mx", 1)
        own_keep, own_send = weight_heads(w3, False)
        places = table(tile_counts, image_owner, block_target)
    weights = (own_keep, sib_keep, own_send, sib_send)

    with scope("chunk0"):
        s0 = swap(patches, "mx", 1)
        part0, stat0, again = send_part(patches, s0, own_send, sib_send)
        got0 = swap(part0, "mx", 2)
    with scope("rows_far"):
        x3 = shift(again, "my", 2)
    with scope("sum0"):
        (kept0,) = kept_part([patches], [s0], own_keep, sib_keep, stat0)
    with scope("chunk12"):
        x12 = [next_rows, last_rows]
        s12 = [swap(x, "mx", 1) for x in x12]
        product = own_product(x12, own_send, (kept0,))
        own0, next0 = add_part(kept0, got0, after=(product,))
        end0 = swap(next0, "mx", 4)
        part12, stat12 = rest_part(x12, s12, sib_send, product, (next0,))
        got12 = swap(part12, "mx", 2)
    with scope("chunk3"):
        (x3,) = gate([x3], (part12, end0))
        s3 = swap(x3, "mx", 1)
        (kept12,) = kept_part(x12, s12, own_keep, sib_keep, stat12, after=(part12,))
        part3, stat3, _ = send_part(x3, s3, own_send, sib_send, (stat0, stat12), (kept12, places))
        kept3, mine, note = kept_part([x3], [s3], own_keep, sib_keep, stat3, True, (part3,))
        (held3,) = gate([part3], (kept3, kept12))
        got3 = swap(held3, "mx", 2)
    with scope("sum12"):

        own12, next12, tot0 = add_part(kept12, got12, (own0, end0))
        end12 = swap(next12, "mx", 4)
    with scope("sum3"):
        own3, next3, near = add_part(kept3, got3, note=note, after=(next12,))
        tot3, coef, cs = last_sum(own3, swap(next3, "mx", 4), mine, near)
    with scope("out_weight"):
        w_next, w_last = shift(out_weight, "my", 1), shift(out_weight, "my", -1)
        w_far = [shift(w_next[: 4 * HD], "my", 1), shift(w_last[4 * HD :], "my", -1)]

    with scope("attention"):
        attended = attention(places, coef, cs, tot0, own12, end12, tot3)
        other = swap(attended, "img", 1)
        far, up, down, own = route(places, attended, other)
        near = [own, shift(far, "my", 2), shift(down, "my", 1), shift(up, "my", -1)]

    with scope("out"):
        block = join(near, 1, (0, 3, 1, 2))
        lanes = lane_rows([block] + [swap(block, "mx", 2 * j) for j in SENT])
        sibs = [swap(lane, "mx", 1) for lane in lanes]
        so_far = project_lane(lanes, [out_weight, w_next, w_last])
        return project(so_far, lanes, sibs, [out_weight, w_next, w_last] + w_far)


def solution(mesh):
    in_specs = (
        P(("img", "my"), "mx"),
        P(),
        P(),
        P("img", None),
        P("mx", None, "my"),
        P("my", "mx"),
    )
    out_specs = P(("img", "my"), "mx")
    return jax.shard_map(shards, mesh=mesh, in_specs=in_specs, out_specs=out_specs, check_vma=False)
```
